32 devices in a mesh: gx: 4 (over y, core), gy: 8 (over z, x).
Axes of the slice: x: 2, y: 2, z: 4, core: 2. Of those that a mesh axis runs over, the one named last changes fastest.
Arguments:
- right_side: float32 [2, 64, 256, 256], P(None, 'gx', 'gy'), may hold values from -11 to 11
- coupling_from: float32 [64, 256, 256], P('gx', 'gy'), may hold values from 0.6 to 1.4
- coupling_to: float32 [64, 256, 256], P('gx', 'gy'), may hold values from 0.6 to 1.4
- mass_real: float32 [64, 256, 256], P('gx', 'gy'), may hold values from 0.9 to 1.2
- damping: float32 [64, 256, 256], P('gx', 'gy'), may hold values from 0.1 to 0.6
Outputs:
- solution: float32 [2, 64, 256, 256], P(None, 'gx', 'gy')
- residual: float32 [2, 64, 256, 256], P(None, 'gx', 'gy')
The draws below stay inside these ranges and needn't reach their ends.
All inputs are finite; a program needn't handle non-finite values.
Results may differ from the reference program's by a relative error of at most 0.0003.
Values sent between devices are 32-bit elements; how exact they have to be, the bound alone decides.
No kernel may reach another device: no remote copies, remote signals or barrier semaphores. Data moves between devices by JAX's collectives and lax.ppermute only.
A program may use at most 64 MiB of HBM per device.

```python
import jax
import jax.numpy as jnp
from jax import lax

NZ = 256
ITERS = 2
NX = 64
NY = 256


def draw_right_side(key, part):
    values = jnp.clip(jax.random.normal(key, (2, NX, NY, NZ), jnp.float32), -5.0, 5.0)
    return values


def block_levels(stream_key, extent, split, low, high):
    def one(dim, shards_of):
        steps = jax.random.uniform(jax.random.fold_in(jax.random.fold_in(stream_key, 6), dim), (shards_of,), jnp.float32, low / len(split), high / len(split))
        return jnp.repeat(jnp.exp(steps), extent[dim] // shards_of).reshape((-1,) + (1,) * (len(extent) - dim - 1))

    loudness = one(*split[0])
    for cut in split[1:]:
        loudness = loudness * one(*cut)
    return loudness


def setup_inputs(seed: int = 0) -> dict:
    key_of = jax.random.split(jax.random.key(seed), 6)
    right_side = draw_right_side(jax.random.fold_in(key_of[5], 71), 0)
    coupling_from = jnp.clip(0.6 + 0.79999995 * jax.random.uniform(key_of[1], (NX, NY, NZ), jnp.float32) ** block_levels(key_of[1], (NX, NY, NZ), ((0, 4), (1, 8)), -0.2, 0.2), 0.6, 1.4)
    coupling_to = jnp.clip(0.6 + 0.79999995 * jax.random.uniform(key_of[2], (NX, NY, NZ), jnp.float32) ** block_levels(key_of[2], (NX, NY, NZ), ((0, 4), (1, 8)), -0.2, 0.2), 0.6, 1.4)
    mass_real = jnp.clip(0.9 + 0.30000007 * jax.random.uniform(key_of[3], (NX, NY, NZ), jnp.float32) ** block_levels(key_of[3], (NX, NY, NZ), ((0, 4), (1, 8)), -0.2, 0.2), 0.9, 1.2)
    damping = jnp.clip(0.1 + 0.5 * jax.random.uniform(key_of[4], (NX, NY, NZ), jnp.float32) ** block_levels(key_of[4], (NX, NY, NZ), ((0, 4), (1, 8)), -0.2, 0.2), 0.1, 0.6)
    return {"right_side": right_side, "coupling_from": coupling_from, "coupling_to": coupling_to, "mass_real": mass_real, "damping": damping}


OMEGA = 0.8
EPSILON = 1e-6


def filter_axis(field, axis):
    padded = jnp.pad(field, [(1, 1) if k == axis else (0, 0) for k in range(field.ndim)])
    length = field.shape[axis]
    lower = lax.slice_in_dim(padded, 0, length, axis=axis)
    upper = lax.slice_in_dim(padded, 2, length + 2, axis=axis)
    return lower + 2.0 * field + upper


def neighbours(field):
    total = field
    for axis in (1, 2, 3):
        total = filter_axis(total, axis)
    return (total - 8.0 * field) / 160.0


def complex_mul(real_part, imag_part, field):
    return jnp.stack([real_part * field[0] - imag_part * field[1], real_part * field[1] + imag_part * field[0]])


def complex_div(numer, denom):
    scale = denom[0] * denom[0] + denom[1] * denom[1]
    return ((numer[0] * denom[0] + numer[1] * denom[1]) / scale, (numer[1] * denom[0] - numer[0] * denom[1]) / scale)


def inner_product(left, right):
    return (jnp.sum(left[0] * right[0] + left[1] * right[1]), jnp.sum(left[0] * right[1] - left[1] * right[0]))


def operate(field, coupling_from, coupling_to, diag_re, diag_im):
    return complex_mul(diag_re, diag_im, field) - coupling_to * neighbours(coupling_from * field)


def reference(right_side, coupling_from, coupling_to, mass_real, damping):
    shift_im = damping + 0.5 * mass_real
    modulus = mass_real * mass_real + shift_im * shift_im
    inv_re = mass_real / modulus
    inv_im = -shift_im / modulus

    def precondition(source):
        first = OMEGA * complex_mul(inv_re, inv_im, source)
        applied = operate(first, coupling_from, coupling_to, mass_real, shift_im)
        return first + OMEGA * complex_mul(inv_re, inv_im, source - applied)

    def helm(field):
        return operate(field, coupling_from, coupling_to, mass_real, damping)

    solution = jnp.zeros_like(right_side)
    residual = right_side
    shadow = right_side
    direction = right_side
    rho = inner_product(shadow, residual)
    for step in range(ITERS):
        dhat = precondition(direction)
        image = helm(dhat)
        alpha = complex_div(rho, inner_product(shadow, image))
        half = residual - complex_mul(alpha[0], alpha[1], image)
        hhat = precondition(half)
        second_image = helm(hhat)
        prod_ts = inner_product(second_image, half)
        norm_tt = inner_product(second_image, second_image)[0] + EPSILON
        omega = (prod_ts[0] / norm_tt, prod_ts[1] / norm_tt)
        solution = solution + complex_mul(alpha[0], alpha[1], dhat) + complex_mul(omega[0], omega[1], hhat)
        residual = half - complex_mul(omega[0], omega[1], second_image)
        if step + 1 < ITERS:
            rho_next = inner_product(shadow, residual)
            ratio = complex_div(rho_next, rho)
            factor = complex_div(alpha, omega)
            beta = (ratio[0] * factor[0] - ratio[1] * factor[1], ratio[0] * factor[1] + ratio[1] * factor[0])
            direction = residual + complex_mul(beta[0], beta[1], direction - complex_mul(omega[0], omega[1], image))
            rho = rho_next
    return solution, residual
```

```python
import jax
import jax.numpy as jnp
from jax import lax
from jax.experimental import pallas as pl
from jax.experimental.pallas import tpu as pltpu
from jax.sharding import PartitionSpec as P

OMEGA = 0.8
EPSILON = 1e-06
H = 4
AXES = ("gx", "gy")
F32 = jnp.float32
LIMIT = 48 * 1024 * 1024


def vmem(n):
    return [pl.BlockSpec(memory_space=pltpu.VMEM)] * n


def cmul(a, b):
    return (a[0] * b[0] - a[1] * b[1], a[0] * b[1] + a[1] * b[0])


def cconj(a):
    return (a[0], -a[1])


def cadd(a, b):
    return (a[0] + b[0], a[1] + b[1])


def csub(a, b):
    return (a[0] - b[0], a[1] - b[1])


def cdiv(n, d):
    scale = d[0] * d[0] + d[1] * d[1]
    return (
        (n[0] * d[0] + n[1] * d[1]) / scale,
        (n[1] * d[0] - n[0] * d[1]) / scale,
    )


def smooth_yz(plane):
    rows, lanes = plane.shape
    y = plane + plane + pltpu.roll(plane, 1, 0) + pltpu.roll(plane, rows - 1, 0)
    lane = lax.broadcasted_iota(jnp.int32, plane.shape, 1)
    up = jnp.where(lane == 0, 0.0, pltpu.roll(y, 1, 1))
    down = jnp.where(lane == lanes - 1, 0.0, pltpu.roll(y, lanes - 1, 1))
    return y + y + up + down


def weighted(ref, i):
    out = []
    for part in range(2):
        mid = ref[part, i]
        total = smooth_yz(ref[part, i - 1] + mid + mid + ref[part, i + 1])
        out.append((total - 8.0 * mid) * (1.0 / 160.0))
    return tuple(out)


def coefficients(c, mr, d):
    shift = d + 0.5 * mr
    mod = mr * mr + shift * shift
    den = mod * c
    inv = 1.0 / jnp.where(den == 0.0, 1.0, den)
    k = OMEGA * c * c * inv
    rc = mod * inv
    return (k * mr, -(k * shift)), (rc * mr, rc * d)


def half_step(u_ref, p_ref, w_ref, lo, hi):
    def body(i, carry):
        pw = cmul((p_ref[0, i], p_ref[1, i]), weighted(u_ref, i))
        w_ref[0, i] = 1.2 * u_ref[0, i] + pw[0]
        w_ref[1, i] = 1.2 * u_ref[1, i] + pw[1]
        return carry

    lax.fori_loop(lo, hi, body, 0)


def image_plane(w_ref, n_ref, i):
    nw = cmul((n_ref[0, i], n_ref[1, i]), (w_ref[0, i], w_ref[1, i]))
    return csub(nw, weighted(w_ref, i))


def total_of(ref):
    rows = ref[...].reshape(ref.shape[0], ref.shape[-1])
    tot = jnp.sum(rows, axis=0, keepdims=True)
    lane = lax.broadcasted_iota(jnp.int32, tot.shape, 1)
    return lambda k: jnp.sum(jnp.where(lane == k, tot, 0.0), axis=1, keepdims=True)


def pack_lanes(values):
    lane = lax.broadcasted_iota(jnp.int32, (1, 128), 1)
    row = jnp.zeros((1, 128), F32)
    for k, v in enumerate(values):
        s = jnp.sum(jnp.sum(v, axis=0, keepdims=True), axis=1, keepdims=True)
        row = jnp.where(lane == k, s, row)
    return row


def fold(x):
    rows, lanes = x.shape
    out = None
    for a in range(0, rows, 8):
        for b in range(0, lanes, 128):
            t = x[a : a + 8, b : b + 128]
            out = t if out is None else out + t
    return out


def shift_kernel(b_ref, cf_ref, ct_ref, mr_ref, d_ref, out_ref, u_ref, w_ref, p_ref, n_ref):
    nx, ny, nz = cf_ref.shape
    zero = jnp.zeros((ny + 8, nz), F32)
    for ref in (u_ref, w_ref):
        for part in range(2):
            ref[part, 0] = zero
            ref[part, nx + 1] = zero

    pad = jnp.zeros((8, nz), F32)

    def ext(x):
        return jnp.concatenate([x, pad], axis=0)

    def fill(i, carry):
        ct = ct_ref[i]
        r = 1.0 / ct
        p, n = coefficients(cf_ref[i] * ct, mr_ref[i], d_ref[i])
        u = cmul(p, (b_ref[0, i] * r, b_ref[1, i] * r))
        for part in range(2):
            p_ref[part, i + 1] = ext(p[part])
            n_ref[part, i + 1] = ext(n[part])
            u_ref[part, i + 1] = ext(u[part])
        return carry

    lax.fori_loop(0, nx, fill, 0)
    half_step(u_ref, p_ref, w_ref, 1, nx + 1)

    def dots(i, acc):
        y = image_plane(w_ref, n_ref, i + 1)
        ct = ct_ref[i]
        yr, yi = y[0][:ny] * ct, y[1][:ny] * ct
        br, bi = b_ref[0, i], b_ref[1, i]
        return (
            acc[0] + fold(br * yr + bi * yi),
            acc[1] + fold(br * yi - bi * yr),
            acc[2] + fold(br * br + bi * bi),
        )

    acc = lax.fori_loop(0, nx, dots, (jnp.zeros((8, 128), F32),) * 3)
    row = pack_lanes(acc)
    for k in range(out_ref.shape[0]):
        out_ref[k] = row


def local_shift(b, cf, ct, mr, d, peers):
    nx, ny, nz = cf.shape
    big = pltpu.VMEM((2, nx + 2, ny + 8, nz), F32)
    return pl.pallas_call(
        shift_kernel,
        out_shape=jax.ShapeDtypeStruct((peers, 1, 128), F32),
        in_specs=vmem(5),
        out_specs=pl.BlockSpec(memory_space=pltpu.VMEM),
        scratch_shapes=[big] * 4,
        compiler_params=pltpu.CompilerParams(vmem_limit_bytes=LIMIT),
    )(b, cf, ct, mr, d)


def pack_pair(first, second, top):
    sub = lax.broadcasted_iota(jnp.int32, first.shape, 0)
    rolled = pltpu.roll(second, 4, 0)
    if top:
        return jnp.where(sub < 4, first, rolled)
    return jnp.where(sub < 4, rolled, first)


def unpack_pair(right, left):
    sub = lax.broadcasted_iota(jnp.int32, right.shape, 0)
    first = jnp.where(sub < 4, right, left)
    second = pltpu.roll(jnp.where(sub < 4, left, right), 4, 0)
    return first, second


def pack_first_kernel(xl_ref, xr_ref, b_ref, cf_ref, ct_ref, mr_ref, d_ref, top_ref, bot_ref):
    nx, ny, _ = cf_ref.shape

    def own(rows):
        def get(i):
            ct = ct_ref[i, rows]
            r = 1.0 / ct
            return (
                b_ref[0, i, rows] * r,
                b_ref[1, i, rows] * r,
                cf_ref[i, rows] * ct,
                mr_ref[i, rows],
                d_ref[i, rows],
            )

        return get

    def halo(ref, rows):
        return lambda i: tuple(ref[f, i, rows] for f in range(5))

    for out_ref, rows, top in ((top_ref, pl.ds(0, 8), True), (bot_ref, pl.ds(ny - 8, 8), False)):

        def run(get, count, base):
            def body(j, carry):
                a, b = get(2 * j), get(2 * j + 1)
                plane = base + 2 * j
                out_ref[plane] = pack_pair(a[0], a[1], top)
                out_ref[plane + 1] = pack_pair(b[0], b[1], top)
                for f in range(3):
                    at = (nx + 2 * H) + f * (nx + 2 * H) // 2 + base // 2 + j
                    out_ref[at] = pack_pair(a[2 + f], b[2 + f], top)
                return carry

            lax.fori_loop(0, count // 2, body, 0)

        run(halo(xl_ref, rows), H, 0)
        run(own(rows), nx, H)
        run(halo(xr_ref, rows), H, H + nx)


def pack_later_kernel(xl_ref, xr_ref, v_ref, top_ref, bot_ref):
    nx, ny = v_ref.shape[1:3]
    for out_ref, rows, top in ((top_ref, pl.ds(0, 8), True), (bot_ref, pl.ds(ny - 8, 8), False)):
        for ref, count, base in ((xl_ref, H, 0), (v_ref, nx, H), (xr_ref, H, H + nx)):

            def body(i, carry):
                out_ref[base + i] = pack_pair(ref[0, i, rows], ref[1, i, rows], top)
                return carry

            lax.fori_loop(0, count, body, 0)


def first_kernel(
    th_ref, xl_ref, xr_ref, yl_ref, yr_ref, b_ref, cf_ref, ct_ref, mr_ref, d_ref,
    p_ref, n_ref, w0_ref, w1_ref, v1_ref, v2_ref, sl_ref, sr_ref,
    u_ref, w_ref, v_ref,
):
    nx, ny, nz = cf_ref.shape
    planes = nx + 2 * H
    th = shift_from(th_ref)

    def own(i):
        ct = ct_ref[i]
        r = 1.0 / ct
        return (b_ref[0, i] * r, b_ref[1, i] * r, cf_ref[i] * ct, mr_ref[i], d_ref[i])

    def halo(ref):
        return lambda i: tuple(ref[f, i] for f in range(5))

    def run(get, count, base):
        def body(j, carry):
            plane = base + 2 * j
            tails = []
            for k in range(2):
                tails.append(list(unpack_pair(yr_ref[plane + k], yl_ref[plane + k])))
            for f in range(3):
                at = planes + f * planes // 2 + base // 2 + j
                a, b = unpack_pair(yr_ref[at], yl_ref[at])
                tails[0].append(a)
                tails[1].append(b)
            for k in range(2):
                body_rows = get(2 * j + k)
                vr, vi, c, mr, d = (
                    jnp.concatenate([body_rows[f], tails[k][f]], axis=0) for f in range(5)
                )
                p, n = coefficients(c, mr, d)
                u = cmul(p, (vr, vi))
                v_ref[0, plane + k], v_ref[1, plane + k] = vr, vi
                for part in range(2):
                    p_ref[part, plane + k] = p[part]
                    n_ref[part, plane + k] = n[part]
                    u_ref[part, plane + k] = u[part]
            return carry

        lax.fori_loop(0, count // 2, body, 0)

    run(halo(xl_ref), H, 0)
    run(own, nx, H)
    run(halo(xr_ref), H, H + nx)

    half_step(u_ref, p_ref, w_ref, 1, planes - 1)

    def second(i, carry):
        y = csub(image_plane(w_ref, n_ref, i), cmul(th, (v_ref[0, i], v_ref[1, i])))
        u = cmul((p_ref[0, i], p_ref[1, i]), y)
        for part in range(2):
            v_ref[part, i] = y[part]
            u_ref[part, i] = u[part]
        return carry

    lax.fori_loop(2, planes - 2, second, 0)

    def keep(i, carry):
        for part in range(2):
            w0_ref[part, i] = w_ref[part, i + H, pl.ds(0, ny)]
            v1_ref[part, i] = v_ref[part, i + H, pl.ds(0, ny)]
        return carry

    lax.fori_loop(0, nx, keep, 0)
    half_step(u_ref, p_ref, w_ref, 3, planes - 3)

    def last(i, carry):
        at = i + H
        y = csub(image_plane(w_ref, n_ref, at), cmul(th, (v_ref[0, at], v_ref[1, at])))
        for part in range(2):
            v2_ref[part, i] = y[part][:ny]
            w1_ref[part, i] = w_ref[part, at, pl.ds(0, ny)]
        return carry

    lax.fori_loop(0, nx, last, 0)
    for part in range(2):
        for i in range(H):
            sl_ref[part, i] = v2_ref[part, i]
            sr_ref[part, i] = v2_ref[part, nx - H + i]


def shift_from(th_ref):
    pick = total_of(th_ref)
    den = pick(2)
    safe = jnp.where(den > 0.0, den, 1.0)
    return (
        jnp.where(den > 0.0, pick(0) / safe, 0.72),
        jnp.where(den > 0.0, pick(1) / safe, -0.28),
    )


def second_kernel(
    th_ref, xl_ref, xr_ref, yl_ref, yr_ref, p_ref, n_ref, b_ref, ct_ref, v1_ref, v2_ref,
    w2_ref, w3_ref, v3_ref, v4_ref, out_ref,
    u_ref, w_ref, v_ref,
):
    nx, ny, nz = ct_ref.shape
    planes = nx + 2 * H
    th = shift_from(th_ref)

    for ref, count, base in ((xl_ref, H, 0), (v2_ref, nx, H), (xr_ref, H, H + nx)):

        def fill(i, carry):
            at = base + i
            tail = unpack_pair(yr_ref[at], yl_ref[at])
            v = tuple(jnp.concatenate([ref[part, i], tail[part]], axis=0) for part in range(2))
            u = cmul((p_ref[0, at], p_ref[1, at]), v)
            for part in range(2):
                v_ref[part, at] = v[part]
                u_ref[part, at] = u[part]
            return carry

        lax.fori_loop(0, count, fill, 0)

    half_step(u_ref, p_ref, w_ref, 1, planes - 1)

    def second(i, carry):
        y = csub(image_plane(w_ref, n_ref, i), cmul(th, (v_ref[0, i], v_ref[1, i])))
        u = cmul((p_ref[0, i], p_ref[1, i]), y)
        for part in range(2):
            v_ref[part, i] = y[part]
            u_ref[part, i] = u[part]
        return carry

    lax.fori_loop(2, planes - 2, second, 0)

    def keep(i, carry):
        for part in range(2):
            w2_ref[part, i] = w_ref[part, i + H, pl.ds(0, ny)]
            v3_ref[part, i] = v_ref[part, i + H, pl.ds(0, ny)]
        return carry

    lax.fori_loop(0, nx, keep, 0)
    half_step(u_ref, p_ref, w_ref, 3, planes - 3)

    def last(i, carry):
        at = i + H
        y = csub(image_plane(w_ref, n_ref, at), cmul(th, (v_ref[0, at], v_ref[1, at])))
        for part in range(2):
            v4_ref[part, i] = y[part][:ny]
            w3_ref[part, i] = w_ref[part, at, pl.ds(0, ny)]
        return carry

    lax.fori_loop(0, nx, last, 0)

    def dots(i, acc):
        acc = list(acc)
        for a in range(0, ny, 8):
            rows = pl.ds(a, 8)
            ct = ct_ref[i, rows]
            vs = [(b_ref[0, i, rows], b_ref[1, i, rows])]
            for ref in (v1_ref, v2_ref, v3_ref, v4_ref):
                vs.append((ct * ref[0, i, rows], ct * ref[1, i, rows]))
            k = 0
            for left in range(5):
                for right in range(left, 5):
                    (lr, li), (rr, ri) = vs[left], vs[right]
                    acc[k] = acc[k] + fold(lr * rr + li * ri)
                    k += 1
                    if right > left:
                        acc[k] = acc[k] + fold(lr * ri - li * rr)
                        k += 1
        return tuple(acc)

    acc = lax.fori_loop(0, nx, dots, (jnp.zeros((8, 128), F32),) * 25)
    row = pack_lanes(acc)
    for k in range(out_ref.shape[0]):
        out_ref[k] = row


def recurrences(th, gram):
    def inner(x, y):
        total = None
        for i, xi in enumerate(x):
            part = None
            for j, yj in enumerate(y):
                t = cmul(gram(i, j), yj)
                part = t if part is None else cadd(part, t)
            t = cmul(cconj(xi), part)
            total = t if total is None else cadd(total, t)
        return total

    def apply(x):
        scaled = [cmul(th, c) for c in x]
        return [scaled[0]] + [cadd(x[k], scaled[k + 1]) for k in range(len(x) - 1)] + [x[-1]]

    def lincomb(x, s, y):
        out = []
        for k in range(max(len(x), len(y))):
            a = x[k] if k < len(x) else None
            b = cmul(s, y[k]) if k < len(y) else None
            out.append(b if a is None else a if b is None else cadd(a, b))
        return out

    def neg(s):
        return (-s[0], -s[1])

    one = (jnp.ones((1, 1), F32), jnp.zeros((1, 1), F32))
    residual, direction, shadow, answer = [one], [one], [one], []
    rho = inner(shadow, residual)
    for step in range(2):
        image = apply(direction)
        alpha = cdiv(rho, inner(shadow, image))
        half = lincomb(residual, neg(alpha), image)
        second = apply(half)
        prod = inner(second, half)
        norm = inner(second, second)[0] + EPSILON
        omega = (prod[0] / norm, prod[1] / norm)
        answer = lincomb(lincomb(answer, alpha, direction), omega, half)
        residual = lincomb(half, neg(omega), second)
        if step == 0:
            rho_next = inner(shadow, residual)
            beta = cmul(cdiv(rho_next, rho), cdiv(alpha, omega))
            direction = lincomb(residual, beta, lincomb(direction, neg(omega), image))
            rho = rho_next
    return answer, residual


def final_kernel(
    th_ref, g_ref, b_ref, cf_ref, ct_ref,
    w0_ref, w1_ref, w2_ref, w3_ref, v1_ref, v2_ref, v3_ref, v4_ref,
    sol_ref, res_ref,
):
    nx = cf_ref.shape[0]
    th = shift_from(th_ref)
    pick = total_of(g_ref)
    entries, k = {}, 0
    for left in range(5):
        for right in range(left, 5):
            if right > left:
                entries[left, right] = (pick(k), pick(k + 1))
                entries[right, left] = cconj(entries[left, right])
                k += 2
            else:
                entries[left, right] = (pick(k), jnp.zeros((1, 1), F32))
                k += 1
    answer, residual = recurrences(th, lambda i, j: entries[i, j])

    def body(i, carry):
        acc = None
        for c, ref in zip(answer, (w0_ref, w1_ref, w2_ref, w3_ref)):
            t = cmul(c, (ref[0, i], ref[1, i]))
            acc = t if acc is None else cadd(acc, t)
        inv = 1.0 / cf_ref[i]
        sol_ref[0, i] = acc[0] * inv
        sol_ref[1, i] = acc[1] * inv
        acc = None
        for c, ref in zip(residual[1:], (v1_ref, v2_ref, v3_ref, v4_ref)):
            t = cmul(c, (ref[0, i], ref[1, i]))
            acc = t if acc is None else cadd(acc, t)
        ct = ct_ref[i]
        t = cmul(residual[0], (b_ref[0, i], b_ref[1, i]))
        res_ref[0, i] = acc[0] * ct + t[0]
        res_ref[1, i] = acc[1] * ct + t[1]
        return carry

    lax.fori_loop(0, nx, body, 0)


def call(kernel, outs, scratch, *args):
    return pl.pallas_call(
        kernel,
        out_shape=[jax.ShapeDtypeStruct(s, F32) for s in outs],
        in_specs=vmem(len(args)),
        out_specs=vmem(len(outs)),
        scratch_shapes=[pltpu.VMEM(s, F32) for s in scratch],
        compiler_params=pltpu.CompilerParams(vmem_limit_bytes=LIMIT),
    )(*args)


def both_ways(to_lower, to_upper, axis):
    n = lax.axis_size(axis)
    up = [(i, i + 1) for i in range(n - 1)]
    down = [(i + 1, i) for i in range(n - 1)]
    return lax.ppermute(to_upper, axis, up), lax.ppermute(to_lower, axis, down)


def local(b, cf, ct, mr, d):
    nx, ny, nz = cf.shape
    peers = lax.axis_size("gx") * lax.axis_size("gy")
    planes = nx + 2 * H
    own = (2, nx, ny, nz)
    ext = (2, planes, ny + 2 * H, nz)

    def edge(s):
        return jnp.concatenate(
            [b[:, s] / ct[s], (cf[s] * ct[s])[None], mr[s][None], d[s][None]], axis=0
        )

    xl, xr = both_ways(edge(slice(0, H)), edge(slice(nx - H, nx)), "gx")
    th = local_shift(b, cf, ct, mr, d, peers)
    th = lax.all_to_all(th, AXES, 0, 0)
    count = planes + 3 * planes // 2
    top, bot = call(pack_first_kernel, [(count, 8, nz)] * 2, [], xl, xr, b, cf, ct, mr, d)
    yl, yr = both_ways(top, bot, "gy")
    p, n, w0, w1, v1, v2, sl, sr = call(
        first_kernel,
        [ext, ext, own, own, own, own, (2, H, ny, nz), (2, H, ny, nz)],
        [ext, ext, ext],
        th, xl, xr, yl, yr, b, cf, ct, mr, d,
    )
    xl, xr = both_ways(sl, sr, "gx")
    top, bot = call(pack_later_kernel, [(planes, 8, nz)] * 2, [], xl, xr, v2)
    yl, yr = both_ways(top, bot, "gy")
    w2, w3, v3, v4, g = call(
        second_kernel,
        [own, own, own, own, (peers, 1, 128)],
        [ext, ext, ext],
        th, xl, xr, yl, yr, p, n, b, ct, v1, v2,
    )
    g = lax.all_to_all(g, AXES, 0, 0)
    sol, res = call(
        final_kernel, [own, own], [], th, g, b, cf, ct, w0, w1, w2, w3, v1, v2, v3, v4
    )
    return sol, res


def solution(mesh):
    field, coef = P(None, "gx", "gy", None), P("gx", "gy", None)
    return jax.shard_map(
        local,
        mesh=mesh,
        in_specs=(field, coef, coef, coef, coef),
        out_specs=(field, field),
        check_vma=False,
    )
```

```python
import jax
import jax.numpy as jnp
from jax import lax
from jax.experimental import pallas as pl
from jax.experimental.pallas import tpu as pltpu
from jax.sharding import PartitionSpec as P

OMEGA = 0.8
EPSILON = 1e-06
H = 4
AXES = ("gx", "gy")
F32 = jnp.float32
LIMIT = 24 * 1024 * 1024
SHIFTS = ((0.72, -0.28), (0.55, -0.2))


def vmem(n):
    return [pl.BlockSpec(memory_space=pltpu.VMEM)] * n


def cmul(a, b):
    return (a[0] * b[0] - a[1] * b[1], a[0] * b[1] + a[1] * b[0])


def cconj(a):
    return (a[0], -a[1])


def cadd(a, b):
    return (a[0] + b[0], a[1] + b[1])


def csub(a, b):
    return (a[0] - b[0], a[1] - b[1])


def cdiv(n, d):
    scale = d[0] * d[0] + d[1] * d[1]
    return (
        (n[0] * d[0] + n[1] * d[1]) / scale,
        (n[1] * d[0] - n[0] * d[1]) / scale,
    )


def smooth_yz(plane):
    rows, lanes = plane.shape
    y = plane + plane + pltpu.roll(plane, 1, 0) + pltpu.roll(plane, rows - 1, 0)
    lane = lax.broadcasted_iota(jnp.int32, plane.shape, 1)
    up = jnp.where(lane == 0, 0.0, pltpu.roll(y, 1, 1))
    down = jnp.where(lane == lanes - 1, 0.0, pltpu.roll(y, lanes - 1, 1))
    return y + y + up + down


def weighted(ref, i):
    out = []
    for part in range(2):
        mid = ref[part, i]
        total = smooth_yz(ref[part, i - 1] + mid + mid + ref[part, i + 1])
        out.append((total - 8.0 * mid) * (1.0 / 160.0))
    return tuple(out)


def coefficients(c, mr, d):
    shift = d + 0.5 * mr
    mod = mr * mr + shift * shift
    den = mod * c
    inv = 1.0 / jnp.where(den == 0.0, 1.0, den)
    k = OMEGA * c * c * inv
    rc = mod * inv
    return (k * mr, -(k * shift)), (rc * mr, rc * d)


def half_step(u_ref, p_ref, w_ref, lo, hi):
    def body(i, carry):
        pw = cmul((p_ref[0, i], p_ref[1, i]), weighted(u_ref, i))
        w_ref[0, i] = 1.2 * u_ref[0, i] + pw[0]
        w_ref[1, i] = 1.2 * u_ref[1, i] + pw[1]
        return carry

    lax.fori_loop(lo, hi, body, 0, unroll=2)


def image(w_ref, n_ref, v_ref, th, i, at):
    w = (w_ref[0, i], w_ref[1, i])
    nw = cmul((n_ref[0, i], n_ref[1, i]), w)
    rows = v_ref.shape[2]
    v = cmul(th, (v_ref[0, at], v_ref[1, at]))
    y = csub(nw, weighted(w_ref, i))
    return csub((y[0][:rows], y[1][:rows]), v)


def apply_wide(w_ref, n_ref, v_ref, p_ref, th, next_ref, u_ref, lo, hi):
    def body(i, carry):
        y = image(w_ref, n_ref, v_ref, th, i, i)
        u = cmul((p_ref[0, i], p_ref[1, i]), y)
        for part in range(2):
            next_ref[part, i] = y[part]
            u_ref[part, i] = u[part]
        return carry

    lax.fori_loop(lo, hi, body, 0, unroll=2)


def apply_own(w_ref, n_ref, v_ref, th, next_ref):
    nx, ny = next_ref.shape[1:3]

    def body(i, carry):
        y = image(w_ref, n_ref, v_ref, th, i + H, i + H)
        for part in range(2):
            next_ref[part, i] = y[part][:ny]
        return carry

    lax.fori_loop(0, nx, body, 0, unroll=2)


def total_of(ref):
    rows = ref[...].reshape(ref.shape[0], ref.shape[-1])
    tot = jnp.sum(rows, axis=0, keepdims=True)
    lane = lax.broadcasted_iota(jnp.int32, tot.shape, 1)
    return lambda k: jnp.sum(jnp.where(lane == k, tot, 0.0), axis=1, keepdims=True)


def pack_lanes(values):
    lane = lax.broadcasted_iota(jnp.int32, (1, 128), 1)
    row = jnp.zeros((1, 128), F32)
    for k, v in enumerate(values):
        s = jnp.sum(jnp.sum(v, axis=0, keepdims=True), axis=1, keepdims=True)
        row = jnp.where(lane == k, s, row)
    return row


def fold(x):
    out = x[:, :128]
    for b in range(128, x.shape[1], 128):
        out = out + x[:, b : b + 128]
    return out


def pairs_of(rights):
    return [(left, right) for right in rights for left in range(right + 1)]


def gram_rows(fields, ct_ref, pairs, out_ref):
    nx, ny, _ = ct_ref.shape
    used = sorted({k for pair in pairs for k in pair})
    count = sum(1 if left == right else 2 for left, right in pairs)

    def body(i, acc):
        acc = list(acc)
        for a in range(0, ny, 8):
            rows = pl.ds(a, 8)
            ct = ct_ref[i, rows]
            vs = {}
            for k in used:
                ref, base, scaled = fields[k]
                v = (ref[0, i + base, rows], ref[1, i + base, rows])
                vs[k] = (ct * v[0], ct * v[1]) if scaled else v
            k = 0
            for left, right in pairs:
                (lr, li), (rr, ri) = vs[left], vs[right]
                acc[k] = acc[k] + fold(lr * rr + li * ri)
                k += 1
                if right > left:
                    acc[k] = acc[k] + fold(lr * ri - li * rr)
                    k += 1
        return tuple(acc)

    acc = lax.fori_loop(0, nx, body, (jnp.zeros((8, 128), F32),) * count)
    row = pack_lanes(acc)
    for k in range(out_ref.shape[0]):
        out_ref[k] = row


def gram_entries(ref, pairs, entries):
    pick = total_of(ref)
    k = 0
    for left, right in pairs:
        if left == right:
            entries[left, right] = (pick(k), jnp.zeros((1, 1), F32))
            k += 1
        else:
            entries[left, right] = (pick(k), pick(k + 1))
            entries[right, left] = cconj(entries[left, right])
            k += 2
    return entries


def later_shift(entries):
    den = entries[0, 0][0]
    safe = jnp.where(den > 0.0, den, 1.0)
    num = entries[0, 1]
    return (SHIFTS[0][0] + num[0] / safe, SHIFTS[0][1] + num[1] / safe)


EARLY = pairs_of((0, 1, 2))
LATE = pairs_of((3, 4))


def pack_pair(first, second, top):
    sub = lax.broadcasted_iota(jnp.int32, first.shape, 0)
    rolled = pltpu.roll(second, 4, 0)
    if top:
        return jnp.where(sub < 4, first, rolled)
    return jnp.where(sub < 4, rolled, first)


def unpack_pair(right, left):
    sub = lax.broadcasted_iota(jnp.int32, right.shape, 0)
    first = jnp.where(sub < 4, right, left)
    second = pltpu.roll(jnp.where(sub < 4, left, right), 4, 0)
    return first, second


def own_values(b_ref, cf_ref, ct_ref, mr_ref, d_ref):
    def get(i, rows):
        ct = ct_ref[i, rows]
        r = 1.0 / ct
        return (
            b_ref[0, i, rows] * r,
            b_ref[1, i, rows] * r,
            cf_ref[i, rows] * ct,
            mr_ref[i, rows],
            d_ref[i, rows],
        )

    return get


def edges_kernel(b_ref, cf_ref, ct_ref, mr_ref, d_ref, lo_ref, hi_ref, top_ref, bot_ref):
    nx, ny, _ = cf_ref.shape
    get = own_values(b_ref, cf_ref, ct_ref, mr_ref, d_ref)
    for out_ref, base in ((lo_ref, 0), (hi_ref, nx - H)):
        for i in range(H):
            for f, value in enumerate(get(base + i, pl.ds(0, ny))):
                out_ref[f, i] = value
    for out_ref, rows, top in ((top_ref, pl.ds(0, 8), True), (bot_ref, pl.ds(ny - 8, 8), False)):

        def body(j, carry):
            a, b = get(2 * j, rows), get(2 * j + 1, rows)
            out_ref[2 * j] = pack_pair(a[0], a[1], top)
            out_ref[2 * j + 1] = pack_pair(b[0], b[1], top)
            for f in range(3):
                out_ref[nx + f * nx // 2 + j] = pack_pair(a[2 + f], b[2 + f], top)
            return carry

        lax.fori_loop(0, nx // 2, body, 0, unroll=2)


def corners_kernel(yl_ref, yr_ref, lo_ref, hi_ref):
    count = yl_ref.shape[0]
    nx = count * 2 // 5
    for k, ref in enumerate((yl_ref, yr_ref)):
        for out_ref, base in ((lo_ref, 0), (hi_ref, nx - H)):
            for i in range(H):
                out_ref[k, i] = ref[base + i]
            for f in range(3):
                for j in range(H // 2):
                    at = nx + f * nx // 2 + base // 2 + j
                    out_ref[k, H + f * H // 2 + j] = ref[at]


def store_fields(refs, plane, rows, v, c, mr, d):
    p_ref, n_ref, u_ref, v_ref = refs
    p, n = coefficients(c, mr, d)
    u = cmul(p, v)
    for part in range(2):
        p_ref[part, plane, rows] = p[part]
        n_ref[part, plane, rows] = n[part]
        u_ref[part, plane, rows] = u[part]
        v_ref[part, plane, rows] = v[part]


def own_kernel(b_ref, cf_ref, ct_ref, mr_ref, d_ref, p_ref, n_ref, u_ref, v_ref):
    nx, ny, _ = cf_ref.shape
    get = own_values(b_ref, cf_ref, ct_ref, mr_ref, d_ref)
    rows = pl.ds(0, ny)

    def body(i, carry):
        vr, vi, c, mr, d = get(i, rows)
        store_fields((p_ref, n_ref, u_ref, v_ref), i + H, rows, (vr, vi), c, mr, d)
        return carry

    lax.fori_loop(0, nx, body, 0, unroll=2)


def tails(refs, left, right, ny, fields, coefs, planes):
    rows = pl.ds(ny, 8)
    v = [unpack_pair(right(k), left(k)) for k in fields]
    c = [unpack_pair(right(k), left(k)) for k in coefs]
    for k in range(2):
        store_fields(refs, planes[k], rows, v[k], c[0][k], c[1][k], c[2][k])


def sides_kernel(xl_ref, xr_ref, yl_ref, yr_ref, *refs):
    refs = refs[4:]
    ny = xl_ref.shape[2]
    nx = refs[0].shape[1] - 2 * H
    rows = pl.ds(0, ny)
    for ref, base in ((xl_ref, 0), (xr_ref, nx + H)):

        def body(i, carry):
            vr, vi, c, mr, d = (ref[f, i] for f in range(5))
            store_fields(refs, base + i, rows, (vr, vi), c, mr, d)
            return carry

        lax.fori_loop(0, H, body, 0, unroll=2)

    def body(j, carry):
        coefs = [nx + f * nx // 2 + j for f in range(3)]
        at = (H + 2 * j, H + 2 * j + 1)
        tails(
            refs, lambda k: yl_ref[k], lambda k: yr_ref[k], ny, (2 * j, 2 * j + 1), coefs, at
        )
        return carry

    lax.fori_loop(0, nx // 2, body, 0, unroll=2)


def first_kernel(cl_ref, cr_ref, *refs):
    (p_ref, n_ref, u_ref, v_ref), rest = refs[4:8], refs[8:]
    w0_ref, w1_ref, v1_ref, v2_ref, sl_ref, sr_ref = rest
    nx, ny = v2_ref.shape[1:3]
    planes = nx + 2 * H
    for ref, base in ((cl_ref, 0), (cr_ref, nx + H)):
        for j in range(H // 2):
            coefs = [H + f * H // 2 + j for f in range(3)]
            at = (base + 2 * j, base + 2 * j + 1)
            tails(
                (p_ref, n_ref, u_ref, v_ref), lambda k: ref[0, k], lambda k: ref[1, k],
                ny, (2 * j, 2 * j + 1), coefs, at,
            )
    half_step(u_ref, p_ref, w0_ref, 1, planes - 1)
    apply_wide(w0_ref, n_ref, v_ref, p_ref, SHIFTS[0], v1_ref, u_ref, 2, planes - 2)
    half_step(u_ref, p_ref, w1_ref, 3, planes - 3)
    apply_own(w1_ref, n_ref, v1_ref, SHIFTS[1], v2_ref)
    for part in range(2):
        for i in range(H):
            sl_ref[part, i] = v2_ref[part, i]
            sr_ref[part, i] = v2_ref[part, nx - H + i]


def pack_kernel(xl_ref, xr_ref, v_ref, top_ref, bot_ref):
    nx, ny = v_ref.shape[1:3]
    for out_ref, rows, top in ((top_ref, pl.ds(0, 8), True), (bot_ref, pl.ds(ny - 8, 8), False)):
        for ref, count, base in ((xl_ref, H, 0), (v_ref, nx, H), (xr_ref, H, H + nx)):

            def body(i, carry):
                out_ref[base + i] = pack_pair(ref[0, i, rows], ref[1, i, rows], top)
                return carry

            lax.fori_loop(0, count, body, 0, unroll=2)


def early_kernel(b_ref, ct_ref, v1_ref, v2_ref, out_ref):
    fields = ((b_ref, 0, False), (v1_ref, H, True), (v2_ref, 0, True))
    gram_rows(fields, ct_ref, EARLY, out_ref)


def second_kernel(
    e_ref, xl_ref, xr_ref, yl_ref, yr_ref, p_ref, n_ref, b_ref, ct_ref, v1_ref, v2_ref,
    w2_ref, w3_ref, v3_ref, v4_ref, out_ref,
    u_ref, v_ref,
):
    nx, ny, _ = ct_ref.shape
    planes = nx + 2 * H
    th = later_shift(gram_entries(e_ref, EARLY[:2], {}))

    for ref, count, base in ((xl_ref, H, 0), (v2_ref, nx, H), (xr_ref, H, H + nx)):

        def fill(i, carry):
            at = base + i
            tail = unpack_pair(yr_ref[at], yl_ref[at])
            v = tuple(jnp.concatenate([ref[part, i], tail[part]], axis=0) for part in range(2))
            u = cmul((p_ref[0, at], p_ref[1, at]), v)
            for part in range(2):
                v_ref[part, at] = v[part]
                u_ref[part, at] = u[part]
            return carry

        lax.fori_loop(0, count, fill, 0, unroll=2)

    half_step(u_ref, p_ref, w2_ref, 1, planes - 1)
    apply_wide(w2_ref, n_ref, v_ref, p_ref, th, v3_ref, u_ref, 2, planes - 2)
    half_step(u_ref, p_ref, w3_ref, 3, planes - 3)
    apply_own(w3_ref, n_ref, v3_ref, th, v4_ref)
    fields = (
        (b_ref, 0, False), (v1_ref, H, True), (v2_ref, 0, True), (v3_ref, H, True),
        (v4_ref, 0, True),
    )
    gram_rows(fields, ct_ref, LATE, out_ref)


def recurrences(shifts, gram):
    def inner(x, y):
        total = None
        for i, xi in enumerate(x):
            part = None
            for j, yj in enumerate(y):
                t = cmul(gram[i, j], yj)
                part = t if part is None else cadd(part, t)
            t = cmul(cconj(xi), part)
            total = t if total is None else cadd(total, t)
        return total

    def apply(x):
        scaled = [cmul(th, c) for th, c in zip(shifts, x)]
        return [scaled[0]] + [cadd(x[k], scaled[k + 1]) for k in range(len(x) - 1)] + [x[-1]]

    def lincomb(x, s, y):
        out = []
        for k in range(max(len(x), len(y))):
            a = x[k] if k < len(x) else None
            b = cmul(s, y[k]) if k < len(y) else None
            out.append(b if a is None else a if b is None else cadd(a, b))
        return out

    def neg(s):
        return (-s[0], -s[1])

    one = (jnp.ones((1, 1), F32), jnp.zeros((1, 1), F32))
    residual, direction, shadow, answer = [one], [one], [one], []
    rho = inner(shadow, residual)
    for step in range(2):
        image = apply(direction)
        alpha = cdiv(rho, inner(shadow, image))
        half = lincomb(residual, neg(alpha), image)
        second = apply(half)
        prod = inner(second, half)
        norm = inner(second, second)[0] + EPSILON
        omega = (prod[0] / norm, prod[1] / norm)
        answer = lincomb(lincomb(answer, alpha, direction), omega, half)
        residual = lincomb(half, neg(omega), second)
        if step == 0:
            rho_next = inner(shadow, residual)
            beta = cmul(cdiv(rho_next, rho), cdiv(alpha, omega))
            direction = lincomb(residual, beta, lincomb(direction, neg(omega), image))
            rho = rho_next
    return answer, residual


def final_kernel(
    e_ref, g_ref, b_ref, cf_ref, ct_ref,
    w0_ref, w1_ref, w2_ref, w3_ref, v1_ref, v2_ref, v3_ref, v4_ref,
    sol_ref, res_ref,
):
    nx, ny, nz = cf_ref.shape
    entries = gram_entries(g_ref, LATE, gram_entries(e_ref, EARLY, {}))
    th = later_shift(entries)
    answer, residual = recurrences(SHIFTS + (th, th), entries)

    def spread(c):
        return tuple(jnp.broadcast_to(x, (8, nz)) for x in c)

    answer, residual = [spread(c) for c in answer], [spread(c) for c in residual]

    def body(i, carry):
        for a in range(0, ny, 8):
            rows = pl.ds(a, 8)
            acc = None
            for c, ref in zip(answer, (w0_ref, w1_ref, w2_ref, w3_ref)):
                t = cmul(c, (ref[0, i + H, rows], ref[1, i + H, rows]))
                acc = t if acc is None else cadd(acc, t)
            inv = 1.0 / cf_ref[i, rows]
            sol_ref[0, i, rows] = acc[0] * inv
            sol_ref[1, i, rows] = acc[1] * inv
            acc = None
            for c, ref, base in zip(residual[1:], (v1_ref, v2_ref, v3_ref, v4_ref), (H, 0, H, 0)):
                t = cmul(c, (ref[0, i + base, rows], ref[1, i + base, rows]))
                acc = t if acc is None else cadd(acc, t)
            ct = ct_ref[i, rows]
            t = cmul(residual[0], (b_ref[0, i, rows], b_ref[1, i, rows]))
            res_ref[0, i, rows] = acc[0] * ct + t[0]
            res_ref[1, i, rows] = acc[1] * ct + t[1]
        return carry

    lax.fori_loop(0, nx, body, 0)


def call(kernel, outs, scratch, *args, alias=None):
    return pl.pallas_call(
        kernel,
        out_shape=[jax.ShapeDtypeStruct(s, F32) for s in outs],
        in_specs=vmem(len(args)),
        out_specs=vmem(len(outs)),
        scratch_shapes=[pltpu.VMEM(s, F32) for s in scratch],
        input_output_aliases=alias or {},
        compiler_params=pltpu.CompilerParams(vmem_limit_bytes=LIMIT),
    )(*args)


def both_ways(to_lower, to_upper, axis):
    n = lax.axis_size(axis)
    up = [(i, i + 1) for i in range(n - 1)]
    down = [(i + 1, i) for i in range(n - 1)]
    return lax.ppermute(to_upper, axis, up), lax.ppermute(to_lower, axis, down)


def local(b, cf, ct, mr, d):
    nx, ny, nz = cf.shape
    peers = lax.axis_size("gx") * lax.axis_size("gy")
    planes = nx + 2 * H
    own = (2, nx, ny, nz)
    ext = (2, planes, ny + 2 * H, nz)
    face = (2, H, ny, nz)
    rim = (nx + 3 * nx // 2, 8, nz)
    corner = (2, H + 3 * H // 2, 8, nz)

    lo, hi, top, bot = call(
        edges_kernel, [(5, H, ny, nz), (5, H, ny, nz), rim, rim], [], b, cf, ct, mr, d
    )
    yl, yr = both_ways(top, bot, "gy")
    xl, xr = both_ways(lo, hi, "gx")
    state = call(own_kernel, [ext] * 4, [], b, cf, ct, mr, d)
    lo, hi = call(corners_kernel, [corner] * 2, [], yl, yr)
    cl, cr = both_ways(lo, hi, "gx")
    state = call(
        sides_kernel, [ext] * 4, [], xl, xr, yl, yr, *state, alias={4 + k: k for k in range(4)}
    )
    p, n, _, _, w0, w1, v1, v2, sl, sr = call(
        first_kernel, [ext] * 7 + [own, face, face], [], cl, cr, *state,
        alias={2 + k: k for k in range(4)},
    )
    xl, xr = both_ways(sl, sr, "gx")
    early = call(early_kernel, [(peers, 1, 128)], [], b, ct, v1, v2)[0]
    early = lax.all_to_all(early, AXES, 0, 0)
    top, bot = call(pack_kernel, [(planes, 8, nz)] * 2, [], xl, xr, v2)
    yl, yr = both_ways(top, bot, "gy")
    w2, w3, v3, v4, late = call(
        second_kernel, [ext, ext, ext, own, (peers, 1, 128)], [ext, ext],
        early, xl, xr, yl, yr, p, n, b, ct, v1, v2,
    )
    late = lax.all_to_all(late, AXES, 0, 0)
    return tuple(
        call(final_kernel, [own, own], [], early, late, b, cf, ct, w0, w1, w2, w3, v1, v2, v3, v4)
    )


def solution(mesh):
    field, coef = P(None, "gx", "gy", None), P("gx", "gy", None)
    return jax.shard_map(
        local,
        mesh=mesh,
        in_specs=(field, coef, coef, coef, coef),
        out_specs=(field, field),
        check_vma=False,
    )
```

```python
import jax
import jax.numpy as jnp
from jax import lax
from jax.experimental import pallas as pl
from jax.experimental.pallas import tpu as pltpu
from jax.sharding import PartitionSpec as P

OMEGA = 0.8
EPSILON = 1e-06
H = 4
AXES = ("gx", "gy")
F32 = jnp.float32
LIMIT = 24 * 1024 * 1024
FALLBACK = (0.72, -0.28)


def vmem(n):
    return [pl.BlockSpec(memory_space=pltpu.VMEM)] * n


def cmul(a, b):
    return (a[0] * b[0] - a[1] * b[1], a[0] * b[1] + a[1] * b[0])


def cconj(a):
    return (a[0], -a[1])


def cadd(a, b):
    return (a[0] + b[0], a[1] + b[1])


def csub(a, b):
    return (a[0] - b[0], a[1] - b[1])


def cdiv(n, d):
    scale = d[0] * d[0] + d[1] * d[1]
    return (
        (n[0] * d[0] + n[1] * d[1]) / scale,
        (n[1] * d[0] - n[0] * d[1]) / scale,
    )


def smooth_yz(plane):
    rows, lanes = plane.shape
    y = plane + plane + pltpu.roll(plane, 1, 0) + pltpu.roll(plane, rows - 1, 0)
    lane = lax.broadcasted_iota(jnp.int32, plane.shape, 1)
    up = jnp.where(lane == 0, 0.0, pltpu.roll(y, 1, 1))
    down = jnp.where(lane == lanes - 1, 0.0, pltpu.roll(y, lanes - 1, 1))
    return y + y + up + down


def weighted(ref, i):
    out = []
    for part in range(2):
        mid = ref[part, i]
        total = smooth_yz(ref[part, i - 1] + mid + mid + ref[part, i + 1])
        out.append((total - 8.0 * mid) * (1.0 / 160.0))
    return tuple(out)


def coefficients(c, mr, d):
    shift = d + 0.5 * mr
    mod = mr * mr + shift * shift
    den = mod * c
    inv = 1.0 / jnp.where(den == 0.0, 1.0, den)
    k = OMEGA * c * c * inv
    rc = mod * inv
    return (k * mr, -(k * shift)), (rc * mr, rc * d)


def loop(ranges, body):
    for lo, hi in ranges:

        def step(i, carry):
            body(i)
            return carry

        lax.fori_loop(lo, hi, step, 0, unroll=2)


def half_step(u_ref, p_ref, w_ref, ranges):
    def body(i):
        pw = cmul((p_ref[0, i], p_ref[1, i]), weighted(u_ref, i))
        w_ref[0, i] = 1.2 * u_ref[0, i] + pw[0]
        w_ref[1, i] = 1.2 * u_ref[1, i] + pw[1]

    loop(ranges, body)


def image(w_ref, n_ref, i):
    nw = cmul((n_ref[0, i], n_ref[1, i]), (w_ref[0, i], w_ref[1, i]))
    return csub(nw, weighted(w_ref, i))


def advance(w_ref, n_ref, v_ref, th, next_ref, ranges, p_ref=None, u_ref=None):
    def body(i):
        y = csub(image(w_ref, n_ref, i), cmul(th, (v_ref[0, i], v_ref[1, i])))
        for part in range(2):
            next_ref[part, i] = y[part]
        if p_ref is not None:
            u = cmul((p_ref[0, i], p_ref[1, i]), y)
            for part in range(2):
                u_ref[part, i] = u[part]

    loop(ranges, body)


def inside(planes, k):
    return [(H + k, planes - H - k)]


def outside(planes, k):
    return [(k, H + k), (planes - H - k, planes - k)]


def two_applications(part_of, planes, th, p_ref, n_ref, u_ref, v_ref, w_refs, next_refs):
    half_step(u_ref, p_ref, w_refs[0], part_of(planes, 1))
    advance(w_refs[0], n_ref, v_ref, th, next_refs[0], part_of(planes, 2), p_ref, u_ref)
    half_step(u_ref, p_ref, w_refs[1], part_of(planes, 3))
    advance(w_refs[1], n_ref, next_refs[0], th, next_refs[1], part_of(planes, 4))


def total_of(ref):
    rows = ref[...].reshape(ref.shape[0], ref.shape[-1])
    tot = jnp.sum(rows, axis=0, keepdims=True)
    lane = lax.broadcasted_iota(jnp.int32, tot.shape, 1)
    return lambda k: jnp.sum(jnp.where(lane == k, tot, 0.0), axis=1, keepdims=True)


def pack_lanes(values, first=0):
    lane = lax.broadcasted_iota(jnp.int32, (1, 128), 1)
    row = jnp.zeros((1, 128), F32)
    for k, v in enumerate(values, first):
        s = jnp.sum(jnp.sum(v, axis=0, keepdims=True), axis=1, keepdims=True)
        row = jnp.where(lane == k, s, row)
    return row


def fold(x):
    out = x[:, :128]
    for b in range(128, x.shape[1], 128):
        out = out + x[:, b : b + 128]
    return out


def pairs_of(rights):
    return [(left, right) for right in rights for left in range(right + 1)]


def gram_rows(fields, ct_ref, pairs, first=0):
    nx, ny, _ = ct_ref.shape
    used = sorted({k for pair in pairs for k in pair})
    count = sum(1 if left == right else 2 for left, right in pairs)

    def body(i, acc):
        acc = list(acc)
        for a in range(0, ny, 8):
            rows = pl.ds(a, 8)
            ct = ct_ref[i, rows]
            vs = {}
            for k in used:
                ref, base, scaled = fields[k]
                v = (ref[0, i + base, rows], ref[1, i + base, rows])
                vs[k] = (ct * v[0], ct * v[1]) if scaled else v
            k = 0
            for left, right in pairs:
                (lr, li), (rr, ri) = vs[left], vs[right]
                acc[k] = acc[k] + fold(lr * rr + li * ri)
                k += 1
                if right > left:
                    acc[k] = acc[k] + fold(lr * ri - li * rr)
                    k += 1
        return tuple(acc)

    acc = lax.fori_loop(0, nx, body, (jnp.zeros((8, 128), F32),) * count)
    return pack_lanes(acc, first)


def put(row, out_ref):
    for k in range(out_ref.shape[0]):
        out_ref[k] = row


def gram_entries(pick, pairs, entries):
    k = 0
    for left, right in pairs:
        if left == right:
            entries[left, right] = (pick(k), jnp.zeros((1, 1), F32))
            k += 1
        else:
            entries[left, right] = (pick(k), pick(k + 1))
            entries[right, left] = cconj(entries[left, right])
            k += 2
    return entries


def shift_from(ref):
    pick = total_of(ref)
    den = pick(2)
    safe = jnp.where(den > 0.0, den, 1.0)
    return tuple(jnp.where(den > 0.0, pick(k) / safe, FALLBACK[k]) for k in range(2))


EARLY = pairs_of((0, 1, 2))
LATE = pairs_of((3, 4))


def pack_pair(first, second, top):
    sub = lax.broadcasted_iota(jnp.int32, first.shape, 0)
    rolled = pltpu.roll(second, 4, 0)
    if top:
        return jnp.where(sub < 4, first, rolled)
    return jnp.where(sub < 4, rolled, first)


def unpack_pair(right, left):
    sub = lax.broadcasted_iota(jnp.int32, right.shape, 0)
    first = jnp.where(sub < 4, right, left)
    second = pltpu.roll(jnp.where(sub < 4, left, right), 4, 0)
    return first, second


def own_values(b_ref, cf_ref, ct_ref, mr_ref, d_ref):
    def get(i, rows):
        ct = ct_ref[i, rows]
        r = 1.0 / ct
        return (
            b_ref[0, i, rows] * r,
            b_ref[1, i, rows] * r,
            cf_ref[i, rows] * ct,
            mr_ref[i, rows],
            d_ref[i, rows],
        )

    return get


def fetch(pairs, sems):
    copies = [pltpu.make_async_copy(a, b, sems.at[k]) for k, (a, b) in enumerate(pairs)]
    for c in copies:
        c.start()
    for c in copies:
        c.wait()


def rows_kernel(b_ref, cf_ref, ct_ref, mr_ref, d_ref, top_ref, bot_ref, *scratch):
    blocks, coefs, sems = scratch
    nx, ny, _ = cf_ref.shape
    pairs = []
    for side, at in enumerate((0, ny - 8)):
        rows = pl.ds(at, 8)
        pairs.append((b_ref.at[:, :, rows], blocks.at[side]))
        for k, ref in enumerate((cf_ref, ct_ref, mr_ref, d_ref)):
            pairs.append((ref.at[:, rows], coefs.at[side, k]))
    fetch(pairs, sems)
    for side, out_ref in enumerate((top_ref, bot_ref)):
        get = own_values(blocks.at[side], *(coefs.at[side, k] for k in range(4)))
        top = side == 0

        def body(j, carry):
            a, b = get(2 * j, pl.ds(0, 8)), get(2 * j + 1, pl.ds(0, 8))
            out_ref[2 * j] = pack_pair(a[0], a[1], top)
            out_ref[2 * j + 1] = pack_pair(b[0], b[1], top)
            for f in range(3):
                out_ref[nx + f * nx // 2 + j] = pack_pair(a[2 + f], b[2 + f], top)
            return carry

        lax.fori_loop(0, nx // 2, body, 0, unroll=2)


def planes_kernel(after_ref, b_ref, cf_ref, ct_ref, mr_ref, d_ref, lo_ref, hi_ref, *scratch):
    blocks, coefs, sems = scratch
    nx, ny, _ = cf_ref.shape
    pairs = []
    for side, at in enumerate((0, nx - H)):
        span = pl.ds(at, H)
        pairs.append((b_ref.at[:, span], blocks.at[side]))
        for k, ref in enumerate((cf_ref, ct_ref, mr_ref, d_ref)):
            pairs.append((ref.at[span], coefs.at[side, k]))
    fetch(pairs, sems)
    for side, out_ref in enumerate((lo_ref, hi_ref)):
        get = own_values(blocks.at[side], *(coefs.at[side, k] for k in range(4)))
        for i in range(H):
            for f, value in enumerate(get(i, pl.ds(0, ny))):
                out_ref[f, i] = value


def corners_kernel(yl_ref, yr_ref, lo_ref, hi_ref):
    count = yl_ref.shape[0]
    nx = count * 2 // 5
    for k, ref in enumerate((yl_ref, yr_ref)):
        for out_ref, base in ((lo_ref, 0), (hi_ref, nx - H)):
            for i in range(H):
                out_ref[k, i] = ref[base + i]
            for f in range(3):
                for j in range(H // 2):
                    at = nx + f * nx // 2 + base // 2 + j
                    out_ref[k, H + f * H // 2 + j] = ref[at]


def store_fields(refs, plane, rows, v, c, mr, d):
    p_ref, n_ref, u_ref, v_ref = refs
    p, n = coefficients(c, mr, d)
    u = cmul(p, v)
    for part in range(2):
        p_ref[part, plane, rows] = p[part]
        n_ref[part, plane, rows] = n[part]
        u_ref[part, plane, rows] = u[part]
        v_ref[part, plane, rows] = v[part]


def own_kernel(b_ref, cf_ref, ct_ref, mr_ref, d_ref, p_ref, n_ref, u_ref, v_ref, out_ref, w_ref):
    nx, ny, nz = cf_ref.shape
    get = own_values(b_ref, cf_ref, ct_ref, mr_ref, d_ref)
    rows, rest = pl.ds(0, ny), pl.ds(ny, 8)
    zero = jnp.zeros((8, nz), F32)

    def body(i):
        vr, vi, c, mr, d = get(i, rows)
        store_fields((p_ref, n_ref, u_ref, v_ref), i + H, rows, (vr, vi), c, mr, d)
        for part in range(2):
            p_ref[part, i + H, rest] = zero
            u_ref[part, i + H, rest] = zero

    loop([(0, nx)], body)
    blank = jnp.zeros((ny + 8, nz), F32)
    for ref in (u_ref, w_ref):
        for part in range(2):
            ref[part, H - 1] = blank
            ref[part, nx + H] = blank
    half_step(u_ref, p_ref, w_ref, [(H, nx + H)])

    def dots(i, acc):
        acc = list(acc)
        y = image(w_ref, n_ref, i + H)
        for a in range(0, ny, 8):
            ct = ct_ref[i, pl.ds(a, 8)]
            yr, yi = y[0][a : a + 8] * ct, y[1][a : a + 8] * ct
            br, bi = b_ref[0, i, pl.ds(a, 8)], b_ref[1, i, pl.ds(a, 8)]
            acc[0] = acc[0] + fold(br * yr + bi * yi)
            acc[1] = acc[1] + fold(br * yi - bi * yr)
            acc[2] = acc[2] + fold(br * br + bi * bi)
        return tuple(acc)

    acc = lax.fori_loop(0, nx, dots, (jnp.zeros((8, 128), F32),) * 3, unroll=2)
    put(pack_lanes(acc), out_ref)


def tails(refs, left, right, ny, fields, coefs, planes):
    rows = pl.ds(ny, 8)
    v = [unpack_pair(right(k), left(k)) for k in fields]
    c = [unpack_pair(right(k), left(k)) for k in coefs]
    for k in range(2):
        store_fields(refs, planes[k], rows, v[k], c[0][k], c[1][k], c[2][k])


def sides_kernel(th_ref, xl_ref, xr_ref, yl_ref, yr_ref, *refs):
    p_ref, n_ref, u_ref, v_ref, w0_ref, w1_ref, v1_ref, v2_ref = refs[4:]
    state = (p_ref, n_ref, u_ref, v_ref)
    ny = xl_ref.shape[2]
    planes = p_ref.shape[1]
    nx = planes - 2 * H
    rows = pl.ds(0, ny)
    for ref, base in ((xl_ref, 0), (xr_ref, nx + H)):

        def side(i):
            vr, vi, c, mr, d = (ref[f, i] for f in range(5))
            store_fields(state, base + i, rows, (vr, vi), c, mr, d)

        loop([(0, H)], side)

    def pair(j):
        coefs = [nx + f * nx // 2 + j for f in range(3)]
        at = (H + 2 * j, H + 2 * j + 1)
        own = (2 * j, 2 * j + 1)
        tails(state, lambda k: yl_ref[k], lambda k: yr_ref[k], ny, own, coefs, at)

    loop([(0, nx // 2)], pair)
    th = shift_from(th_ref)
    two_applications(inside, planes, th, *state, (w0_ref, w1_ref), (v1_ref, v2_ref))


def first_kernel(th_ref, cl_ref, cr_ref, *refs):
    p_ref, n_ref, u_ref, v_ref, w0_ref, w1_ref, v1_ref, v2_ref, top_ref, bot_ref = refs[8:]
    state = (p_ref, n_ref, u_ref, v_ref)
    planes = p_ref.shape[1]
    nx, ny = planes - 2 * H, p_ref.shape[2] - 8
    for ref, base in ((cl_ref, 0), (cr_ref, nx + H)):
        for j in range(H // 2):
            coefs = [H + f * H // 2 + j for f in range(3)]
            at = (base + 2 * j, base + 2 * j + 1)
            own = (2 * j, 2 * j + 1)
            tails(state, lambda k: ref[0, k], lambda k: ref[1, k], ny, own, coefs, at)
    th = shift_from(th_ref)
    two_applications(outside, planes, th, *state, (w0_ref, w1_ref), (v1_ref, v2_ref))
    for out_ref, rows, top in ((top_ref, pl.ds(0, 8), True), (bot_ref, pl.ds(ny - 8, 8), False)):

        def pack(i):
            a, b = v2_ref[0, i + H, rows], v2_ref[1, i + H, rows]
            out_ref[i] = pack_pair(a, b, top)

        loop([(0, nx)], pack)


def early_kernel(b_ref, ct_ref, v1_ref, v2_ref, out_ref):
    fields = ((b_ref, 0, False), (v1_ref, H, True), (v2_ref, H, True))
    put(gram_rows(fields, ct_ref, EARLY), out_ref)


def rows_back_kernel(yl_ref, yr_ref, _, v_ref, lo_ref, hi_ref):
    nx, ny = yl_ref.shape[0], v_ref.shape[2] - 8
    rows = pl.ds(ny, 8)

    def tail(i):
        for part, value in enumerate(unpack_pair(yr_ref[i], yl_ref[i])):
            v_ref[part, i + H, rows] = value

    loop([(0, nx)], tail)
    for part in range(2):
        for i in range(H):
            lo_ref[part, i] = v_ref[part, H + i]
            hi_ref[part, i] = v_ref[part, nx + i]


def inner_kernel(th_ref, p_ref, n_ref, v_ref, u_ref, w2_ref, w3_ref, v3_ref, v4_ref):
    planes = p_ref.shape[1]
    th = shift_from(th_ref)

    def fill(i):
        u = cmul((p_ref[0, i], p_ref[1, i]), (v_ref[0, i], v_ref[1, i]))
        for part in range(2):
            u_ref[part, i] = u[part]

    loop([(H, planes - H)], fill)
    two_applications(
        inside, planes, th, p_ref, n_ref, u_ref, v_ref, (w2_ref, w3_ref), (v3_ref, v4_ref)
    )


def second_kernel(th_ref, e_ref, xl_ref, xr_ref, p_ref, n_ref, b_ref, ct_ref, v1_ref, *refs):
    v2_ref, u_ref, w2_ref, w3_ref, v3_ref, v4_ref, out_ref = refs[6:]
    planes = p_ref.shape[1]
    th = shift_from(th_ref)
    for ref, base in ((xl_ref, 0), (xr_ref, planes - H)):
        for i in range(H):
            v = (ref[0, i], ref[1, i])
            u = cmul((p_ref[0, base + i], p_ref[1, base + i]), v)
            for part in range(2):
                v2_ref[part, base + i] = v[part]
                u_ref[part, base + i] = u[part]
    two_applications(
        outside, planes, th, p_ref, n_ref, u_ref, v2_ref, (w2_ref, w3_ref), (v3_ref, v4_ref)
    )
    fields = (
        (b_ref, 0, False), (v1_ref, H, True), (v2_ref, H, True), (v3_ref, H, True),
        (v4_ref, H, True),
    )
    put(e_ref[0] + gram_rows(fields, ct_ref, LATE, 9), out_ref)


def recurrences(th, gram):
    def inner(x, y):
        total = None
        for i, xi in enumerate(x):
            part = None
            for j, yj in enumerate(y):
                t = cmul(gram[i, j], yj)
                part = t if part is None else cadd(part, t)
            t = cmul(cconj(xi), part)
            total = t if total is None else cadd(total, t)
        return total

    def apply(x):
        scaled = [cmul(th, c) for c in x]
        return [scaled[0]] + [cadd(x[k], scaled[k + 1]) for k in range(len(x) - 1)] + [x[-1]]

    def lincomb(x, s, y):
        out = []
        for k in range(max(len(x), len(y))):
            a = x[k] if k < len(x) else None
            b = cmul(s, y[k]) if k < len(y) else None
            out.append(b if a is None else a if b is None else cadd(a, b))
        return out

    def neg(s):
        return (-s[0], -s[1])

    one = (jnp.ones((1, 1), F32), jnp.zeros((1, 1), F32))
    residual, direction, shadow, answer = [one], [one], [one], []
    rho = inner(shadow, residual)
    for step in range(2):
        image = apply(direction)
        alpha = cdiv(rho, inner(shadow, image))
        half = lincomb(residual, neg(alpha), image)
        second = apply(half)
        prod = inner(second, half)
        norm = inner(second, second)[0] + EPSILON
        omega = (prod[0] / norm, prod[1] / norm)
        answer = lincomb(lincomb(answer, alpha, direction), omega, half)
        residual = lincomb(half, neg(omega), second)
        if step == 0:
            rho_next = inner(shadow, residual)
            beta = cmul(cdiv(rho_next, rho), cdiv(alpha, omega))
            direction = lincomb(residual, beta, lincomb(direction, neg(omega), image))
            rho = rho_next
    return answer, residual


def final_kernel(
    th_ref, g_ref, b_ref, cf_ref, ct_ref,
    w0_ref, w1_ref, w2_ref, w3_ref, v1_ref, v2_ref, v3_ref, v4_ref,
    sol_ref, res_ref,
):
    nx, ny, nz = cf_ref.shape
    th = shift_from(th_ref)
    entries = gram_entries(total_of(g_ref), EARLY + LATE, {})
    answer, residual = recurrences(th, entries)

    def spread(c):
        return tuple(jnp.broadcast_to(x, (8, nz)) for x in c)

    answer, residual = [spread(c) for c in answer], [spread(c) for c in residual]

    def body(i, carry):
        for a in range(0, ny, 8):
            rows = pl.ds(a, 8)
            acc = None
            for c, ref in zip(answer, (w0_ref, w1_ref, w2_ref, w3_ref)):
                t = cmul(c, (ref[0, i + H, rows], ref[1, i + H, rows]))
                acc = t if acc is None else cadd(acc, t)
            inv = 1.0 / cf_ref[i, rows]
            sol_ref[0, i, rows] = acc[0] * inv
            sol_ref[1, i, rows] = acc[1] * inv
            acc = None
            for c, ref in zip(residual[1:], (v1_ref, v2_ref, v3_ref, v4_ref)):
                t = cmul(c, (ref[0, i + H, rows], ref[1, i + H, rows]))
                acc = t if acc is None else cadd(acc, t)
            ct = ct_ref[i, rows]
            t = cmul(residual[0], (b_ref[0, i, rows], b_ref[1, i, rows]))
            res_ref[0, i, rows] = acc[0] * ct + t[0]
            res_ref[1, i, rows] = acc[1] * ct + t[1]
        return carry

    lax.fori_loop(0, nx, body, 0)


def call(kernel, outs, scratch, *args, alias=None):
    return pl.pallas_call(
        kernel,
        out_shape=[jax.ShapeDtypeStruct(s, F32) for s in outs],
        in_specs=vmem(len(args)),
        out_specs=vmem(len(outs)),
        scratch_shapes=[pltpu.VMEM(s, F32) for s in scratch],
        input_output_aliases=alias or {},
        compiler_params=pltpu.CompilerParams(vmem_limit_bytes=LIMIT),
    )(*args)


def edge_call(kernel, outs, scratch, *args):
    return pl.pallas_call(
        kernel,
        out_shape=[jax.ShapeDtypeStruct(s, F32) for s in outs],
        in_specs=[pl.BlockSpec(memory_space=pl.ANY)] * len(args),
        out_specs=vmem(len(outs)),
        scratch_shapes=[pltpu.VMEM(s, F32) for s in scratch] + [pltpu.SemaphoreType.DMA((10,))],
        compiler_params=pltpu.CompilerParams(vmem_limit_bytes=LIMIT),
    )(*args)


def both_ways(to_lower, to_upper, axis):
    n = lax.axis_size(axis)
    up = [(i, i + 1) for i in range(n - 1)]
    down = [(i + 1, i) for i in range(n - 1)]
    return lax.ppermute(to_upper, axis, up), lax.ppermute(to_lower, axis, down)


def local(b, cf, ct, mr, d):
    nx, ny, nz = cf.shape
    peers = lax.axis_size("gx") * lax.axis_size("gy")
    planes = nx + 2 * H
    own = (2, nx, ny, nz)
    ext = (2, planes, ny + 2 * H, nz)
    face = (2, H, ny + 2 * H, nz)
    rim = (nx + 3 * nx // 2, 8, nz)
    corner = (2, H + 3 * H // 2, 8, nz)
    inputs = (b, cf, ct, mr, d)

    top, bot = edge_call(
        rows_kernel, [rim, rim], [(2, 2, nx, 8, nz), (2, 4, nx, 8, nz)], *inputs
    )
    yl, yr = both_ways(top, bot, "gy")
    lo, hi = edge_call(
        planes_kernel, [(5, H, ny, nz)] * 2, [(2, 2, H, ny, nz), (2, 4, H, ny, nz)], top, *inputs
    )
    xl, xr = both_ways(lo, hi, "gx")
    *state, th = call(own_kernel, [ext] * 4 + [(peers, 1, 128)], [ext], *inputs)
    th = lax.all_to_all(th, AXES, 0, 0)
    lo, hi = call(corners_kernel, [corner] * 2, [], yl, yr)
    cl, cr = both_ways(lo, hi, "gx")
    state = call(
        sides_kernel, [ext] * 8, [], th, xl, xr, yl, yr, *state,
        alias={5 + k: k for k in range(4)},
    )
    p, n, _, _, w0, w1, v1, v2, top, bot = call(
        first_kernel, [ext] * 8 + [(nx, 8, nz)] * 2, [], th, cl, cr, *state,
        alias={3 + k: k for k in range(8)},
    )
    yl, yr = both_ways(top, bot, "gy")
    early = call(early_kernel, [(1, 1, 128)], [], b, ct, v1, v2)[0]
    v2, lo, hi = call(rows_back_kernel, [ext, face, face], [], yl, yr, v2, alias={2: 0})
    xl, xr = both_ways(lo, hi, "gx")
    state = call(inner_kernel, [ext] * 5, [], th, p, n, v2)
    v2, _, w2, w3, v3, v4, gram = call(
        second_kernel, [ext] * 6 + [(peers, 1, 128)], [],
        th, early, xl, xr, p, n, b, ct, v1, v2, *state,
        alias={9 + k: k for k in range(6)},
    )
    gram = lax.all_to_all(gram, AXES, 0, 0)
    return tuple(
        call(final_kernel, [own, own], [], th, gram, b, cf, ct, w0, w1, w2, w3, v1, v2, v3, v4)
    )


def solution(mesh):
    field, coef = P(None, "gx", "gy", None), P("gx", "gy", None)
    return jax.shard_map(
        local,
        mesh=mesh,
        in_specs=(field, coef, coef, coef, coef),
        out_specs=(field, field),
        check_vma=False,
    )
```

```python
import jax
import jax.numpy as jnp
from jax import lax
from jax.experimental import pallas as pl
from jax.experimental.pallas import tpu as pltpu
from jax.sharding import PartitionSpec as P

OMEGA = 0.8
EPSILON = 1e-06
H = 4
AXES = ("gx", "gy")
F32 = jnp.float32
LIMIT = 24 * 1024 * 1024
FALLBACK = (0.72, -0.28)


def vmem(n):
    return [pl.BlockSpec(memory_space=pltpu.VMEM)] * n


def cmul(a, b):
    return (a[0] * b[0] - a[1] * b[1], a[0] * b[1] + a[1] * b[0])


def cconj(a):
    return (a[0], -a[1])


def cadd(a, b):
    return (a[0] + b[0], a[1] + b[1])


def csub(a, b):
    return (a[0] - b[0], a[1] - b[1])


def cdiv(n, d):
    scale = d[0] * d[0] + d[1] * d[1]
    return (
        (n[0] * d[0] + n[1] * d[1]) / scale,
        (n[1] * d[0] - n[0] * d[1]) / scale,
    )


def smooth_yz(plane):
    rows, lanes = plane.shape
    y = plane + plane + pltpu.roll(plane, 1, 0) + pltpu.roll(plane, rows - 1, 0)
    lane = lax.broadcasted_iota(jnp.int32, plane.shape, 1)
    up = jnp.where(lane == 0, 0.0, pltpu.roll(y, 1, 1))
    down = jnp.where(lane == lanes - 1, 0.0, pltpu.roll(y, lanes - 1, 1))
    return y + y + up + down


def weighted(ref, i):
    out = []
    for part in range(2):
        mid = ref[part, i]
        total = smooth_yz(ref[part, i - 1] + mid + mid + ref[part, i + 1])
        out.append((total - 8.0 * mid) * (1.0 / 160.0))
    return tuple(out)


def coefficients(c, mr, d):
    shift = d + 0.5 * mr
    mod = mr * mr + shift * shift
    den = mod * c
    inv = 1.0 / jnp.where(den == 0.0, 1.0, den)
    k = OMEGA * c * c * inv
    rc = mod * inv
    return (k * mr, -(k * shift)), (rc * mr, rc * d)


def loop(ranges, body):
    for lo, hi in ranges:

        def step(i, carry):
            body(i)
            return carry

        lax.fori_loop(lo, hi, step, 0, unroll=2)


def half_step(u_ref, p_ref, w_ref, ranges):
    def body(i):
        pw = cmul((p_ref[0, i], p_ref[1, i]), weighted(u_ref, i))
        w_ref[0, i] = 1.2 * u_ref[0, i] + pw[0]
        w_ref[1, i] = 1.2 * u_ref[1, i] + pw[1]

    loop(ranges, body)


def image(w_ref, n_ref, i):
    nw = cmul((n_ref[0, i], n_ref[1, i]), (w_ref[0, i], w_ref[1, i]))
    return csub(nw, weighted(w_ref, i))


def advance(w_ref, n_ref, v_ref, th, next_ref, ranges, p_ref=None, u_ref=None):
    def body(i):
        y = csub(image(w_ref, n_ref, i), cmul(th, (v_ref[0, i], v_ref[1, i])))
        for part in range(2):
            next_ref[part, i] = y[part]
        if p_ref is not None:
            u = cmul((p_ref[0, i], p_ref[1, i]), y)
            for part in range(2):
                u_ref[part, i] = u[part]

    loop(ranges, body)


def inside(planes, k):
    return [(H + k, planes - H - k)]


def outside(planes, k):
    return [(k, H + k), (planes - H - k, planes - k)]


def two_applications(part_of, planes, th, p_ref, n_ref, u_ref, v_ref, w_refs, next_refs):
    half_step(u_ref, p_ref, w_refs[0], part_of(planes, 1))
    advance(w_refs[0], n_ref, v_ref, th, next_refs[0], part_of(planes, 2), p_ref, u_ref)
    half_step(u_ref, p_ref, w_refs[1], part_of(planes, 3))
    advance(w_refs[1], n_ref, next_refs[0], th, next_refs[1], part_of(planes, 4))


def total_of(ref):
    rows = ref[...].reshape(ref.shape[0], ref.shape[-1])
    tot = jnp.sum(rows, axis=0, keepdims=True)
    lane = lax.broadcasted_iota(jnp.int32, tot.shape, 1)
    return lambda k: jnp.sum(jnp.where(lane == k, tot, 0.0), axis=1, keepdims=True)


def pack_lanes(values, first=0):
    lane = lax.broadcasted_iota(jnp.int32, (1, 128), 1)
    row = jnp.zeros((1, 128), F32)
    for k, v in enumerate(values, first):
        s = jnp.sum(jnp.sum(v, axis=0, keepdims=True), axis=1, keepdims=True)
        row = jnp.where(lane == k, s, row)
    return row


def fold(x):
    out = x[:, :128]
    for b in range(128, x.shape[1], 128):
        out = out + x[:, b : b + 128]
    return out


def pairs_of(rights):
    return [(left, right) for right in rights for left in range(right + 1)]


def gram_rows(fields, ct_ref, pairs, first=0):
    nx, ny, _ = ct_ref.shape
    used = sorted({k for pair in pairs for k in pair})
    count = sum(1 if left == right else 2 for left, right in pairs)

    def body(i, acc):
        acc = list(acc)
        for a in range(0, ny, 8):
            rows = pl.ds(a, 8)
            ct = ct_ref[i, rows]
            vs = {}
            for k in used:
                ref, base, scaled = fields[k]
                v = (ref[0, i + base, rows], ref[1, i + base, rows])
                vs[k] = (ct * v[0], ct * v[1]) if scaled else v
            k = 0
            for left, right in pairs:
                (lr, li), (rr, ri) = vs[left], vs[right]
                acc[k] = acc[k] + fold(lr * rr + li * ri)
                k += 1
                if right > left:
                    acc[k] = acc[k] + fold(lr * ri - li * rr)
                    k += 1
        return tuple(acc)

    acc = lax.fori_loop(0, nx, body, (jnp.zeros((8, 128), F32),) * count)
    return pack_lanes(acc, first)


def put(row, out_ref):
    for k in range(out_ref.shape[0]):
        out_ref[k] = row


def gram_entries(pick, pairs, entries):
    k = 0
    for left, right in pairs:
        if left == right:
            entries[left, right] = (pick(k), jnp.zeros((1, 1), F32))
            k += 1
        else:
            entries[left, right] = (pick(k), pick(k + 1))
            entries[right, left] = cconj(entries[left, right])
            k += 2
    return entries


def shift_from(ref):
    pick = total_of(ref)
    den = pick(2)
    safe = jnp.where(den > 0.0, den, 1.0)
    return tuple(jnp.where(den > 0.0, pick(k) / safe, FALLBACK[k]) for k in range(2))


EARLY = pairs_of((0, 1, 2))
LATE = pairs_of((3, 4))


def pack_pair(first, second, top):
    sub = lax.broadcasted_iota(jnp.int32, first.shape, 0)
    rolled = pltpu.roll(second, 4, 0)
    if top:
        return jnp.where(sub < 4, first, rolled)
    return jnp.where(sub < 4, rolled, first)


def unpack_pair(right, left):
    sub = lax.broadcasted_iota(jnp.int32, right.shape, 0)
    first = jnp.where(sub < 4, right, left)
    second = pltpu.roll(jnp.where(sub < 4, left, right), 4, 0)
    return first, second


def own_values(b_ref, cf_ref, ct_ref, mr_ref, d_ref):
    def get(i, rows):
        ct = ct_ref[i, rows]
        r = 1.0 / ct
        return (
            b_ref[0, i, rows] * r,
            b_ref[1, i, rows] * r,
            cf_ref[i, rows] * ct,
            mr_ref[i, rows],
            d_ref[i, rows],
        )

    return get


def fetch(pairs, sems):
    copies = [pltpu.make_async_copy(a, b, sems.at[k]) for k, (a, b) in enumerate(pairs)]
    for c in copies:
        c.start()
    for c in copies:
        c.wait()


def rows_kernel(b_ref, cf_ref, ct_ref, mr_ref, d_ref, top_ref, bot_ref, *scratch):
    blocks, coefs, sems = scratch
    nx, ny, _ = cf_ref.shape
    pairs = []
    for side, at in enumerate((0, ny - 8)):
        rows = pl.ds(at, 8)
        pairs.append((b_ref.at[:, :, rows], blocks.at[side]))
        for k, ref in enumerate((cf_ref, ct_ref, mr_ref, d_ref)):
            pairs.append((ref.at[:, rows], coefs.at[side, k]))
    fetch(pairs, sems)
    for side, out_ref in enumerate((top_ref, bot_ref)):
        get = own_values(blocks.at[side], *(coefs.at[side, k] for k in range(4)))
        top = side == 0

        def body(j, carry):
            a, b = get(2 * j, pl.ds(0, 8)), get(2 * j + 1, pl.ds(0, 8))
            out_ref[2 * j] = pack_pair(a[0], a[1], top)
            out_ref[2 * j + 1] = pack_pair(b[0], b[1], top)
            for f in range(3):
                out_ref[nx + f * nx // 2 + j] = pack_pair(a[2 + f], b[2 + f], top)
            return carry

        lax.fori_loop(0, nx // 2, body, 0, unroll=2)


def planes_kernel(b_ref, cf_ref, ct_ref, mr_ref, d_ref, lo_ref, hi_ref, *scratch):
    blocks, coefs, sems = scratch
    nx, ny, _ = cf_ref.shape
    pairs = []
    for side, at in enumerate((0, nx - H)):
        span = pl.ds(at, H)
        pairs.append((b_ref.at[:, span], blocks.at[side]))
        for k, ref in enumerate((cf_ref, ct_ref, mr_ref, d_ref)):
            pairs.append((ref.at[span], coefs.at[side, k]))
    fetch(pairs, sems)
    for side, out_ref in enumerate((lo_ref, hi_ref)):
        get = own_values(blocks.at[side], *(coefs.at[side, k] for k in range(4)))
        for i in range(H):
            for f, value in enumerate(get(i, pl.ds(0, ny))):
                out_ref[f, i] = value


def corners_kernel(after_ref, yl_ref, yr_ref, lo_ref, hi_ref):
    count = yl_ref.shape[0]
    nx = count * 2 // 5
    for k, ref in enumerate((yl_ref, yr_ref)):
        for out_ref, base in ((lo_ref, 0), (hi_ref, nx - H)):
            for i in range(H):
                out_ref[k, i] = ref[base + i]
            for f in range(3):
                for j in range(H // 2):
                    at = nx + f * nx // 2 + base // 2 + j
                    out_ref[k, H + f * H // 2 + j] = ref[at]


def store_fields(refs, plane, rows, v, c, mr, d):
    p_ref, n_ref, u_ref, v_ref = refs
    p, n = coefficients(c, mr, d)
    u = cmul(p, v)
    for part in range(2):
        p_ref[part, plane, rows] = p[part]
        n_ref[part, plane, rows] = n[part]
        u_ref[part, plane, rows] = u[part]
        v_ref[part, plane, rows] = v[part]


def own_kernel(
    b_any, cf_any, ct_any, mr_any, d_any,
    p_ref, n_ref, u_ref, v_ref, out_ref, b_ref, cf_ref, ct_ref,
    mr_ref, d_ref, w_ref, sems,
):
    nx, ny, nz = cf_ref.shape
    sources = (b_any, cf_any, ct_any, mr_any, d_any)
    fetch(list(zip(sources, (b_ref, cf_ref, ct_ref, mr_ref, d_ref))), sems)
    get = own_values(b_ref, cf_ref, ct_ref, mr_ref, d_ref)
    rows, rest = pl.ds(0, ny), pl.ds(ny, 8)
    zero = jnp.zeros((8, nz), F32)

    def body(i):
        vr, vi, c, mr, d = get(i, rows)
        store_fields((p_ref, n_ref, u_ref, v_ref), i + H, rows, (vr, vi), c, mr, d)
        for part in range(2):
            p_ref[part, i + H, rest] = zero
            u_ref[part, i + H, rest] = zero

    loop([(0, nx)], body)
    blank = jnp.zeros((ny + 8, nz), F32)
    for ref in (u_ref, w_ref):
        for part in range(2):
            ref[part, H - 1] = blank
            ref[part, nx + H] = blank
    half_step(u_ref, p_ref, w_ref, [(H, nx + H)])

    def dots(i, acc):
        acc = list(acc)
        y = image(w_ref, n_ref, i + H)
        for a in range(0, ny, 8):
            ct = ct_ref[i, pl.ds(a, 8)]
            yr, yi = y[0][a : a + 8] * ct, y[1][a : a + 8] * ct
            br, bi = b_ref[0, i, pl.ds(a, 8)], b_ref[1, i, pl.ds(a, 8)]
            acc[0] = acc[0] + fold(br * yr + bi * yi)
            acc[1] = acc[1] + fold(br * yi - bi * yr)
            acc[2] = acc[2] + fold(br * br + bi * bi)
        return tuple(acc)

    acc = lax.fori_loop(0, nx, dots, (jnp.zeros((8, 128), F32),) * 3, unroll=2)
    put(pack_lanes(acc), out_ref)


def tails(refs, left, right, ny, fields, coefs, planes):
    rows = pl.ds(ny, 8)
    v = [unpack_pair(right(k), left(k)) for k in fields]
    c = [unpack_pair(right(k), left(k)) for k in coefs]
    for k in range(2):
        store_fields(refs, planes[k], rows, v[k], c[0][k], c[1][k], c[2][k])


def sides_kernel(th_ref, xl_ref, xr_ref, yl_ref, yr_ref, *refs):
    p_ref, n_ref, u_ref, v_ref, w0_ref, w1_ref, v1_ref, v2_ref = refs[4:]
    state = (p_ref, n_ref, u_ref, v_ref)
    ny = xl_ref.shape[2]
    planes = p_ref.shape[1]
    nx = planes - 2 * H
    rows = pl.ds(0, ny)
    for ref, base in ((xl_ref, 0), (xr_ref, nx + H)):

        def side(i):
            vr, vi, c, mr, d = (ref[f, i] for f in range(5))
            store_fields(state, base + i, rows, (vr, vi), c, mr, d)

        loop([(0, H)], side)

    def pair(j):
        coefs = [nx + f * nx // 2 + j for f in range(3)]
        at = (H + 2 * j, H + 2 * j + 1)
        own = (2 * j, 2 * j + 1)
        tails(state, lambda k: yl_ref[k], lambda k: yr_ref[k], ny, own, coefs, at)

    loop([(0, nx // 2)], pair)
    th = shift_from(th_ref)
    two_applications(inside, planes, th, *state, (w0_ref, w1_ref), (v1_ref, v2_ref))


def first_kernel(th_ref, cl_ref, cr_ref, *refs):
    p_ref, n_ref, u_ref, v_ref, w0_ref, w1_ref, v1_ref, v2_ref, top_ref, bot_ref = refs[8:]
    state = (p_ref, n_ref, u_ref, v_ref)
    planes = p_ref.shape[1]
    nx, ny = planes - 2 * H, p_ref.shape[2] - 8
    for ref, base in ((cl_ref, 0), (cr_ref, nx + H)):
        for j in range(H // 2):
            coefs = [H + f * H // 2 + j for f in range(3)]
            at = (base + 2 * j, base + 2 * j + 1)
            own = (2 * j, 2 * j + 1)
            tails(state, lambda k: ref[0, k], lambda k: ref[1, k], ny, own, coefs, at)
    th = shift_from(th_ref)
    two_applications(outside, planes, th, *state, (w0_ref, w1_ref), (v1_ref, v2_ref))
    for out_ref, rows, top in ((top_ref, pl.ds(0, 8), True), (bot_ref, pl.ds(ny - 8, 8), False)):

        def pack(i):
            a, b = v2_ref[0, i + H, rows], v2_ref[1, i + H, rows]
            out_ref[i] = pack_pair(a, b, top)

        loop([(0, nx)], pack)


def early_kernel(b_ref, ct_ref, v1_ref, v2_ref, out_ref):
    fields = ((b_ref, 0, False), (v1_ref, H, True), (v2_ref, H, True))
    put(gram_rows(fields, ct_ref, EARLY), out_ref)


def rows_back_kernel(yl_ref, yr_ref, _, v_ref, lo_ref, hi_ref):
    nx, ny = yl_ref.shape[0], v_ref.shape[2] - 8
    rows = pl.ds(ny, 8)

    def tail(i):
        for part, value in enumerate(unpack_pair(yr_ref[i], yl_ref[i])):
            v_ref[part, i + H, rows] = value

    loop([(0, nx)], tail)
    for part in range(2):
        for i in range(H):
            lo_ref[part, i] = v_ref[part, H + i]
            hi_ref[part, i] = v_ref[part, nx + i]


def inner_kernel(th_ref, p_ref, n_ref, v_ref, u_ref, w2_ref, w3_ref, v3_ref, v4_ref):
    planes = p_ref.shape[1]
    th = shift_from(th_ref)

    def fill(i):
        u = cmul((p_ref[0, i], p_ref[1, i]), (v_ref[0, i], v_ref[1, i]))
        for part in range(2):
            u_ref[part, i] = u[part]

    loop([(H, planes - H)], fill)
    two_applications(
        inside, planes, th, p_ref, n_ref, u_ref, v_ref, (w2_ref, w3_ref), (v3_ref, v4_ref)
    )


def second_kernel(th_ref, e_ref, xl_ref, xr_ref, p_ref, n_ref, b_ref, ct_ref, v1_ref, *refs):
    v2_ref, u_ref, w2_ref, w3_ref, v3_ref, v4_ref, out_ref = refs[6:]
    planes = p_ref.shape[1]
    th = shift_from(th_ref)
    for ref, base in ((xl_ref, 0), (xr_ref, planes - H)):
        for i in range(H):
            v = (ref[0, i], ref[1, i])
            u = cmul((p_ref[0, base + i], p_ref[1, base + i]), v)
            for part in range(2):
                v2_ref[part, base + i] = v[part]
                u_ref[part, base + i] = u[part]
    two_applications(
        outside, planes, th, p_ref, n_ref, u_ref, v2_ref, (w2_ref, w3_ref), (v3_ref, v4_ref)
    )
    fields = (
        (b_ref, 0, False), (v1_ref, H, True), (v2_ref, H, True), (v3_ref, H, True),
        (v4_ref, H, True),
    )
    put(e_ref[0] + gram_rows(fields, ct_ref, LATE, 9), out_ref)


def recurrences(th, gram):
    def inner(x, y):
        total = None
        for i, xi in enumerate(x):
            part = None
            for j, yj in enumerate(y):
                t = cmul(gram[i, j], yj)
                part = t if part is None else cadd(part, t)
            t = cmul(cconj(xi), part)
            total = t if total is None else cadd(total, t)
        return total

    def apply(x):
        scaled = [cmul(th, c) for c in x]
        return [scaled[0]] + [cadd(x[k], scaled[k + 1]) for k in range(len(x) - 1)] + [x[-1]]

    def lincomb(x, s, y):
        out = []
        for k in range(max(len(x), len(y))):
            a = x[k] if k < len(x) else None
            b = cmul(s, y[k]) if k < len(y) else None
            out.append(b if a is None else a if b is None else cadd(a, b))
        return out

    def neg(s):
        return (-s[0], -s[1])

    one = (jnp.ones((1, 1), F32), jnp.zeros((1, 1), F32))
    residual, direction, shadow, answer = [one], [one], [one], []
    rho = inner(shadow, residual)
    for step in range(2):
        image = apply(direction)
        alpha = cdiv(rho, inner(shadow, image))
        half = lincomb(residual, neg(alpha), image)
        second = apply(half)
        prod = inner(second, half)
        norm = inner(second, second)[0] + EPSILON
        omega = (prod[0] / norm, prod[1] / norm)
        answer = lincomb(lincomb(answer, alpha, direction), omega, half)
        residual = lincomb(half, neg(omega), second)
        if step == 0:
            rho_next = inner(shadow, residual)
            beta = cmul(cdiv(rho_next, rho), cdiv(alpha, omega))
            direction = lincomb(residual, beta, lincomb(direction, neg(omega), image))
            rho = rho_next
    return answer, residual


def final_kernel(
    th_ref, g_ref, b_ref, cf_ref, ct_ref,
    w0_ref, w1_ref, w2_ref, w3_ref, v1_ref, v2_ref, v3_ref, v4_ref,
    sol_ref, res_ref,
):
    nx, ny, nz = cf_ref.shape
    th = shift_from(th_ref)
    entries = gram_entries(total_of(g_ref), EARLY + LATE, {})
    answer, residual = recurrences(th, entries)

    def spread(c):
        return tuple(jnp.broadcast_to(x, (8, nz)) for x in c)

    answer, residual = [spread(c) for c in answer], [spread(c) for c in residual]

    def body(i, carry):
        for a in range(0, ny, 8):
            rows = pl.ds(a, 8)
            acc = None
            for c, ref in zip(answer, (w0_ref, w1_ref, w2_ref, w3_ref)):
                t = cmul(c, (ref[0, i + H, rows], ref[1, i + H, rows]))
                acc = t if acc is None else cadd(acc, t)
            inv = 1.0 / cf_ref[i, rows]
            sol_ref[0, i, rows] = acc[0] * inv
            sol_ref[1, i, rows] = acc[1] * inv
            acc = None
            for c, ref in zip(residual[1:], (v1_ref, v2_ref, v3_ref, v4_ref)):
                t = cmul(c, (ref[0, i + H, rows], ref[1, i + H, rows]))
                acc = t if acc is None else cadd(acc, t)
            ct = ct_ref[i, rows]
            t = cmul(residual[0], (b_ref[0, i, rows], b_ref[1, i, rows]))
            res_ref[0, i, rows] = acc[0] * ct + t[0]
            res_ref[1, i, rows] = acc[1] * ct + t[1]
        return carry

    lax.fori_loop(0, nx, body, 0)


def call(kernel, outs, scratch, *args, alias=None):
    return pl.pallas_call(
        kernel,
        out_shape=[jax.ShapeDtypeStruct(s, F32) for s in outs],
        in_specs=vmem(len(args)),
        out_specs=vmem(len(outs)),
        scratch_shapes=[pltpu.VMEM(s, F32) for s in scratch],
        input_output_aliases=alias or {},
        compiler_params=pltpu.CompilerParams(vmem_limit_bytes=LIMIT),
    )(*args)


def edge_call(kernel, outs, scratch, *args):
    return pl.pallas_call(
        kernel,
        out_shape=[jax.ShapeDtypeStruct(s, F32) for s in outs],
        in_specs=[pl.BlockSpec(memory_space=pl.ANY)] * len(args),
        out_specs=vmem(len(outs)),
        scratch_shapes=[pltpu.VMEM(s, F32) for s in scratch] + [pltpu.SemaphoreType.DMA((10,))],
        compiler_params=pltpu.CompilerParams(vmem_limit_bytes=LIMIT),
    )(*(pltpu.with_memory_space_constraint(x, pltpu.HBM) for x in args))


def both_ways(to_lower, to_upper, axis):
    n = lax.axis_size(axis)
    up = [(i, i + 1) for i in range(n - 1)]
    down = [(i + 1, i) for i in range(n - 1)]
    return lax.ppermute(to_upper, axis, up), lax.ppermute(to_lower, axis, down)


def local(b, cf, ct, mr, d):
    nx, ny, nz = cf.shape
    peers = lax.axis_size("gx") * lax.axis_size("gy")
    planes = nx + 2 * H
    own = (2, nx, ny, nz)
    ext = (2, planes, ny + 2 * H, nz)
    face = (2, H, ny + 2 * H, nz)
    rim = (nx + 3 * nx // 2, 8, nz)
    corner = (2, H + 3 * H // 2, 8, nz)
    inputs = (b, cf, ct, mr, d)

    top, bot = edge_call(
        rows_kernel, [rim, rim], [(2, 2, nx, 8, nz), (2, 4, nx, 8, nz)], *inputs
    )
    yl, yr = both_ways(top, bot, "gy")
    lo, hi = edge_call(
        planes_kernel, [(5, H, ny, nz)] * 2, [(2, 2, H, ny, nz), (2, 4, H, ny, nz)], *inputs
    )
    xl, xr = both_ways(lo, hi, "gx")
    *state, th, b, cf, ct = edge_call(
        own_kernel, [ext] * 4 + [(peers, 1, 128), b.shape, cf.shape, ct.shape],
        [mr.shape, d.shape, ext], *inputs,
    )
    th = lax.all_to_all(th, AXES, 0, 0)
    lo, hi = call(corners_kernel, [corner] * 2, [], th, yl, yr)
    cl, cr = both_ways(lo, hi, "gx")
    state = call(
        sides_kernel, [ext] * 8, [], th, xl, xr, yl, yr, *state,
        alias={5 + k: k for k in range(4)},
    )
    p, n, _, _, w0, w1, v1, v2, top, bot = call(
        first_kernel, [ext] * 8 + [(nx, 8, nz)] * 2, [], th, cl, cr, *state,
        alias={3 + k: k for k in range(8)},
    )
    yl, yr = both_ways(top, bot, "gy")
    early = call(early_kernel, [(1, 1, 128)], [], b, ct, v1, v2)[0]
    v2, lo, hi = call(rows_back_kernel, [ext, face, face], [], yl, yr, v2, alias={2: 0})
    xl, xr = both_ways(lo, hi, "gx")
    state = call(inner_kernel, [ext] * 5, [], th, p, n, v2)
    v2, _, w2, w3, v3, v4, gram = call(
        second_kernel, [ext] * 6 + [(peers, 1, 128)], [],
        th, early, xl, xr, p, n, b, ct, v1, v2, *state,
        alias={9 + k: k for k in range(6)},
    )
    gram = lax.all_to_all(gram, AXES, 0, 0)
    return tuple(
        call(final_kernel, [own, own], [], th, gram, b, cf, ct, w0, w1, w2, w3, v1, v2, v3, v4)
    )


def solution(mesh):
    field, coef = P(None, "gx", "gy", None), P("gx", "gy", None)
    return jax.shard_map(
        local,
        mesh=mesh,
        in_specs=(field, coef, coef, coef, coef),
        out_specs=(field, field),
        check_vma=False,
    )
```

```python
import jax
import jax.numpy as jnp
from jax import lax
from jax.experimental import pallas as pl
from jax.experimental.pallas import tpu as pltpu
from jax.sharding import PartitionSpec as P

OMEGA = 0.8
EPSILON = 1e-06
H = 4
AXES = ("gx", "gy")
F32 = jnp.float32
LIMIT = 24 * 1024 * 1024
FALLBACK = (0.72, -0.28)


def vmem(n):
    return [pl.BlockSpec(memory_space=pltpu.VMEM)] * n


def cmul(a, b):
    return (a[0] * b[0] - a[1] * b[1], a[0] * b[1] + a[1] * b[0])


def cconj(a):
    return (a[0], -a[1])


def cadd(a, b):
    return (a[0] + b[0], a[1] + b[1])


def csub(a, b):
    return (a[0] - b[0], a[1] - b[1])


def cdiv(n, d):
    scale = d[0] * d[0] + d[1] * d[1]
    return (
        (n[0] * d[0] + n[1] * d[1]) / scale,
        (n[1] * d[0] - n[0] * d[1]) / scale,
    )


def smooth_yz(plane):
    rows, lanes = plane.shape
    y = plane + plane + pltpu.roll(plane, 1, 0) + pltpu.roll(plane, rows - 1, 0)
    lane = lax.broadcasted_iota(jnp.int32, plane.shape, 1)
    up = jnp.where(lane == 0, 0.0, pltpu.roll(y, 1, 1))
    down = jnp.where(lane == lanes - 1, 0.0, pltpu.roll(y, lanes - 1, 1))
    return y + y + up + down


def weighted(ref, i):
    out = []
    for part in range(2):
        mid = ref[part, i]
        total = smooth_yz(ref[part, i - 1] + mid + mid + ref[part, i + 1])
        out.append((total - 8.0 * mid) * (1.0 / 160.0))
    return tuple(out)


def coefficients(c, mr, d):
    shift = d + 0.5 * mr
    mod = mr * mr + shift * shift
    den = mod * c
    inv = 1.0 / jnp.where(den == 0.0, 1.0, den)
    k = OMEGA * c * c * inv
    rc = mod * inv
    return (k * mr, -(k * shift)), (rc * mr, rc * d)


def loop(ranges, body):
    for lo, hi in ranges:

        def step(i, carry):
            body(i)
            return carry

        lax.fori_loop(lo, hi, step, 0, unroll=4)


def half_step(u_ref, p_ref, w_ref, ranges):
    def body(i):
        pw = cmul((p_ref[0, i], p_ref[1, i]), weighted(u_ref, i))
        w_ref[0, i] = 1.2 * u_ref[0, i] + pw[0]
        w_ref[1, i] = 1.2 * u_ref[1, i] + pw[1]

    loop(ranges, body)


def image(w_ref, n_ref, i):
    nw = cmul((n_ref[0, i], n_ref[1, i]), (w_ref[0, i], w_ref[1, i]))
    return csub(nw, weighted(w_ref, i))


def advance(w_ref, n_ref, v_ref, th, next_ref, ranges, p_ref=None, u_ref=None):
    def body(i):
        y = csub(image(w_ref, n_ref, i), cmul(th, (v_ref[0, i], v_ref[1, i])))
        for part in range(2):
            next_ref[part, i] = y[part]
        if p_ref is not None:
            u = cmul((p_ref[0, i], p_ref[1, i]), y)
            for part in range(2):
                u_ref[part, i] = u[part]

    loop(ranges, body)


def inside(planes, k):
    return [(H + k, planes - H - k)]


def outside(planes, k):
    return [(k, H + k), (planes - H - k, planes - k)]


def two_applications(part_of, planes, th, p_ref, n_ref, u_ref, v_ref, w_refs, next_refs):
    half_step(u_ref, p_ref, w_refs[0], part_of(planes, 1))
    advance(w_refs[0], n_ref, v_ref, th, next_refs[0], part_of(planes, 2), p_ref, u_ref)
    half_step(u_ref, p_ref, w_refs[1], part_of(planes, 3))
    advance(w_refs[1], n_ref, next_refs[0], th, next_refs[1], part_of(planes, 4))


def total_of(ref):
    rows = ref[...].reshape(ref.shape[0], ref.shape[-1])
    tot = jnp.sum(rows, axis=0, keepdims=True)
    lane = lax.broadcasted_iota(jnp.int32, tot.shape, 1)
    return lambda k: jnp.sum(jnp.where(lane == k, tot, 0.0), axis=1, keepdims=True)


def pack_lanes(values, first=0):
    lane = lax.broadcasted_iota(jnp.int32, (1, 128), 1)
    row = jnp.zeros((1, 128), F32)
    for k, v in enumerate(values, first):
        s = jnp.sum(jnp.sum(v, axis=0, keepdims=True), axis=1, keepdims=True)
        row = jnp.where(lane == k, s, row)
    return row


def fold(x):
    out = x[:, :128]
    for b in range(128, x.shape[1], 128):
        out = out + x[:, b : b + 128]
    return out


def pairs_of(rights):
    return [(left, right) for right in rights for left in range(right + 1)]


def gram_rows(fields, ct_ref, pairs, first=0):
    nx, ny, _ = ct_ref.shape
    used = sorted({k for pair in pairs for k in pair})
    count = sum(1 if left == right else 2 for left, right in pairs)

    def body(i, acc):
        acc = list(acc)
        for a in range(0, ny, 8):
            rows = pl.ds(a, 8)
            ct = ct_ref[i, rows]
            vs = {}
            for k in used:
                ref, base, scaled = fields[k]
                v = (ref[0, i + base, rows], ref[1, i + base, rows])
                vs[k] = (ct * v[0], ct * v[1]) if scaled else v
            k = 0
            for left, right in pairs:
                (lr, li), (rr, ri) = vs[left], vs[right]
                acc[k] = acc[k] + fold(lr * rr + li * ri)
                k += 1
                if right > left:
                    acc[k] = acc[k] + fold(lr * ri - li * rr)
                    k += 1
        return tuple(acc)

    acc = lax.fori_loop(0, nx, body, (jnp.zeros((8, 128), F32),) * count)
    return pack_lanes(acc, first)


def put(row, out_ref):
    for k in range(out_ref.shape[0]):
        out_ref[k] = row


def gram_entries(pick, pairs, entries):
    k = 0
    for left, right in pairs:
        if left == right:
            entries[left, right] = (pick(k), jnp.zeros((1, 1), F32))
            k += 1
        else:
            entries[left, right] = (pick(k), pick(k + 1))
            entries[right, left] = cconj(entries[left, right])
            k += 2
    return entries


def shift_from(ref):
    pick = total_of(ref)
    den = pick(2)
    safe = jnp.where(den > 0.0, den, 1.0)
    return tuple(jnp.where(den > 0.0, pick(k) / safe, FALLBACK[k]) for k in range(2))


EARLY = pairs_of((0, 1, 2))
LATE = pairs_of((3, 4))


def pack_pair(first, second, top):
    sub = lax.broadcasted_iota(jnp.int32, first.shape, 0)
    rolled = pltpu.roll(second, 4, 0)
    if top:
        return jnp.where(sub < 4, first, rolled)
    return jnp.where(sub < 4, rolled, first)


def unpack_pair(right, left):
    sub = lax.broadcasted_iota(jnp.int32, right.shape, 0)
    first = jnp.where(sub < 4, right, left)
    second = pltpu.roll(jnp.where(sub < 4, left, right), 4, 0)
    return first, second


def own_values(b_ref, cf_ref, ct_ref, mr_ref, d_ref):
    def get(i, rows):
        ct = ct_ref[i, rows]
        r = 1.0 / ct
        return (
            b_ref[0, i, rows] * r,
            b_ref[1, i, rows] * r,
            cf_ref[i, rows] * ct,
            mr_ref[i, rows],
            d_ref[i, rows],
        )

    return get


def fetch(pairs, sems):
    copies = [pltpu.make_async_copy(a, b, sems.at[k]) for k, (a, b) in enumerate(pairs)]
    for c in copies:
        c.start()
    for c in copies:
        c.wait()


def edges_kernel(
    b_ref, cf_ref, ct_ref, mr_ref, d_ref, lo_ref, hi_ref, top_ref, bot_ref,
    blocks, coefs, row_blocks, row_coefs, sems,
):
    nx, ny, _ = cf_ref.shape
    pairs = []
    for side, at in enumerate((0, ny - 8)):
        rows = pl.ds(at, 8)
        pairs.append((b_ref.at[:, :, rows], row_blocks.at[side]))
        for k, ref in enumerate((cf_ref, ct_ref, mr_ref, d_ref)):
            pairs.append((ref.at[:, rows], row_coefs.at[side, k]))
    for side, at in enumerate((0, nx - H)):
        span = pl.ds(at, H)
        pairs.append((b_ref.at[:, span], blocks.at[side]))
        for k, ref in enumerate((cf_ref, ct_ref, mr_ref, d_ref)):
            pairs.append((ref.at[span], coefs.at[side, k]))
    fetch(pairs, sems)
    for side, out_ref in enumerate((lo_ref, hi_ref)):
        get = own_values(blocks.at[side], *(coefs.at[side, k] for k in range(4)))
        for i in range(H):
            for f, value in enumerate(get(i, pl.ds(0, ny))):
                out_ref[f, i] = value
    for side, out_ref in enumerate((top_ref, bot_ref)):
        get = own_values(row_blocks.at[side], *(row_coefs.at[side, k] for k in range(4)))
        top = side == 0

        def body(j, carry):
            a, b = get(2 * j, pl.ds(0, 8)), get(2 * j + 1, pl.ds(0, 8))
            out_ref[2 * j] = pack_pair(a[0], a[1], top)
            out_ref[2 * j + 1] = pack_pair(b[0], b[1], top)
            for f in range(3):
                out_ref[nx + f * nx // 2 + j] = pack_pair(a[2 + f], b[2 + f], top)
            return carry

        lax.fori_loop(0, nx // 2, body, 0, unroll=2)


def corners_kernel(after_ref, yl_ref, yr_ref, lo_ref, hi_ref):
    count = yl_ref.shape[0]
    nx = count * 2 // 5
    for k, ref in enumerate((yl_ref, yr_ref)):
        for out_ref, base in ((lo_ref, 0), (hi_ref, nx - H)):
            for i in range(H):
                out_ref[k, i] = ref[base + i]
            for f in range(3):
                for j in range(H // 2):
                    at = nx + f * nx // 2 + base // 2 + j
                    out_ref[k, H + f * H // 2 + j] = ref[at]


def store_fields(refs, plane, rows, v, c, mr, d):
    p_ref, n_ref, u_ref, v_ref = refs
    p, n = coefficients(c, mr, d)
    u = cmul(p, v)
    for part in range(2):
        p_ref[part, plane, rows] = p[part]
        n_ref[part, plane, rows] = n[part]
        u_ref[part, plane, rows] = u[part]
        v_ref[part, plane, rows] = v[part]


def own_kernel(
    b_any, cf_any, ct_any, mr_any, d_any,
    p_ref, n_ref, u_ref, v_ref, out_ref, b_ref, cf_ref, ct_ref,
    mr_ref, d_ref, w_ref, sems,
):
    nx, ny, nz = cf_ref.shape
    sources = (b_any, cf_any, ct_any, mr_any, d_any)
    fetch(list(zip(sources, (b_ref, cf_ref, ct_ref, mr_ref, d_ref))), sems)
    get = own_values(b_ref, cf_ref, ct_ref, mr_ref, d_ref)
    rows, rest = pl.ds(0, ny), pl.ds(ny, 8)
    zero = jnp.zeros((8, nz), F32)

    def body(i):
        vr, vi, c, mr, d = get(i, rows)
        store_fields((p_ref, n_ref, u_ref, v_ref), i + H, rows, (vr, vi), c, mr, d)
        for part in range(2):
            p_ref[part, i + H, rest] = zero
            u_ref[part, i + H, rest] = zero

    loop([(0, nx)], body)
    blank = jnp.zeros((ny + 8, nz), F32)
    for part in range(2):
        u_ref[part, H - 1] = blank
        w_ref[part, H - 1] = blank
        w_ref[part, nx // 2 + H] = blank
    half_step(u_ref, p_ref, w_ref, [(H, nx // 2 + H)])

    def dots(i, acc):
        acc = list(acc)
        y = image(w_ref, n_ref, i + H)
        for a in range(0, ny, 8):
            ct = ct_ref[i, pl.ds(a, 8)]
            yr, yi = y[0][a : a + 8] * ct, y[1][a : a + 8] * ct
            br, bi = b_ref[0, i, pl.ds(a, 8)], b_ref[1, i, pl.ds(a, 8)]
            acc[0] = acc[0] + fold(br * yr + bi * yi)
            acc[1] = acc[1] + fold(br * yi - bi * yr)
            acc[2] = acc[2] + fold(br * br + bi * bi)
        return tuple(acc)

    acc = lax.fori_loop(0, nx // 2, dots, (jnp.zeros((8, 128), F32),) * 3, unroll=2)
    put(pack_lanes(acc), out_ref)


def tails(refs, left, right, ny, fields, coefs, planes):
    rows = pl.ds(ny, 8)
    v = [unpack_pair(right(k), left(k)) for k in fields]
    c = [unpack_pair(right(k), left(k)) for k in coefs]
    for k in range(2):
        store_fields(refs, planes[k], rows, v[k], c[0][k], c[1][k], c[2][k])


def sides_kernel(th_ref, xl_ref, xr_ref, yl_ref, yr_ref, *refs):
    p_ref, n_ref, u_ref, v_ref, w0_ref, w1_ref, v1_ref, v2_ref = refs[4:]
    state = (p_ref, n_ref, u_ref, v_ref)
    ny = xl_ref.shape[2]
    planes = p_ref.shape[1]
    nx = planes - 2 * H
    rows = pl.ds(0, ny)
    for ref, base in ((xl_ref, 0), (xr_ref, nx + H)):

        def side(i):
            vr, vi, c, mr, d = (ref[f, i] for f in range(5))
            store_fields(state, base + i, rows, (vr, vi), c, mr, d)

        loop([(0, H)], side)

    def pair(j):
        coefs = [nx + f * nx // 2 + j for f in range(3)]
        at = (H + 2 * j, H + 2 * j + 1)
        own = (2 * j, 2 * j + 1)
        tails(state, lambda k: yl_ref[k], lambda k: yr_ref[k], ny, own, coefs, at)

    loop([(0, nx // 2)], pair)
    th = shift_from(th_ref)
    two_applications(inside, planes, th, *state, (w0_ref, w1_ref), (v1_ref, v2_ref))


def first_kernel(th_ref, cl_ref, cr_ref, *refs):
    p_ref, n_ref, u_ref, v_ref, w0_ref, w1_ref, v1_ref, v2_ref, top_ref, bot_ref = refs[8:]
    state = (p_ref, n_ref, u_ref, v_ref)
    planes = p_ref.shape[1]
    nx, ny = planes - 2 * H, p_ref.shape[2] - 8
    for ref, base in ((cl_ref, 0), (cr_ref, nx + H)):
        for j in range(H // 2):
            coefs = [H + f * H // 2 + j for f in range(3)]
            at = (base + 2 * j, base + 2 * j + 1)
            own = (2 * j, 2 * j + 1)
            tails(state, lambda k: ref[0, k], lambda k: ref[1, k], ny, own, coefs, at)
    th = shift_from(th_ref)
    two_applications(outside, planes, th, *state, (w0_ref, w1_ref), (v1_ref, v2_ref))
    for out_ref, rows, top in ((top_ref, pl.ds(0, 8), True), (bot_ref, pl.ds(ny - 8, 8), False)):

        def pack(i):
            a, b = v2_ref[0, i + H, rows], v2_ref[1, i + H, rows]
            out_ref[i] = pack_pair(a, b, top)

        loop([(0, nx)], pack)


def early_kernel(b_ref, ct_ref, v1_ref, v2_ref, out_ref):
    fields = ((b_ref, 0, False), (v1_ref, H, True), (v2_ref, H, True))
    put(gram_rows(fields, ct_ref, EARLY), out_ref)


def rows_back_kernel(yl_ref, yr_ref, _, v_ref, lo_ref, hi_ref):
    nx, ny = yl_ref.shape[0], v_ref.shape[2] - 8
    rows = pl.ds(ny, 8)

    def tail(i):
        for part, value in enumerate(unpack_pair(yr_ref[i], yl_ref[i])):
            v_ref[part, i + H, rows] = value

    loop([(0, nx)], tail)
    for part in range(2):
        for i in range(H):
            lo_ref[part, i] = v_ref[part, H + i]
            hi_ref[part, i] = v_ref[part, nx + i]


def inner_kernel(th_ref, p_ref, n_ref, v_ref, u_ref, w2_ref, w3_ref, v3_ref, v4_ref):
    planes = p_ref.shape[1]
    th = shift_from(th_ref)

    def fill(i):
        u = cmul((p_ref[0, i], p_ref[1, i]), (v_ref[0, i], v_ref[1, i]))
        for part in range(2):
            u_ref[part, i] = u[part]

    loop([(H, planes - H)], fill)
    two_applications(
        inside, planes, th, p_ref, n_ref, u_ref, v_ref, (w2_ref, w3_ref), (v3_ref, v4_ref)
    )


def second_kernel(th_ref, e_ref, xl_ref, xr_ref, p_ref, n_ref, b_ref, ct_ref, v1_ref, *refs):
    v2_ref, u_ref, w2_ref, w3_ref, v3_ref, v4_ref, out_ref = refs[6:]
    planes = p_ref.shape[1]
    th = shift_from(th_ref)
    for ref, base in ((xl_ref, 0), (xr_ref, planes - H)):
        for i in range(H):
            v = (ref[0, i], ref[1, i])
            u = cmul((p_ref[0, base + i], p_ref[1, base + i]), v)
            for part in range(2):
                v2_ref[part, base + i] = v[part]
                u_ref[part, base + i] = u[part]
    two_applications(
        outside, planes, th, p_ref, n_ref, u_ref, v2_ref, (w2_ref, w3_ref), (v3_ref, v4_ref)
    )
    fields = (
        (b_ref, 0, False), (v1_ref, H, True), (v2_ref, H, True), (v3_ref, H, True),
        (v4_ref, H, True),
    )
    put(e_ref[0] + gram_rows(fields, ct_ref, LATE, 9), out_ref)


def recurrences(th, gram):
    def inner(x, y):
        total = None
        for i, xi in enumerate(x):
            part = None
            for j, yj in enumerate(y):
                t = cmul(gram[i, j], yj)
                part = t if part is None else cadd(part, t)
            t = cmul(cconj(xi), part)
            total = t if total is None else cadd(total, t)
        return total

    def apply(x):
        scaled = [cmul(th, c) for c in x]
        return [scaled[0]] + [cadd(x[k], scaled[k + 1]) for k in range(len(x) - 1)] + [x[-1]]

    def lincomb(x, s, y):
        out = []
        for k in range(max(len(x), len(y))):
            a = x[k] if k < len(x) else None
            b = cmul(s, y[k]) if k < len(y) else None
            out.append(b if a is None else a if b is None else cadd(a, b))
        return out

    def neg(s):
        return (-s[0], -s[1])

    one = (jnp.ones((1, 1), F32), jnp.zeros((1, 1), F32))
    residual, direction, shadow, answer = [one], [one], [one], []
    rho = inner(shadow, residual)
    for step in range(2):
        image = apply(direction)
        alpha = cdiv(rho, inner(shadow, image))
        half = lincomb(residual, neg(alpha), image)
        second = apply(half)
        prod = inner(second, half)
        norm = inner(second, second)[0] + EPSILON
        omega = (prod[0] / norm, prod[1] / norm)
        answer = lincomb(lincomb(answer, alpha, direction), omega, half)
        residual = lincomb(half, neg(omega), second)
        if step == 0:
            rho_next = inner(shadow, residual)
            beta = cmul(cdiv(rho_next, rho), cdiv(alpha, omega))
            direction = lincomb(residual, beta, lincomb(direction, neg(omega), image))
            rho = rho_next
    return answer, residual


def final_kernel(
    th_ref, g_ref, b_ref, cf_ref, ct_ref,
    w0_ref, w1_ref, w2_ref, w3_ref, v1_ref, v2_ref, v3_ref, v4_ref,
    sol_ref, res_ref,
):
    nx, ny, nz = cf_ref.shape
    th = shift_from(th_ref)
    entries = gram_entries(total_of(g_ref), EARLY + LATE, {})
    answer, residual = recurrences(th, entries)

    def spread(c):
        return tuple(jnp.broadcast_to(x, (8, nz)) for x in c)

    answer, residual = [spread(c) for c in answer], [spread(c) for c in residual]

    def body(i, carry):
        for a in range(0, ny, 8):
            rows = pl.ds(a, 8)
            acc = None
            for c, ref in zip(answer, (w0_ref, w1_ref, w2_ref, w3_ref)):
                t = cmul(c, (ref[0, i + H, rows], ref[1, i + H, rows]))
                acc = t if acc is None else cadd(acc, t)
            inv = 1.0 / cf_ref[i, rows]
            sol_ref[0, i, rows] = acc[0] * inv
            sol_ref[1, i, rows] = acc[1] * inv
            acc = None
            for c, ref in zip(residual[1:], (v1_ref, v2_ref, v3_ref, v4_ref)):
                t = cmul(c, (ref[0, i + H, rows], ref[1, i + H, rows]))
                acc = t if acc is None else cadd(acc, t)
            ct = ct_ref[i, rows]
            t = cmul(residual[0], (b_ref[0, i, rows], b_ref[1, i, rows]))
            res_ref[0, i, rows] = acc[0] * ct + t[0]
            res_ref[1, i, rows] = acc[1] * ct + t[1]
        return carry

    lax.fori_loop(0, nx, body, 0)


def call(kernel, outs, scratch, *args, alias=None):
    return pl.pallas_call(
        kernel,
        out_shape=[jax.ShapeDtypeStruct(s, F32) for s in outs],
        in_specs=vmem(len(args)),
        out_specs=vmem(len(outs)),
        scratch_shapes=[pltpu.VMEM(s, F32) for s in scratch],
        input_output_aliases=alias or {},
        compiler_params=pltpu.CompilerParams(vmem_limit_bytes=LIMIT),
    )(*args)


def edge_call(kernel, outs, scratch, *args):
    return pl.pallas_call(
        kernel,
        out_shape=[jax.ShapeDtypeStruct(s, F32) for s in outs],
        in_specs=[pl.BlockSpec(memory_space=pl.ANY)] * len(args),
        out_specs=vmem(len(outs)),
        scratch_shapes=[pltpu.VMEM(s, F32) for s in scratch] + [pltpu.SemaphoreType.DMA((20,))],
        compiler_params=pltpu.CompilerParams(vmem_limit_bytes=LIMIT),
    )(*(pltpu.with_memory_space_constraint(x, pltpu.HBM) for x in args))


def both_ways(to_lower, to_upper, axis):
    n = lax.axis_size(axis)
    up = [(i, i + 1) for i in range(n - 1)]
    down = [(i + 1, i) for i in range(n - 1)]
    return lax.ppermute(to_upper, axis, up), lax.ppermute(to_lower, axis, down)


def local(b, cf, ct, mr, d):
    nx, ny, nz = cf.shape
    peers = lax.axis_size("gx") * lax.axis_size("gy")
    planes = nx + 2 * H
    own = (2, nx, ny, nz)
    ext = (2, planes, ny + 2 * H, nz)
    face = (2, H, ny + 2 * H, nz)
    rim = (nx + 3 * nx // 2, 8, nz)
    corner = (2, H + 3 * H // 2, 8, nz)
    inputs = (b, cf, ct, mr, d)

    lo, hi, top, bot = edge_call(
        edges_kernel, [(5, H, ny, nz)] * 2 + [rim, rim],
        [(2, 2, H, ny, nz), (2, 4, H, ny, nz), (2, 2, nx, 8, nz), (2, 4, nx, 8, nz)], *inputs
    )
    yl, yr = both_ways(top, bot, "gy")
    xl, xr = both_ways(lo, hi, "gx")
    *state, th, b, cf, ct = edge_call(
        own_kernel, [ext] * 4 + [(peers, 1, 128), b.shape, cf.shape, ct.shape],
        [mr.shape, d.shape, ext], *inputs,
    )
    th = lax.all_to_all(th, AXES, 0, 0)
    lo, hi = call(corners_kernel, [corner] * 2, [], th, yl, yr)
    cl, cr = both_ways(lo, hi, "gx")
    state = call(
        sides_kernel, [ext] * 8, [], th, xl, xr, yl, yr, *state,
        alias={5 + k: k for k in range(4)},
    )
    p, n, _, _, w0, w1, v1, v2, top, bot = call(
        first_kernel, [ext] * 8 + [(nx, 8, nz)] * 2, [], th, cl, cr, *state,
        alias={3 + k: k for k in range(8)},
    )
    yl, yr = both_ways(top, bot, "gy")
    early = call(early_kernel, [(1, 1, 128)], [], b, ct, v1, v2)[0]
    v2, lo, hi = call(rows_back_kernel, [ext, face, face], [], yl, yr, v2, alias={2: 0})
    xl, xr = both_ways(lo, hi, "gx")
    state = call(inner_kernel, [ext] * 5, [], th, p, n, v2)
    v2, _, w2, w3, v3, v4, gram = call(
        second_kernel, [ext] * 6 + [(peers, 1, 128)], [],
        th, early, xl, xr, p, n, b, ct, v1, v2, *state,
        alias={9 + k: k for k in range(6)},
    )
    gram = lax.all_to_all(gram, AXES, 0, 0)
    return tuple(
        call(final_kernel, [own, own], [], th, gram, b, cf, ct, w0, w1, w2, w3, v1, v2, v3, v4)
    )


def solution(mesh):
    field, coef = P(None, "gx", "gy", None), P("gx", "gy", None)
    return jax.shard_map(
        local,
        mesh=mesh,
        in_specs=(field, coef, coef, coef, coef),
        out_specs=(field, field),
        check_vma=False,
    )
```

```python
import jax
import jax.numpy as jnp
from jax import lax
from jax.experimental import pallas as pl
from jax.experimental.pallas import tpu as pltpu
from jax.sharding import PartitionSpec as P

OMEGA = 0.8
EPSILON = 1e-06
H = 4
AXES = ("gx", "gy")
F32 = jnp.float32
LIMIT = 24 * 1024 * 1024
SCALE = 160.0
CHUNKS = 4
FALLBACK = (0.72, -0.28)


def vmem(n):
    return [pl.BlockSpec(memory_space=pltpu.VMEM)] * n


def cmul(a, b):
    return (a[0] * b[0] - a[1] * b[1], a[0] * b[1] + a[1] * b[0])


def cconj(a):
    return (a[0], -a[1])


def cadd(a, b):
    return (a[0] + b[0], a[1] + b[1])


def csub(a, b):
    return (a[0] - b[0], a[1] - b[1])


def cdiv(n, d):
    scale = d[0] * d[0] + d[1] * d[1]
    return (
        (n[0] * d[0] + n[1] * d[1]) / scale,
        (n[1] * d[0] - n[0] * d[1]) / scale,
    )


def smooth_yz(plane):
    rows, lanes = plane.shape
    lane = lax.broadcasted_iota(jnp.int32, (rows, 128), 1)
    parts = [plane[:, k : k + 128] for k in range(0, lanes, 128)]
    parts = [x + pltpu.roll(x, rows - 1, 0) for x in parts]
    parts = [x + pltpu.roll(x, 1, 0) for x in parts]
    ups = [pltpu.roll(x, 1, 1) for x in parts]
    downs = [pltpu.roll(x, 127, 1) for x in parts]
    out = []
    for k, x in enumerate(parts):
        up = jnp.where(lane == 0, ups[k - 1] if k else 0.0, ups[k])
        down = jnp.where(lane == 127, downs[k + 1] if k + 1 < len(parts) else 0.0, downs[k])
        out.append(x + x + up + down)
    return jnp.concatenate(out, axis=1)


def sums(ref, i):
    out = []
    for part in range(2):
        mid = ref[part, i]
        out.append(smooth_yz((ref[part, i - 1] + mid) + (mid + ref[part, i + 1])))
    return tuple(out)


def coefficients(c, mr, d):
    shift = d + 0.5 * mr
    mod = mr * mr + shift * shift
    den = mod * c
    inv = 1.0 / jnp.where(den == 0.0, 1.0, den)
    k = (OMEGA / SCALE) * c * c * inv
    rc = SCALE * mod * inv
    return (k * mr, -(k * shift)), (rc * mr + 8.0, rc * d)


def loop(ranges, body):
    for lo, hi in ranges:

        def step(i, carry):
            body(i)
            return carry

        lax.fori_loop(lo, hi, step, 0, unroll=4)


def half_step(u_ref, p_ref, w_ref, ranges):
    def body(i):
        u = (u_ref[0, i], u_ref[1, i])
        s = sums(u_ref, i)
        pw = cmul((p_ref[0, i], p_ref[1, i]), (s[0] - 8.0 * u[0], s[1] - 8.0 * u[1]))
        w_ref[0, i] = 1.2 * u[0] + pw[0]
        w_ref[1, i] = 1.2 * u[1] + pw[1]

    loop(ranges, body)


def image(w_ref, n_ref, i):
    nw = cmul((n_ref[0, i], n_ref[1, i]), (w_ref[0, i], w_ref[1, i]))
    return csub(nw, sums(w_ref, i))


def advance(w_ref, n_ref, v_ref, th, next_ref, ranges, p_ref=None, u_ref=None):
    def body(i):
        y = csub(image(w_ref, n_ref, i), cmul(th, (v_ref[0, i], v_ref[1, i])))
        for part in range(2):
            next_ref[part, i] = y[part]
        if p_ref is not None:
            u = cmul((p_ref[0, i], p_ref[1, i]), y)
            for part in range(2):
                u_ref[part, i] = u[part]

    loop(ranges, body)


def inside(planes, k):
    return [(H + k, planes - H - k)]


def outside(planes, k):
    return [(k, H + k), (planes - H - k, planes - k)]


def two_applications(part_of, planes, th, p_ref, n_ref, u_ref, v_ref, w_refs, next_refs):
    half_step(u_ref, p_ref, w_refs[0], part_of(planes, 1))
    advance(w_refs[0], n_ref, v_ref, th, next_refs[0], part_of(planes, 2), p_ref, u_ref)
    half_step(u_ref, p_ref, w_refs[1], part_of(planes, 3))
    advance(w_refs[1], n_ref, next_refs[0], th, next_refs[1], part_of(planes, 4))


def total_of(ref):
    rows = ref[...].reshape(ref.shape[0], ref.shape[-1])
    tot = jnp.sum(rows, axis=0, keepdims=True)
    lane = lax.broadcasted_iota(jnp.int32, tot.shape, 1)
    return lambda k: jnp.sum(jnp.where(lane == k, tot, 0.0), axis=1, keepdims=True)


def pack_lanes(values, first=0):
    lane = lax.broadcasted_iota(jnp.int32, (1, 128), 1)
    row = jnp.zeros((1, 128), F32)
    for k, v in enumerate(values, first):
        s = jnp.sum(jnp.sum(v, axis=0, keepdims=True), axis=1, keepdims=True)
        row = jnp.where(lane == k, s, row)
    return row


def fold(x):
    out = x[:, :128]
    for b in range(128, x.shape[1], 128):
        out = out + x[:, b : b + 128]
    return out


def pairs_of(rights):
    return [(left, right) for right in rights for left in range(right + 1)]


def gram_rows(fields, ct_ref, pairs, first=0):
    nx, ny, _ = ct_ref.shape
    used = sorted({k for pair in pairs for k in pair})
    count = sum(1 if left == right else 2 for left, right in pairs)

    def body(i, acc):
        acc = list(acc)
        for a in range(0, ny, 8):
            rows = pl.ds(a, 8)
            ct = ct_ref[i, rows]
            vs = {}
            for k in used:
                ref, base, scaled = fields[k]
                v = (ref[0, i + base, rows], ref[1, i + base, rows])
                vs[k] = (ct * v[0], ct * v[1]) if scaled else v
            k = 0
            for left, right in pairs:
                (lr, li), (rr, ri) = vs[left], vs[right]
                acc[k] = acc[k] + fold(lr * rr + li * ri)
                k += 1
                if right > left:
                    acc[k] = acc[k] + fold(lr * ri - li * rr)
                    k += 1
        return tuple(acc)

    acc = lax.fori_loop(0, nx, body, (jnp.zeros((8, 128), F32),) * count)
    return pack_lanes(acc, first)


def put(row, out_ref):
    for k in range(out_ref.shape[0]):
        out_ref[k] = row


def gram_entries(pick, pairs, entries):
    k = 0
    for left, right in pairs:
        if left == right:
            entries[left, right] = (pick(k), jnp.zeros((1, 1), F32))
            k += 1
        else:
            entries[left, right] = (pick(k), pick(k + 1))
            entries[right, left] = cconj(entries[left, right])
            k += 2
    return entries


def shift_from(ref):
    pick = total_of(ref)
    den = pick(2)
    safe = jnp.where(den > 0.0, den, 1.0)
    return tuple(jnp.where(den > 0.0, pick(k) / safe, FALLBACK[k]) for k in range(2))


EARLY = pairs_of((0, 1, 2))
LATE = pairs_of((3, 4))


def pack_pair(first, second, top):
    sub = lax.broadcasted_iota(jnp.int32, first.shape, 0)
    rolled = pltpu.roll(second, 4, 0)
    if top:
        return jnp.where(sub < 4, first, rolled)
    return jnp.where(sub < 4, rolled, first)


def unpack_pair(right, left):
    sub = lax.broadcasted_iota(jnp.int32, right.shape, 0)
    first = jnp.where(sub < 4, right, left)
    second = pltpu.roll(jnp.where(sub < 4, left, right), 4, 0)
    return first, second


def own_values(b_ref, cf_ref, ct_ref, mr_ref, d_ref):
    def get(i, rows):
        ct = ct_ref[i, rows]
        r = 1.0 / ct
        return (
            b_ref[0, i, rows] * r,
            b_ref[1, i, rows] * r,
            cf_ref[i, rows] * ct,
            mr_ref[i, rows],
            d_ref[i, rows],
        )

    return get


def fetch(pairs, sems):
    copies = [pltpu.make_async_copy(a, b, sems.at[k]) for k, (a, b) in enumerate(pairs)]
    for c in copies:
        c.start()
    return copies


def wait_for(copies):
    for c in copies:
        c.wait()


def edges_kernel(
    b_ref, cf_ref, ct_ref, mr_ref, d_ref, lo_ref, hi_ref, top_ref, bot_ref,
    blocks, coefs, row_blocks, row_coefs, sems,
):
    nx, ny, _ = cf_ref.shape
    pairs = []
    for side, at in enumerate((0, nx - H)):
        span = pl.ds(at, H)
        pairs.append((b_ref.at[:, span], blocks.at[side]))
        for k, ref in enumerate((cf_ref, ct_ref, mr_ref, d_ref)):
            pairs.append((ref.at[span], coefs.at[side, k]))
    for side, at in enumerate((0, ny - 8)):
        rows = pl.ds(at, 8)
        pairs.append((b_ref.at[:, :, rows], row_blocks.at[side]))
        for k, ref in enumerate((cf_ref, ct_ref, mr_ref, d_ref)):
            pairs.append((ref.at[:, rows], row_coefs.at[side, k]))
    copies = fetch(pairs, sems)
    wait_for(copies[:10])
    for side, out_ref in enumerate((lo_ref, hi_ref)):
        get = own_values(blocks.at[side], *(coefs.at[side, k] for k in range(4)))
        for i in range(H):
            for f, value in enumerate(get(i, pl.ds(0, ny))):
                out_ref[f, i] = value
    wait_for(copies[10:])
    for side, out_ref in enumerate((top_ref, bot_ref)):
        get = own_values(row_blocks.at[side], *(row_coefs.at[side, k] for k in range(4)))
        top = side == 0

        def body(j, carry):
            a, b = get(2 * j, pl.ds(0, 8)), get(2 * j + 1, pl.ds(0, 8))
            out_ref[2 * j] = pack_pair(a[0], a[1], top)
            out_ref[2 * j + 1] = pack_pair(b[0], b[1], top)
            for f in range(3):
                out_ref[nx + f * nx // 2 + j] = pack_pair(a[2 + f], b[2 + f], top)
            return carry

        lax.fori_loop(0, nx // 2, body, 0, unroll=2)


def corners_kernel(after_ref, yl_ref, yr_ref, lo_ref, hi_ref):
    count = yl_ref.shape[0]
    nx = count * 2 // 5
    for k, ref in enumerate((yl_ref, yr_ref)):
        for out_ref, base in ((lo_ref, 0), (hi_ref, nx - H)):
            for i in range(H):
                out_ref[k, i] = ref[base + i]
            for f in range(3):
                for j in range(H // 2):
                    at = nx + f * nx // 2 + base // 2 + j
                    out_ref[k, H + f * H // 2 + j] = ref[at]


def store_fields(refs, plane, rows, v, c, mr, d):
    p_ref, n_ref, u_ref, v_ref = refs
    p, n = coefficients(c, mr, d)
    u = cmul(p, v)
    for part in range(2):
        p_ref[part, plane, rows] = p[part]
        n_ref[part, plane, rows] = n[part]
        u_ref[part, plane, rows] = u[part]
        v_ref[part, plane, rows] = v[part]


def own_kernel(
    b_any, cf_any, ct_any, mr_any, d_any,
    p_ref, n_ref, u_ref, v_ref, out_ref, b_ref, cf_ref, ct_ref,
    mr_ref, d_ref, w_ref, sems,
):
    nx, ny, nz = cf_ref.shape
    sources = (b_any, cf_any, ct_any, mr_any, d_any)
    wait_for(fetch(list(zip(sources, (b_ref, cf_ref, ct_ref, mr_ref, d_ref))), sems))
    get = own_values(b_ref, cf_ref, ct_ref, mr_ref, d_ref)
    rows, rest = pl.ds(0, ny), pl.ds(ny, 8)
    zero = jnp.zeros((8, nz), F32)

    def body(i):
        vr, vi, c, mr, d = get(i, rows)
        store_fields((p_ref, n_ref, u_ref, v_ref), i + H, rows, (vr, vi), c, mr, d)
        for part in range(2):
            p_ref[part, i + H, rest] = zero
            u_ref[part, i + H, rest] = zero

    loop([(0, nx)], body)
    blank = jnp.zeros((ny + 8, nz), F32)
    for part in range(2):
        u_ref[part, H - 1] = blank
        w_ref[part, H - 1] = blank
        w_ref[part, nx // 2 + H] = blank
    half_step(u_ref, p_ref, w_ref, [(H, nx // 2 + H)])

    def dots(i, acc):
        acc = list(acc)
        y = image(w_ref, n_ref, i + H)
        for a in range(0, ny, 8):
            ct = ct_ref[i, pl.ds(a, 8)]
            yr, yi = y[0][a : a + 8] * ct, y[1][a : a + 8] * ct
            br, bi = b_ref[0, i, pl.ds(a, 8)], b_ref[1, i, pl.ds(a, 8)]
            acc[0] = acc[0] + fold(br * yr + bi * yi)
            acc[1] = acc[1] + fold(br * yi - bi * yr)
            acc[2] = acc[2] + fold(br * br + bi * bi)
        return tuple(acc)

    acc = lax.fori_loop(0, nx // 2, dots, (jnp.zeros((8, 128), F32),) * 3, unroll=2)
    put(pack_lanes(acc), out_ref)


def tails(refs, left, right, ny, fields, coefs, planes):
    rows = pl.ds(ny, 8)
    v = [unpack_pair(right(k), left(k)) for k in fields]
    c = [unpack_pair(right(k), left(k)) for k in coefs]
    for k in range(2):
        store_fields(refs, planes[k], rows, v[k], c[0][k], c[1][k], c[2][k])


def sides_kernel(th_ref, xl_ref, xr_ref, yl_ref, yr_ref, *refs):
    p_ref, n_ref, u_ref, v_ref, w0_ref, w1_ref, v1_ref, v2_ref = refs[4:]
    state = (p_ref, n_ref, u_ref, v_ref)
    ny = xl_ref.shape[2]
    planes = p_ref.shape[1]
    nx = planes - 2 * H
    rows = pl.ds(0, ny)
    for ref, base in ((xl_ref, 0), (xr_ref, nx + H)):

        def side(i):
            vr, vi, c, mr, d = (ref[f, i] for f in range(5))
            store_fields(state, base + i, rows, (vr, vi), c, mr, d)

        loop([(0, H)], side)

    def pair(j):
        coefs = [nx + f * nx // 2 + j for f in range(3)]
        at = (H + 2 * j, H + 2 * j + 1)
        own = (2 * j, 2 * j + 1)
        tails(state, lambda k: yl_ref[k], lambda k: yr_ref[k], ny, own, coefs, at)

    loop([(0, nx // 2)], pair)
    th = shift_from(th_ref)
    two_applications(inside, planes, th, *state, (w0_ref, w1_ref), (v1_ref, v2_ref))


def first_kernel(th_ref, cl_ref, cr_ref, *refs):
    p_ref, n_ref, u_ref, v_ref, w0_ref, w1_ref, v1_ref, v2_ref, top_ref, bot_ref = refs[8:]
    state = (p_ref, n_ref, u_ref, v_ref)
    planes = p_ref.shape[1]
    nx, ny = planes - 2 * H, p_ref.shape[2] - 8
    for ref, base in ((cl_ref, 0), (cr_ref, nx + H)):
        for j in range(H // 2):
            coefs = [H + f * H // 2 + j for f in range(3)]
            at = (base + 2 * j, base + 2 * j + 1)
            own = (2 * j, 2 * j + 1)
            tails(state, lambda k: ref[0, k], lambda k: ref[1, k], ny, own, coefs, at)
    th = shift_from(th_ref)
    two_applications(outside, planes, th, *state, (w0_ref, w1_ref), (v1_ref, v2_ref))
    for out_ref, rows, top in ((top_ref, pl.ds(0, 8), True), (bot_ref, pl.ds(ny - 8, 8), False)):

        def pack(i):
            a, b = v2_ref[0, i + H, rows], v2_ref[1, i + H, rows]
            out_ref[i] = pack_pair(a, b, top)

        loop([(0, nx)], pack)


def early_kernel(b_ref, ct_ref, v1_ref, v2_ref, out_ref):
    fields = ((b_ref, 0, False), (v1_ref, H, True), (v2_ref, H, True))
    put(gram_rows(fields, ct_ref, EARLY), out_ref)


def rows_back_kernel(yl_ref, yr_ref, _, v_ref, lo_ref, hi_ref):
    nx, ny = yl_ref.shape[0], v_ref.shape[2] - 8
    rows = pl.ds(ny, 8)

    def tail(i):
        for part, value in enumerate(unpack_pair(yr_ref[i], yl_ref[i])):
            v_ref[part, i + H, rows] = value

    loop([(0, nx)], tail)
    for part in range(2):
        for i in range(H):
            lo_ref[part, i] = v_ref[part, H + i]
            hi_ref[part, i] = v_ref[part, nx + i]


def inner_kernel(th_ref, p_ref, n_ref, v_ref, u_ref, w2_ref, w3_ref, v3_ref, v4_ref):
    planes = p_ref.shape[1]
    th = shift_from(th_ref)

    def fill(i):
        u = cmul((p_ref[0, i], p_ref[1, i]), (v_ref[0, i], v_ref[1, i]))
        for part in range(2):
            u_ref[part, i] = u[part]

    loop([(H, planes - H)], fill)
    two_applications(
        inside, planes, th, p_ref, n_ref, u_ref, v_ref, (w2_ref, w3_ref), (v3_ref, v4_ref)
    )


def second_kernel(th_ref, e_ref, xl_ref, xr_ref, p_ref, n_ref, b_ref, ct_ref, v1_ref, *refs):
    v2_ref, u_ref, w2_ref, w3_ref, v3_ref, v4_ref, out_ref = refs[6:]
    planes = p_ref.shape[1]
    th = shift_from(th_ref)
    for ref, base in ((xl_ref, 0), (xr_ref, planes - H)):
        for i in range(H):
            v = (ref[0, i], ref[1, i])
            u = cmul((p_ref[0, base + i], p_ref[1, base + i]), v)
            for part in range(2):
                v2_ref[part, base + i] = v[part]
                u_ref[part, base + i] = u[part]
    two_applications(
        outside, planes, th, p_ref, n_ref, u_ref, v2_ref, (w2_ref, w3_ref), (v3_ref, v4_ref)
    )
    fields = (
        (b_ref, 0, False), (v1_ref, H, True), (v2_ref, H, True), (v3_ref, H, True),
        (v4_ref, H, True),
    )
    put(e_ref[0] + gram_rows(fields, ct_ref, LATE, 9), out_ref)


def recurrences(th, gram):
    def inner(x, y):
        total = None
        for i, xi in enumerate(x):
            part = None
            for j, yj in enumerate(y):
                t = cmul(gram[i, j], yj)
                part = t if part is None else cadd(part, t)
            t = cmul(cconj(xi), part)
            total = t if total is None else cadd(total, t)
        return total

    def apply(x):
        scaled = [cmul(th, c) for c in x]
        return [scaled[0]] + [cadd(x[k], scaled[k + 1]) for k in range(len(x) - 1)] + [x[-1]]

    def lincomb(x, s, y):
        out = []
        for k in range(max(len(x), len(y))):
            a = x[k] if k < len(x) else None
            b = cmul(s, y[k]) if k < len(y) else None
            out.append(b if a is None else a if b is None else cadd(a, b))
        return out

    def neg(s):
        return (-s[0], -s[1])

    one = (jnp.ones((1, 1), F32), jnp.zeros((1, 1), F32))
    residual, direction, shadow, answer = [one], [one], [one], []
    rho = inner(shadow, residual)
    for step in range(2):
        image = apply(direction)
        alpha = cdiv(rho, inner(shadow, image))
        half = lincomb(residual, neg(alpha), image)
        second = apply(half)
        prod = inner(second, half)
        norm = inner(second, second)[0] + EPSILON
        omega = (prod[0] / norm, prod[1] / norm)
        answer = lincomb(lincomb(answer, alpha, direction), omega, half)
        residual = lincomb(half, neg(omega), second)
        if step == 0:
            rho_next = inner(shadow, residual)
            beta = cmul(cdiv(rho_next, rho), cdiv(alpha, omega))
            direction = lincomb(residual, beta, lincomb(direction, neg(omega), image))
            rho = rho_next
    return answer, residual


def final_kernel(
    th_ref, g_ref, b_ref, cf_ref, ct_ref,
    w0_ref, w1_ref, w2_ref, w3_ref, v1_ref, v2_ref, v3_ref, v4_ref,
    sol_any, res_any,
    sol_ref, res_ref, sems,
):
    nx, ny, nz = cf_ref.shape
    th = shift_from(th_ref)
    entries = gram_entries(total_of(g_ref), EARLY + LATE, {})
    answer, residual = recurrences(th, entries)

    def spread(c):
        return tuple(jnp.broadcast_to(x, (8, nz)) for x in c)

    answer, residual = [spread(c) for c in answer], [spread(c) for c in residual]

    def body(i, carry):
        for a in range(0, ny, 8):
            rows = pl.ds(a, 8)
            acc = None
            for c, ref in zip(answer, (w0_ref, w1_ref, w2_ref, w3_ref)):
                t = cmul(c, (ref[0, i + H, rows], ref[1, i + H, rows]))
                acc = t if acc is None else cadd(acc, t)
            inv = SCALE / cf_ref[i, rows]
            sol_ref[0, i, rows] = acc[0] * inv
            sol_ref[1, i, rows] = acc[1] * inv
            acc = None
            for c, ref in zip(residual[1:], (v1_ref, v2_ref, v3_ref, v4_ref)):
                t = cmul(c, (ref[0, i + H, rows], ref[1, i + H, rows]))
                acc = t if acc is None else cadd(acc, t)
            ct = ct_ref[i, rows]
            t = cmul(residual[0], (b_ref[0, i, rows], b_ref[1, i, rows]))
            res_ref[0, i, rows] = acc[0] * ct + t[0]
            res_ref[1, i, rows] = acc[1] * ct + t[1]
        return carry

    copies = []
    for k in range(CHUNKS):
        lo, hi = k * nx // CHUNKS, (k + 1) * nx // CHUNKS
        lax.fori_loop(lo, hi, body, 0)
        span = pl.ds(lo, hi - lo)
        for a, b in ((sol_ref, sol_any), (res_ref, res_any)):
            copies.append(
                pltpu.make_async_copy(a.at[:, span], b.at[:, span], sems.at[len(copies)])
            )
            copies[-1].start()
    for copy in copies:
        copy.wait()


def call(kernel, outs, scratch, *args, alias=None):
    return pl.pallas_call(
        kernel,
        out_shape=[jax.ShapeDtypeStruct(s, F32) for s in outs],
        in_specs=vmem(len(args)),
        out_specs=vmem(len(outs)),
        scratch_shapes=[pltpu.VMEM(s, F32) for s in scratch],
        input_output_aliases=alias or {},
        compiler_params=pltpu.CompilerParams(vmem_limit_bytes=LIMIT),
    )(*args)


def edge_call(kernel, outs, scratch, *args):
    return pl.pallas_call(
        kernel,
        out_shape=[jax.ShapeDtypeStruct(s, F32) for s in outs],
        in_specs=[pl.BlockSpec(memory_space=pl.ANY)] * len(args),
        out_specs=vmem(len(outs)),
        scratch_shapes=[pltpu.VMEM(s, F32) for s in scratch] + [pltpu.SemaphoreType.DMA((20,))],
        compiler_params=pltpu.CompilerParams(vmem_limit_bytes=LIMIT),
    )(*(pltpu.with_memory_space_constraint(x, pltpu.HBM) for x in args))


def both_ways(to_lower, to_upper, axis):
    n = lax.axis_size(axis)
    up = [(i, i + 1) for i in range(n - 1)]
    down = [(i + 1, i) for i in range(n - 1)]
    return lax.ppermute(to_upper, axis, up), lax.ppermute(to_lower, axis, down)


def local(b, cf, ct, mr, d):
    nx, ny, nz = cf.shape
    peers = lax.axis_size("gx") * lax.axis_size("gy")
    planes = nx + 2 * H
    own = (2, nx, ny, nz)
    ext = (2, planes, ny + 2 * H, nz)
    face = (2, H, ny + 2 * H, nz)
    rim = (nx + 3 * nx // 2, 8, nz)
    corner = (2, H + 3 * H // 2, 8, nz)
    inputs = (b, cf, ct, mr, d)

    lo, hi, top, bot = edge_call(
        edges_kernel, [(5, H, ny, nz)] * 2 + [rim, rim],
        [(2, 2, H, ny, nz), (2, 4, H, ny, nz), (2, 2, nx, 8, nz), (2, 4, nx, 8, nz)], *inputs
    )
    yl, yr = both_ways(top, bot, "gy")
    xl, xr = both_ways(lo, hi, "gx")
    *state, th, b, cf, ct = edge_call(
        own_kernel, [ext] * 4 + [(peers, 1, 128), b.shape, cf.shape, ct.shape],
        [mr.shape, d.shape, ext], *inputs,
    )
    th = lax.all_to_all(th, AXES, 0, 0)
    lo, hi = call(corners_kernel, [corner] * 2, [], th, yl, yr)
    cl, cr = both_ways(lo, hi, "gx")
    state = call(
        sides_kernel, [ext] * 8, [], th, xl, xr, yl, yr, *state,
        alias={5 + k: k for k in range(4)},
    )
    p, n, _, _, w0, w1, v1, v2, top, bot = call(
        first_kernel, [ext] * 8 + [(nx, 8, nz)] * 2, [], th, cl, cr, *state,
        alias={3 + k: k for k in range(8)},
    )
    yl, yr = both_ways(top, bot, "gy")
    early = call(early_kernel, [(1, 1, 128)], [], b, ct, v1, v2)[0]
    v2, lo, hi = call(rows_back_kernel, [ext, face, face], [], yl, yr, v2, alias={2: 0})
    xl, xr = both_ways(lo, hi, "gx")
    state = call(inner_kernel, [ext] * 5, [], th, p, n, v2)
    v2, _, w2, w3, v3, v4, gram = call(
        second_kernel, [ext] * 6 + [(peers, 1, 128)], [],
        th, early, xl, xr, p, n, b, ct, v1, v2, *state,
        alias={9 + k: k for k in range(6)},
    )
    gram = lax.all_to_all(gram, AXES, 0, 0)
    args = (th, gram, b, cf, ct, w0, w1, w2, w3, v1, v2, v3, v4)
    return tuple(
        pl.pallas_call(
            final_kernel,
            out_shape=[jax.ShapeDtypeStruct(own, F32)] * 2,
            in_specs=vmem(len(args)),
            out_specs=[pl.BlockSpec(memory_space=pl.ANY)] * 2,
            scratch_shapes=[pltpu.VMEM(own, F32)] * 2 + [pltpu.SemaphoreType.DMA((2 * CHUNKS,))],
            compiler_params=pltpu.CompilerParams(vmem_limit_bytes=LIMIT),
        )(*args)
    )


def solution(mesh):
    field, coef = P(None, "gx", "gy", None), P("gx", "gy", None)
    return jax.shard_map(
        local,
        mesh=mesh,
        in_specs=(field, coef, coef, coef, coef),
        out_specs=(field, field),
        check_vma=False,
    )
```

```python
import jax
import jax.numpy as jnp
from jax import lax
from jax.experimental import pallas as pl
from jax.experimental.pallas import tpu as pltpu
from jax.sharding import PartitionSpec as P

OMEGA = 0.8
EPSILON = 1e-06
H = 4
AXES = ("gx", "gy")
F32 = jnp.float32
LIMIT = 24 * 1024 * 1024
SCALE = 160.0
CHUNKS = 4
FALLBACK = (0.72, -0.28)


def vmem(n):
    return [pl.BlockSpec(memory_space=pltpu.VMEM)] * n


def cmul(a, b):
    return (a[0] * b[0] - a[1] * b[1], a[0] * b[1] + a[1] * b[0])


def cconj(a):
    return (a[0], -a[1])


def cadd(a, b):
    return (a[0] + b[0], a[1] + b[1])


def csub(a, b):
    return (a[0] - b[0], a[1] - b[1])


def cdiv(n, d):
    scale = d[0] * d[0] + d[1] * d[1]
    return (
        (n[0] * d[0] + n[1] * d[1]) / scale,
        (n[1] * d[0] - n[0] * d[1]) / scale,
    )


def smooth_yz(plane):
    rows, lanes = plane.shape
    lane = lax.broadcasted_iota(jnp.int32, (rows, 128), 1)
    parts = [plane[:, k : k + 128] for k in range(0, lanes, 128)]
    parts = [x + pltpu.roll(x, rows - 1, 0) for x in parts]
    parts = [x + pltpu.roll(x, 1, 0) for x in parts]
    ups = [pltpu.roll(x, 1, 1) for x in parts]
    downs = [pltpu.roll(x, 127, 1) for x in parts]
    out = []
    for k, x in enumerate(parts):
        up = jnp.where(lane == 0, ups[k - 1] if k else 0.0, ups[k])
        down = jnp.where(lane == 127, downs[k + 1] if k + 1 < len(parts) else 0.0, downs[k])
        out.append(x + x + up + down)
    return jnp.concatenate(out, axis=1)


def sums(ref, i):
    out = []
    for part in range(2):
        mid = ref[part, i]
        out.append(smooth_yz((ref[part, i - 1] + mid) + (mid + ref[part, i + 1])))
    return tuple(out)


def coefficients(c, mr, d):
    shift = d + 0.5 * mr
    mod = mr * mr + shift * shift
    den = mod * c
    inv = 1.0 / jnp.where(den == 0.0, 1.0, den)
    k = (OMEGA / SCALE) * c * c * inv
    rc = SCALE * mod * inv
    return (k * mr, -(k * shift)), (rc * mr + 8.0, rc * d)


def loop(ranges, body):
    for lo, hi in ranges:

        def step(i, carry):
            body(i)
            return carry

        lax.fori_loop(lo, hi, step, 0, unroll=4)


def half_step(u_ref, p_ref, w_ref, ranges):
    def body(i):
        u = (u_ref[0, i], u_ref[1, i])
        s = sums(u_ref, i)
        pw = cmul((p_ref[0, i], p_ref[1, i]), (s[0] - 8.0 * u[0], s[1] - 8.0 * u[1]))
        w_ref[0, i] = 1.2 * u[0] + pw[0]
        w_ref[1, i] = 1.2 * u[1] + pw[1]

    loop(ranges, body)


def image(w_ref, n_ref, i):
    nw = cmul((n_ref[0, i], n_ref[1, i]), (w_ref[0, i], w_ref[1, i]))
    return csub(nw, sums(w_ref, i))


def advance(w_ref, n_ref, v_ref, th, next_ref, ranges, p_ref=None, u_ref=None):
    def body(i):
        y = csub(image(w_ref, n_ref, i), cmul(th, (v_ref[0, i], v_ref[1, i])))
        for part in range(2):
            next_ref[part, i] = y[part]
        if p_ref is not None:
            u = cmul((p_ref[0, i], p_ref[1, i]), y)
            for part in range(2):
                u_ref[part, i] = u[part]

    loop(ranges, body)


def inside(planes, k):
    return [(H + k, planes - H - k)]


def outside(planes, k):
    return [(k, H + k), (planes - H - k, planes - k)]


def two_applications(part_of, planes, th, p_ref, n_ref, u_ref, v_ref, w_refs, next_refs):
    half_step(u_ref, p_ref, w_refs[0], part_of(planes, 1))
    advance(w_refs[0], n_ref, v_ref, th, next_refs[0], part_of(planes, 2), p_ref, u_ref)
    half_step(u_ref, p_ref, w_refs[1], part_of(planes, 3))
    advance(w_refs[1], n_ref, next_refs[0], th, next_refs[1], part_of(planes, 4))


def total_of(ref):
    rows = ref[...].reshape(ref.shape[0], ref.shape[-1])
    tot = jnp.sum(rows, axis=0, keepdims=True)
    lane = lax.broadcasted_iota(jnp.int32, tot.shape, 1)
    return lambda k: jnp.sum(jnp.where(lane == k, tot, 0.0), axis=1, keepdims=True)


def pack_lanes(values, first=0):
    lane = lax.broadcasted_iota(jnp.int32, (1, 128), 1)
    row = jnp.zeros((1, 128), F32)
    for k, v in enumerate(values, first):
        s = jnp.sum(jnp.sum(v, axis=0, keepdims=True), axis=1, keepdims=True)
        row = jnp.where(lane == k, s, row)
    return row


def fold(x):
    out = x[:, :128]
    for b in range(128, x.shape[1], 128):
        out = out + x[:, b : b + 128]
    return out


def pairs_of(rights):
    return [(left, right) for right in rights for left in range(right + 1)]


def gram_rows(fields, ct_ref, pairs, spans, first=0):
    ny = ct_ref.shape[1]
    used = sorted({k for pair in pairs for k in pair})
    count = sum(1 if left == right else 2 for left, right in pairs)

    def body(i, acc):
        acc = list(acc)
        for a in range(0, ny, 8):
            rows = pl.ds(a, 8)
            ct = ct_ref[i, rows]
            vs = {}
            for k in used:
                ref, base, scaled = fields[k]
                v = (ref[0, i + base, rows], ref[1, i + base, rows])
                vs[k] = (ct * v[0], ct * v[1]) if scaled else v
            k = 0
            for left, right in pairs:
                (lr, li), (rr, ri) = vs[left], vs[right]
                acc[k] = acc[k] + fold(lr * rr + li * ri)
                k += 1
                if right > left:
                    acc[k] = acc[k] + fold(lr * ri - li * rr)
                    k += 1
        return tuple(acc)

    acc = (jnp.zeros((8, 128), F32),) * count
    for lo, hi in spans:
        acc = lax.fori_loop(lo, hi, body, acc)
    return pack_lanes(acc, first)


def put(row, out_ref):
    for k in range(out_ref.shape[0]):
        out_ref[k] = row


def gram_entries(pick, pairs, entries):
    k = 0
    for left, right in pairs:
        if left == right:
            entries[left, right] = (pick(k), jnp.zeros((1, 1), F32))
            k += 1
        else:
            entries[left, right] = (pick(k), pick(k + 1))
            entries[right, left] = cconj(entries[left, right])
            k += 2
    return entries


def shift_from(ref):
    pick = total_of(ref)
    den = pick(2)
    safe = jnp.where(den > 0.0, den, 1.0)
    return tuple(jnp.where(den > 0.0, pick(k) / safe, FALLBACK[k]) for k in range(2))


EARLY = pairs_of((0, 1, 2))
LATE = pairs_of((3, 4))


def pack_pair(first, second, top):
    sub = lax.broadcasted_iota(jnp.int32, first.shape, 0)
    rolled = pltpu.roll(second, 4, 0)
    if top:
        return jnp.where(sub < 4, first, rolled)
    return jnp.where(sub < 4, rolled, first)


def unpack_pair(right, left):
    sub = lax.broadcasted_iota(jnp.int32, right.shape, 0)
    first = jnp.where(sub < 4, right, left)
    second = pltpu.roll(jnp.where(sub < 4, left, right), 4, 0)
    return first, second


def own_values(b_ref, cf_ref, ct_ref, mr_ref, d_ref):
    def get(i, rows):
        ct = ct_ref[i, rows]
        r = 1.0 / ct
        return (
            b_ref[0, i, rows] * r,
            b_ref[1, i, rows] * r,
            cf_ref[i, rows] * ct,
            mr_ref[i, rows],
            d_ref[i, rows],
        )

    return get


def fetch(pairs, sems):
    copies = [pltpu.make_async_copy(a, b, sems.at[k]) for k, (a, b) in enumerate(pairs)]
    for c in copies:
        c.start()
    return copies


def wait_for(copies):
    for c in copies:
        c.wait()


def edges_kernel(
    b_ref, cf_ref, ct_ref, mr_ref, d_ref, lo_ref, hi_ref, top_ref, bot_ref,
    blocks, coefs, row_blocks, row_coefs, sems,
):
    nx, ny, _ = cf_ref.shape
    pairs = []
    for side, at in enumerate((0, nx - H)):
        span = pl.ds(at, H)
        pairs.append((b_ref.at[:, span], blocks.at[side]))
        for k, ref in enumerate((cf_ref, ct_ref, mr_ref, d_ref)):
            pairs.append((ref.at[span], coefs.at[side, k]))
    for side, at in enumerate((0, ny - 8)):
        rows = pl.ds(at, 8)
        pairs.append((b_ref.at[:, :, rows], row_blocks.at[side]))
        for k, ref in enumerate((cf_ref, ct_ref, mr_ref, d_ref)):
            pairs.append((ref.at[:, rows], row_coefs.at[side, k]))
    copies = fetch(pairs, sems)
    wait_for(copies[:10])
    for side, out_ref in enumerate((lo_ref, hi_ref)):
        get = own_values(blocks.at[side], *(coefs.at[side, k] for k in range(4)))
        for i in range(H):
            for f, value in enumerate(get(i, pl.ds(0, ny))):
                out_ref[f, i] = value
    wait_for(copies[10:])
    for side, out_ref in enumerate((top_ref, bot_ref)):
        get = own_values(row_blocks.at[side], *(row_coefs.at[side, k] for k in range(4)))
        top = side == 0

        def body(j, carry):
            a, b = get(2 * j, pl.ds(0, 8)), get(2 * j + 1, pl.ds(0, 8))
            out_ref[2 * j] = pack_pair(a[0], a[1], top)
            out_ref[2 * j + 1] = pack_pair(b[0], b[1], top)
            for f in range(3):
                out_ref[nx + f * nx // 2 + j] = pack_pair(a[2 + f], b[2 + f], top)
            return carry

        lax.fori_loop(0, nx // 2, body, 0, unroll=2)


def corners_kernel(after_ref, yl_ref, yr_ref, lo_ref, hi_ref):
    count = yl_ref.shape[0]
    nx = count * 2 // 5
    for k, ref in enumerate((yl_ref, yr_ref)):
        for out_ref, base in ((lo_ref, 0), (hi_ref, nx - H)):
            for i in range(H):
                out_ref[k, i] = ref[base + i]
            for f in range(3):
                for j in range(H // 2):
                    at = nx + f * nx // 2 + base // 2 + j
                    out_ref[k, H + f * H // 2 + j] = ref[at]


def store_fields(refs, plane, rows, v, c, mr, d):
    p_ref, n_ref, u_ref, v_ref = refs
    p, n = coefficients(c, mr, d)
    u = cmul(p, v)
    for part in range(2):
        p_ref[part, plane, rows] = p[part]
        n_ref[part, plane, rows] = n[part]
        u_ref[part, plane, rows] = u[part]
        v_ref[part, plane, rows] = v[part]


def own_kernel(
    b_any, cf_any, ct_any, mr_any, d_any,
    p_ref, n_ref, u_ref, v_ref, out_ref, b_ref, cf_ref, ct_ref,
    mr_ref, d_ref, w_ref, sems,
):
    nx, ny, nz = cf_ref.shape
    sources = (b_any, cf_any, ct_any, mr_any, d_any)
    wait_for(fetch(list(zip(sources, (b_ref, cf_ref, ct_ref, mr_ref, d_ref))), sems))
    get = own_values(b_ref, cf_ref, ct_ref, mr_ref, d_ref)
    rows, rest = pl.ds(0, ny), pl.ds(ny, 8)
    zero = jnp.zeros((8, nz), F32)

    def body(i):
        vr, vi, c, mr, d = get(i, rows)
        store_fields((p_ref, n_ref, u_ref, v_ref), i + H, rows, (vr, vi), c, mr, d)
        for part in range(2):
            p_ref[part, i + H, rest] = zero
            u_ref[part, i + H, rest] = zero

    loop([(0, nx)], body)
    blank = jnp.zeros((ny + 8, nz), F32)
    for part in range(2):
        u_ref[part, H - 1] = blank
        w_ref[part, H - 1] = blank
        w_ref[part, nx // 2 + H] = blank
    half_step(u_ref, p_ref, w_ref, [(H, nx // 2 + H)])

    def dots(i, acc):
        acc = list(acc)
        y = image(w_ref, n_ref, i + H)
        for a in range(0, ny, 8):
            ct = ct_ref[i, pl.ds(a, 8)]
            yr, yi = y[0][a : a + 8] * ct, y[1][a : a + 8] * ct
            br, bi = b_ref[0, i, pl.ds(a, 8)], b_ref[1, i, pl.ds(a, 8)]
            acc[0] = acc[0] + fold(br * yr + bi * yi)
            acc[1] = acc[1] + fold(br * yi - bi * yr)
            acc[2] = acc[2] + fold(br * br + bi * bi)
        return tuple(acc)

    acc = lax.fori_loop(0, nx // 2, dots, (jnp.zeros((8, 128), F32),) * 3, unroll=2)
    put(pack_lanes(acc), out_ref)


def tails(refs, left, right, ny, fields, coefs, planes):
    rows = pl.ds(ny, 8)
    v = [unpack_pair(right(k), left(k)) for k in fields]
    c = [unpack_pair(right(k), left(k)) for k in coefs]
    for k in range(2):
        store_fields(refs, planes[k], rows, v[k], c[0][k], c[1][k], c[2][k])


def sides_kernel(th_ref, xl_ref, xr_ref, yl_ref, yr_ref, *refs):
    p_ref, n_ref, u_ref, v_ref, w0_ref, w1_ref, v1_ref, v2_ref = refs[4:]
    state = (p_ref, n_ref, u_ref, v_ref)
    ny = xl_ref.shape[2]
    planes = p_ref.shape[1]
    nx = planes - 2 * H
    rows = pl.ds(0, ny)
    for ref, base in ((xl_ref, 0), (xr_ref, nx + H)):

        def side(i):
            vr, vi, c, mr, d = (ref[f, i] for f in range(5))
            store_fields(state, base + i, rows, (vr, vi), c, mr, d)

        loop([(0, H)], side)

    def pair(j):
        coefs = [nx + f * nx // 2 + j for f in range(3)]
        at = (H + 2 * j, H + 2 * j + 1)
        own = (2 * j, 2 * j + 1)
        tails(state, lambda k: yl_ref[k], lambda k: yr_ref[k], ny, own, coefs, at)

    loop([(0, nx // 2)], pair)
    th = shift_from(th_ref)
    two_applications(inside, planes, th, *state, (w0_ref, w1_ref), (v1_ref, v2_ref))


def first_kernel(th_ref, cl_ref, cr_ref, *refs):
    p_ref, n_ref, u_ref, v_ref, w0_ref, w1_ref, v1_ref, v2_ref, top_ref, bot_ref = refs[8:]
    state = (p_ref, n_ref, u_ref, v_ref)
    planes = p_ref.shape[1]
    nx, ny = planes - 2 * H, p_ref.shape[2] - 8
    for ref, base in ((cl_ref, 0), (cr_ref, nx + H)):
        for j in range(H // 2):
            coefs = [H + f * H // 2 + j for f in range(3)]
            at = (base + 2 * j, base + 2 * j + 1)
            own = (2 * j, 2 * j + 1)
            tails(state, lambda k: ref[0, k], lambda k: ref[1, k], ny, own, coefs, at)
    th = shift_from(th_ref)
    two_applications(outside, planes, th, *state, (w0_ref, w1_ref), (v1_ref, v2_ref))
    for out_ref, rows, top in ((top_ref, pl.ds(0, 8), True), (bot_ref, pl.ds(ny - 8, 8), False)):

        def pack(i):
            a, b = v2_ref[0, i + H, rows], v2_ref[1, i + H, rows]
            out_ref[i] = pack_pair(a, b, top)

        loop([(0, nx)], pack)


def early_kernel(b_ref, ct_ref, v1_ref, v2_ref, out_ref):
    fields = ((b_ref, 0, False), (v1_ref, H, True), (v2_ref, H, True))
    put(gram_rows(fields, ct_ref, EARLY, [(0, ct_ref.shape[0])]), out_ref)


def rows_back_kernel(yl_ref, yr_ref, _, v_ref, lo_ref, hi_ref):
    nx, ny = yl_ref.shape[0], v_ref.shape[2] - 8
    rows = pl.ds(ny, 8)

    def tail(i):
        for part, value in enumerate(unpack_pair(yr_ref[i], yl_ref[i])):
            v_ref[part, i + H, rows] = value

    loop([(0, nx)], tail)
    for part in range(2):
        for i in range(H):
            lo_ref[part, i] = v_ref[part, H + i]
            hi_ref[part, i] = v_ref[part, nx + i]


def late_fields(b_ref, *refs):
    return ((b_ref, 0, False),) + tuple((ref, H, True) for ref in refs)


def inner_kernel(
    th_ref, e_ref, p_ref, n_ref, b_ref, ct_ref, v1_ref, v_ref,
    u_ref, w2_ref, w3_ref, v3_ref, v4_ref, out_ref,
):
    planes = p_ref.shape[1]
    th = shift_from(th_ref)

    def fill(i):
        u = cmul((p_ref[0, i], p_ref[1, i]), (v_ref[0, i], v_ref[1, i]))
        for part in range(2):
            u_ref[part, i] = u[part]

    loop([(H, planes - H)], fill)
    two_applications(
        inside, planes, th, p_ref, n_ref, u_ref, v_ref, (w2_ref, w3_ref), (v3_ref, v4_ref)
    )
    fields = late_fields(b_ref, v1_ref, v_ref, v3_ref, v4_ref)
    put(e_ref[0] + gram_rows(fields, ct_ref, LATE, [(H, planes - 3 * H)], 9), out_ref)


def second_kernel(th_ref, e_ref, xl_ref, xr_ref, p_ref, n_ref, b_ref, ct_ref, v1_ref, *refs):
    v2_ref, u_ref, w2_ref, w3_ref, v3_ref, v4_ref, out_ref = refs[6:]
    planes = p_ref.shape[1]
    th = shift_from(th_ref)
    for ref, base in ((xl_ref, 0), (xr_ref, planes - H)):
        for i in range(H):
            v = (ref[0, i], ref[1, i])
            u = cmul((p_ref[0, base + i], p_ref[1, base + i]), v)
            for part in range(2):
                v2_ref[part, base + i] = v[part]
                u_ref[part, base + i] = u[part]
    two_applications(
        outside, planes, th, p_ref, n_ref, u_ref, v2_ref, (w2_ref, w3_ref), (v3_ref, v4_ref)
    )
    fields = late_fields(b_ref, v1_ref, v2_ref, v3_ref, v4_ref)
    nx = planes - 2 * H
    put(e_ref[0] + gram_rows(fields, ct_ref, LATE, [(0, H), (nx - H, nx)], 9), out_ref)


def recurrences(th, gram):
    def inner(x, y):
        total = None
        for i, xi in enumerate(x):
            part = None
            for j, yj in enumerate(y):
                t = cmul(gram[i, j], yj)
                part = t if part is None else cadd(part, t)
            t = cmul(cconj(xi), part)
            total = t if total is None else cadd(total, t)
        return total

    def apply(x):
        scaled = [cmul(th, c) for c in x]
        return [scaled[0]] + [cadd(x[k], scaled[k + 1]) for k in range(len(x) - 1)] + [x[-1]]

    def lincomb(x, s, y):
        out = []
        for k in range(max(len(x), len(y))):
            a = x[k] if k < len(x) else None
            b = cmul(s, y[k]) if k < len(y) else None
            out.append(b if a is None else a if b is None else cadd(a, b))
        return out

    def neg(s):
        return (-s[0], -s[1])

    one = (jnp.ones((1, 1), F32), jnp.zeros((1, 1), F32))
    residual, direction, shadow, answer = [one], [one], [one], []
    rho = inner(shadow, residual)
    for step in range(2):
        image = apply(direction)
        alpha = cdiv(rho, inner(shadow, image))
        half = lincomb(residual, neg(alpha), image)
        second = apply(half)
        prod = inner(second, half)
        norm = inner(second, second)[0] + EPSILON
        omega = (prod[0] / norm, prod[1] / norm)
        answer = lincomb(lincomb(answer, alpha, direction), omega, half)
        residual = lincomb(half, neg(omega), second)
        if step == 0:
            rho_next = inner(shadow, residual)
            beta = cmul(cdiv(rho_next, rho), cdiv(alpha, omega))
            direction = lincomb(residual, beta, lincomb(direction, neg(omega), image))
            rho = rho_next
    return answer, residual


def final_kernel(
    th_ref, g_ref, b_ref, cf_ref, ct_ref,
    w0_ref, w1_ref, w2_ref, w3_ref, v1_ref, v2_ref, v3_ref, v4_ref,
    sol_any, res_any,
    sol_ref, res_ref, sems,
):
    nx, ny, nz = cf_ref.shape
    th = shift_from(th_ref)
    entries = gram_entries(total_of(g_ref), EARLY + LATE, {})
    answer, residual = recurrences(th, entries)

    def spread(c):
        return tuple(jnp.broadcast_to(x, (8, nz)) for x in c)

    answer, residual = [spread(c) for c in answer], [spread(c) for c in residual]

    def body(i, carry):
        for a in range(0, ny, 8):
            rows = pl.ds(a, 8)
            acc = None
            for c, ref in zip(answer, (w0_ref, w1_ref, w2_ref, w3_ref)):
                t = cmul(c, (ref[0, i + H, rows], ref[1, i + H, rows]))
                acc = t if acc is None else cadd(acc, t)
            inv = SCALE / cf_ref[i, rows]
            sol_ref[0, i, rows] = acc[0] * inv
            sol_ref[1, i, rows] = acc[1] * inv
            acc = None
            for c, ref in zip(residual[1:], (v1_ref, v2_ref, v3_ref, v4_ref)):
                t = cmul(c, (ref[0, i + H, rows], ref[1, i + H, rows]))
                acc = t if acc is None else cadd(acc, t)
            ct = ct_ref[i, rows]
            t = cmul(residual[0], (b_ref[0, i, rows], b_ref[1, i, rows]))
            res_ref[0, i, rows] = acc[0] * ct + t[0]
            res_ref[1, i, rows] = acc[1] * ct + t[1]
        return carry

    copies = []
    for k in range(CHUNKS):
        lo, hi = k * nx // CHUNKS, (k + 1) * nx // CHUNKS
        lax.fori_loop(lo, hi, body, 0)
        span = pl.ds(lo, hi - lo)
        for a, b in ((sol_ref, sol_any), (res_ref, res_any)):
            copies.append(
                pltpu.make_async_copy(a.at[:, span], b.at[:, span], sems.at[len(copies)])
            )
            copies[-1].start()
    for copy in copies:
        copy.wait()


def call(kernel, outs, scratch, *args, alias=None):
    return pl.pallas_call(
        kernel,
        out_shape=[jax.ShapeDtypeStruct(s, F32) for s in outs],
        in_specs=vmem(len(args)),
        out_specs=vmem(len(outs)),
        scratch_shapes=[pltpu.VMEM(s, F32) for s in scratch],
        input_output_aliases=alias or {},
        compiler_params=pltpu.CompilerParams(vmem_limit_bytes=LIMIT),
    )(*args)


def edge_call(kernel, outs, scratch, *args):
    return pl.pallas_call(
        kernel,
        out_shape=[jax.ShapeDtypeStruct(s, F32) for s in outs],
        in_specs=[pl.BlockSpec(memory_space=pl.ANY)] * len(args),
        out_specs=vmem(len(outs)),
        scratch_shapes=[pltpu.VMEM(s, F32) for s in scratch] + [pltpu.SemaphoreType.DMA((20,))],
        compiler_params=pltpu.CompilerParams(vmem_limit_bytes=LIMIT),
    )(*(pltpu.with_memory_space_constraint(x, pltpu.HBM) for x in args))


def both_ways(to_lower, to_upper, axis):
    n = lax.axis_size(axis)
    up = [(i, i + 1) for i in range(n - 1)]
    down = [(i + 1, i) for i in range(n - 1)]
    return lax.ppermute(to_upper, axis, up), lax.ppermute(to_lower, axis, down)


def local(b, cf, ct, mr, d):
    nx, ny, nz = cf.shape
    peers = lax.axis_size("gx") * lax.axis_size("gy")
    planes = nx + 2 * H
    own = (2, nx, ny, nz)
    ext = (2, planes, ny + 2 * H, nz)
    face = (2, H, ny + 2 * H, nz)
    rim = (nx + 3 * nx // 2, 8, nz)
    corner = (2, H + 3 * H // 2, 8, nz)
    inputs = (b, cf, ct, mr, d)

    lo, hi, top, bot = edge_call(
        edges_kernel, [(5, H, ny, nz)] * 2 + [rim, rim],
        [(2, 2, H, ny, nz), (2, 4, H, ny, nz), (2, 2, nx, 8, nz), (2, 4, nx, 8, nz)], *inputs
    )
    yl, yr = both_ways(top, bot, "gy")
    xl, xr = both_ways(lo, hi, "gx")
    *state, th, b, cf, ct = edge_call(
        own_kernel, [ext] * 4 + [(peers, 1, 128), b.shape, cf.shape, ct.shape],
        [mr.shape, d.shape, ext], *inputs,
    )
    th = lax.all_to_all(th, AXES, 0, 0)
    lo, hi = call(corners_kernel, [corner] * 2, [], th, yl, yr)
    cl, cr = both_ways(lo, hi, "gx")
    state = call(
        sides_kernel, [ext] * 8, [], th, xl, xr, yl, yr, *state,
        alias={5 + k: k for k in range(4)},
    )
    p, n, _, _, w0, w1, v1, v2, top, bot = call(
        first_kernel, [ext] * 8 + [(nx, 8, nz)] * 2, [], th, cl, cr, *state,
        alias={3 + k: k for k in range(8)},
    )
    yl, yr = both_ways(top, bot, "gy")
    early = call(early_kernel, [(1, 1, 128)], [], b, ct, v1, v2)[0]
    v2, lo, hi = call(rows_back_kernel, [ext, face, face], [], yl, yr, v2, alias={2: 0})
    xl, xr = both_ways(lo, hi, "gx")
    *state, early = call(
        inner_kernel, [ext] * 5 + [(1, 1, 128)], [], th, early, p, n, b, ct, v1, v2
    )
    v2, _, w2, w3, v3, v4, gram = call(
        second_kernel, [ext] * 6 + [(peers, 1, 128)], [],
        th, early, xl, xr, p, n, b, ct, v1, v2, *state,
        alias={9 + k: k for k in range(6)},
    )
    gram = lax.all_to_all(gram, AXES, 0, 0)
    args = (th, gram, b, cf, ct, w0, w1, w2, w3, v1, v2, v3, v4)
    return tuple(
        pl.pallas_call(
            final_kernel,
            out_shape=[jax.ShapeDtypeStruct(own, F32)] * 2,
            in_specs=vmem(len(args)),
            out_specs=[pl.BlockSpec(memory_space=pl.ANY)] * 2,
            scratch_shapes=[pltpu.VMEM(own, F32)] * 2 + [pltpu.SemaphoreType.DMA((2 * CHUNKS,))],
            compiler_params=pltpu.CompilerParams(vmem_limit_bytes=LIMIT),
        )(*args)
    )


def solution(mesh):
    field, coef = P(None, "gx", "gy", None), P("gx", "gy", None)
    return jax.shard_map(
        local,
        mesh=mesh,
        in_specs=(field, coef, coef, coef, coef),
        out_specs=(field, field),
        check_vma=False,
    )
```

```python
import jax
import jax.numpy as jnp
from jax import lax
from jax.experimental import pallas as pl
from jax.experimental.pallas import tpu as pltpu
from jax.sharding import PartitionSpec as P

OMEGA = 0.8
EPSILON = 1e-06
H = 4
AXES = ("gx", "gy")
F32 = jnp.float32
LIMIT = 24 * 1024 * 1024
SCALE = 160.0
CHUNKS = 8
FALLBACK = (0.72, -0.28)


def vmem(n):
    return [pl.BlockSpec(memory_space=pltpu.VMEM)] * n


def cmul(a, b):
    return (a[0] * b[0] - a[1] * b[1], a[0] * b[1] + a[1] * b[0])


def cconj(a):
    return (a[0], -a[1])


def cadd(a, b):
    return (a[0] + b[0], a[1] + b[1])


def csub(a, b):
    return (a[0] - b[0], a[1] - b[1])


def cdiv(n, d):
    scale = d[0] * d[0] + d[1] * d[1]
    return (
        (n[0] * d[0] + n[1] * d[1]) / scale,
        (n[1] * d[0] - n[0] * d[1]) / scale,
    )


def smooth_yz(plane):
    rows, lanes = plane.shape
    lane = lax.broadcasted_iota(jnp.int32, (rows, 128), 1)
    parts = [plane[:, k : k + 128] for k in range(0, lanes, 128)]
    parts = [x + pltpu.roll(x, rows - 1, 0) for x in parts]
    parts = [x + pltpu.roll(x, 1, 0) for x in parts]
    ups = [pltpu.roll(x, 1, 1) for x in parts]
    downs = [pltpu.roll(x, 127, 1) for x in parts]
    out = []
    for k, x in enumerate(parts):
        up = jnp.where(lane == 0, ups[k - 1] if k else 0.0, ups[k])
        down = jnp.where(lane == 127, downs[k + 1] if k + 1 < len(parts) else 0.0, downs[k])
        out.append(x + x + up + down)
    return jnp.concatenate(out, axis=1)


def sums(ref, i):
    out = []
    for part in range(2):
        mid = ref[part, i]
        out.append(smooth_yz((ref[part, i - 1] + mid) + (mid + ref[part, i + 1])))
    return tuple(out)


def coefficients(c, mr, d):
    shift = d + 0.5 * mr
    mod = mr * mr + shift * shift
    den = mod * c
    inv = 1.0 / jnp.where(den == 0.0, 1.0, den)
    k = (OMEGA / SCALE) * c * c * inv
    rc = SCALE * mod * inv
    return (k * mr, -(k * shift)), (rc * mr + 8.0, rc * d)


def loop(ranges, body):
    for lo, hi in ranges:

        def step(i, carry):
            body(i)
            return carry

        lax.fori_loop(lo, hi, step, 0, unroll=4)


def half_step(u_ref, p_ref, w_ref, ranges):
    def body(i):
        u = (u_ref[0, i], u_ref[1, i])
        s = sums(u_ref, i)
        pw = cmul((p_ref[0, i], p_ref[1, i]), (s[0] - 8.0 * u[0], s[1] - 8.0 * u[1]))
        w_ref[0, i] = 1.2 * u[0] + pw[0]
        w_ref[1, i] = 1.2 * u[1] + pw[1]

    loop(ranges, body)


def image(w_ref, n_ref, i):
    nw = cmul((n_ref[0, i], n_ref[1, i]), (w_ref[0, i], w_ref[1, i]))
    return csub(nw, sums(w_ref, i))


def advance(w_ref, n_ref, v_ref, th, next_ref, ranges, p_ref=None, u_ref=None):
    def body(i):
        y = csub(image(w_ref, n_ref, i), cmul(th, (v_ref[0, i], v_ref[1, i])))
        for part in range(2):
            next_ref[part, i] = y[part]
        if p_ref is not None:
            u = cmul((p_ref[0, i], p_ref[1, i]), y)
            for part in range(2):
                u_ref[part, i] = u[part]

    loop(ranges, body)


def inside(planes, k):
    return [(H + k, planes - H - k)]


def outside(planes, k):
    return [(k, H + k), (planes - H - k, planes - k)]


def two_applications(part_of, planes, th, p_ref, n_ref, u_ref, v_ref, w_refs, next_refs):
    half_step(u_ref, p_ref, w_refs[0], part_of(planes, 1))
    advance(w_refs[0], n_ref, v_ref, th, next_refs[0], part_of(planes, 2), p_ref, u_ref)
    half_step(u_ref, p_ref, w_refs[1], part_of(planes, 3))
    advance(w_refs[1], n_ref, next_refs[0], th, next_refs[1], part_of(planes, 4))


def total_of(ref):
    rows = ref[...].reshape(ref.shape[0], ref.shape[-1])
    tot = jnp.sum(rows, axis=0, keepdims=True)
    lane = lax.broadcasted_iota(jnp.int32, tot.shape, 1)
    return lambda k: jnp.sum(jnp.where(lane == k, tot, 0.0), axis=1, keepdims=True)


def pack_lanes(values, first=0):
    lane = lax.broadcasted_iota(jnp.int32, (1, 128), 1)
    row = jnp.zeros((1, 128), F32)
    for k, v in enumerate(values, first):
        s = jnp.sum(jnp.sum(v, axis=0, keepdims=True), axis=1, keepdims=True)
        row = jnp.where(lane == k, s, row)
    return row


def fold(x):
    out = x[:, :128]
    for b in range(128, x.shape[1], 128):
        out = out + x[:, b : b + 128]
    return out


def pairs_of(rights):
    return [(left, right) for right in rights for left in range(right + 1)]


def gram_rows(fields, ct_ref, pairs, spans, first=0):
    ny = ct_ref.shape[1]
    used = sorted({k for pair in pairs for k in pair})
    count = sum(1 if left == right else 2 for left, right in pairs)

    def body(i, acc):
        acc = list(acc)
        for a in range(0, ny, 8):
            rows = pl.ds(a, 8)
            ct = ct_ref[i, rows]
            vs = {}
            for k in used:
                ref, base, scaled = fields[k]
                v = (ref[0, i + base, rows], ref[1, i + base, rows])
                vs[k] = (ct * v[0], ct * v[1]) if scaled else v
            k = 0
            for left, right in pairs:
                (lr, li), (rr, ri) = vs[left], vs[right]
                acc[k] = acc[k] + fold(lr * rr + li * ri)
                k += 1
                if right > left:
                    acc[k] = acc[k] + fold(lr * ri - li * rr)
                    k += 1
        return tuple(acc)

    acc = (jnp.zeros((8, 128), F32),) * count
    for lo, hi in spans:
        acc = lax.fori_loop(lo, hi, body, acc)
    return pack_lanes(acc, first)


def put(row, out_ref):
    for k in range(out_ref.shape[0]):
        out_ref[k] = row


def gram_entries(pick, pairs, entries):
    k = 0
    for left, right in pairs:
        if left == right:
            entries[left, right] = (pick(k), jnp.zeros((1, 1), F32))
            k += 1
        else:
            entries[left, right] = (pick(k), pick(k + 1))
            entries[right, left] = cconj(entries[left, right])
            k += 2
    return entries


def shift_from(ref):
    pick = total_of(ref)
    den = pick(2)
    safe = jnp.where(den > 0.0, den, 1.0)
    return tuple(jnp.where(den > 0.0, pick(k) / safe, FALLBACK[k]) for k in range(2))


EARLY = pairs_of((0, 1, 2))
LATE = pairs_of((3, 4))


def pack_pair(first, second, top):
    sub = lax.broadcasted_iota(jnp.int32, first.shape, 0)
    rolled = pltpu.roll(second, 4, 0)
    if top:
        return jnp.where(sub < 4, first, rolled)
    return jnp.where(sub < 4, rolled, first)


def unpack_pair(right, left):
    sub = lax.broadcasted_iota(jnp.int32, right.shape, 0)
    first = jnp.where(sub < 4, right, left)
    second = pltpu.roll(jnp.where(sub < 4, left, right), 4, 0)
    return first, second


def own_values(b_ref, cf_ref, ct_ref, mr_ref, d_ref):
    def get(i, rows):
        ct = ct_ref[i, rows]
        r = 1.0 / ct
        return (
            b_ref[0, i, rows] * r,
            b_ref[1, i, rows] * r,
            cf_ref[i, rows] * ct,
            mr_ref[i, rows],
            d_ref[i, rows],
        )

    return get


def fetch(pairs, sems):
    copies = [pltpu.make_async_copy(a, b, sems.at[k]) for k, (a, b) in enumerate(pairs)]
    for c in copies:
        c.start()
    return copies


def wait_for(copies):
    for c in copies:
        c.wait()


def edges_kernel(
    b_ref, cf_ref, ct_ref, mr_ref, d_ref, lo_ref, hi_ref, top_ref, bot_ref,
    blocks, coefs, row_blocks, row_coefs, sems,
):
    nx, ny, _ = cf_ref.shape
    pairs = []
    for side, at in enumerate((0, nx - H)):
        span = pl.ds(at, H)
        pairs.append((b_ref.at[:, span], blocks.at[side]))
        for k, ref in enumerate((cf_ref, ct_ref, mr_ref, d_ref)):
            pairs.append((ref.at[span], coefs.at[side, k]))
    for side, at in enumerate((0, ny - 8)):
        rows = pl.ds(at, 8)
        pairs.append((b_ref.at[:, :, rows], row_blocks.at[side]))
        for k, ref in enumerate((cf_ref, ct_ref, mr_ref, d_ref)):
            pairs.append((ref.at[:, rows], row_coefs.at[side, k]))
    copies = fetch(pairs, sems)
    wait_for(copies[:10])
    for side, out_ref in enumerate((lo_ref, hi_ref)):
        get = own_values(blocks.at[side], *(coefs.at[side, k] for k in range(4)))
        for i in range(H):
            for f, value in enumerate(get(i, pl.ds(0, ny))):
                out_ref[f, i] = value
    wait_for(copies[10:])
    for side, out_ref in enumerate((top_ref, bot_ref)):
        get = own_values(row_blocks.at[side], *(row_coefs.at[side, k] for k in range(4)))
        top = side == 0

        def body(j, carry):
            a, b = get(2 * j, pl.ds(0, 8)), get(2 * j + 1, pl.ds(0, 8))
            out_ref[2 * j] = pack_pair(a[0], a[1], top)
            out_ref[2 * j + 1] = pack_pair(b[0], b[1], top)
            for f in range(3):
                out_ref[nx + f * nx // 2 + j] = pack_pair(a[2 + f], b[2 + f], top)
            return carry

        lax.fori_loop(0, nx // 2, body, 0, unroll=2)


def corners_kernel(after_ref, yl_ref, yr_ref, lo_ref, hi_ref):
    count = yl_ref.shape[0]
    nx = count * 2 // 5
    for k, ref in enumerate((yl_ref, yr_ref)):
        for out_ref, base in ((lo_ref, 0), (hi_ref, nx - H)):
            for i in range(H):
                out_ref[k, i] = ref[base + i]
            for f in range(3):
                for j in range(H // 2):
                    at = nx + f * nx // 2 + base // 2 + j
                    out_ref[k, H + f * H // 2 + j] = ref[at]


def store_fields(refs, plane, rows, v, c, mr, d):
    p_ref, n_ref, u_ref, v_ref = refs
    p, n = coefficients(c, mr, d)
    u = cmul(p, v)
    for part in range(2):
        p_ref[part, plane, rows] = p[part]
        n_ref[part, plane, rows] = n[part]
        u_ref[part, plane, rows] = u[part]
        v_ref[part, plane, rows] = v[part]


def own_kernel(
    b_any, cf_any, ct_any, mr_any, d_any,
    p_ref, n_ref, u_ref, v_ref, out_ref, b_ref, cf_ref, ct_ref,
    mr_ref, d_ref, w_ref, sems,
):
    nx, ny, nz = cf_ref.shape
    sources = (b_any, cf_any, ct_any, mr_any, d_any)
    wait_for(fetch(list(zip(sources, (b_ref, cf_ref, ct_ref, mr_ref, d_ref))), sems))
    get = own_values(b_ref, cf_ref, ct_ref, mr_ref, d_ref)
    rows, rest = pl.ds(0, ny), pl.ds(ny, 8)
    zero = jnp.zeros((8, nz), F32)

    def body(i):
        vr, vi, c, mr, d = get(i, rows)
        store_fields((p_ref, n_ref, u_ref, v_ref), i + H, rows, (vr, vi), c, mr, d)
        for part in range(2):
            p_ref[part, i + H, rest] = zero
            u_ref[part, i + H, rest] = zero

    loop([(0, nx)], body)
    blank = jnp.zeros((ny + 8, nz), F32)
    for part in range(2):
        u_ref[part, H - 1] = blank
        w_ref[part, H - 1] = blank
        w_ref[part, nx // 2 + H] = blank
    half_step(u_ref, p_ref, w_ref, [(H, nx // 2 + H)])

    def dots(i, acc):
        acc = list(acc)
        y = image(w_ref, n_ref, i + H)
        for a in range(0, ny, 8):
            ct = ct_ref[i, pl.ds(a, 8)]
            yr, yi = y[0][a : a + 8] * ct, y[1][a : a + 8] * ct
            br, bi = b_ref[0, i, pl.ds(a, 8)], b_ref[1, i, pl.ds(a, 8)]
            acc[0] = acc[0] + fold(br * yr + bi * yi)
            acc[1] = acc[1] + fold(br * yi - bi * yr)
            acc[2] = acc[2] + fold(br * br + bi * bi)
        return tuple(acc)

    acc = lax.fori_loop(0, nx // 2, dots, (jnp.zeros((8, 128), F32),) * 3, unroll=2)
    put(pack_lanes(acc), out_ref)


def tails(refs, left, right, ny, fields, coefs, planes):
    rows = pl.ds(ny, 8)
    v = [unpack_pair(right(k), left(k)) for k in fields]
    c = [unpack_pair(right(k), left(k)) for k in coefs]
    for k in range(2):
        store_fields(refs, planes[k], rows, v[k], c[0][k], c[1][k], c[2][k])


def sides_kernel(th_ref, xl_ref, xr_ref, yl_ref, yr_ref, *refs):
    p_ref, n_ref, u_ref, v_ref, w0_ref, w1_ref, v1_ref, v2_ref = refs[4:]
    state = (p_ref, n_ref, u_ref, v_ref)
    ny = xl_ref.shape[2]
    planes = p_ref.shape[1]
    nx = planes - 2 * H
    rows = pl.ds(0, ny)
    for ref, base in ((xl_ref, 0), (xr_ref, nx + H)):

        def side(i):
            vr, vi, c, mr, d = (ref[f, i] for f in range(5))
            store_fields(state, base + i, rows, (vr, vi), c, mr, d)

        loop([(0, H)], side)

    def pair(j):
        coefs = [nx + f * nx // 2 + j for f in range(3)]
        at = (H + 2 * j, H + 2 * j + 1)
        own = (2 * j, 2 * j + 1)
        tails(state, lambda k: yl_ref[k], lambda k: yr_ref[k], ny, own, coefs, at)

    loop([(0, nx // 2)], pair)
    th = shift_from(th_ref)
    two_applications(inside, planes, th, *state, (w0_ref, w1_ref), (v1_ref, v2_ref))


def first_kernel(th_ref, cl_ref, cr_ref, *refs):
    p_ref, n_ref, u_ref, v_ref, w0_ref, w1_ref, v1_ref, v2_ref, top_ref, bot_ref = refs[8:]
    state = (p_ref, n_ref, u_ref, v_ref)
    planes = p_ref.shape[1]
    nx, ny = planes - 2 * H, p_ref.shape[2] - 8
    for ref, base in ((cl_ref, 0), (cr_ref, nx + H)):
        for j in range(H // 2):
            coefs = [H + f * H // 2 + j for f in range(3)]
            at = (base + 2 * j, base + 2 * j + 1)
            own = (2 * j, 2 * j + 1)
            tails(state, lambda k: ref[0, k], lambda k: ref[1, k], ny, own, coefs, at)
    th = shift_from(th_ref)
    two_applications(outside, planes, th, *state, (w0_ref, w1_ref), (v1_ref, v2_ref))
    for out_ref, rows, top in ((top_ref, pl.ds(0, 8), True), (bot_ref, pl.ds(ny - 8, 8), False)):

        def pack(i):
            a, b = v2_ref[0, i + H, rows], v2_ref[1, i + H, rows]
            out_ref[i] = pack_pair(a, b, top)

        loop([(0, nx)], pack)


def early_kernel(b_ref, ct_ref, v1_ref, v2_ref, out_ref):
    fields = ((b_ref, 0, False), (v1_ref, H, True), (v2_ref, H, True))
    put(gram_rows(fields, ct_ref, EARLY, [(0, ct_ref.shape[0])]), out_ref)


def rows_back_kernel(yl_ref, yr_ref, _, v_ref, lo_ref, hi_ref):
    nx, ny = yl_ref.shape[0], v_ref.shape[2] - 8
    rows = pl.ds(ny, 8)

    def tail(i):
        for part, value in enumerate(unpack_pair(yr_ref[i], yl_ref[i])):
            v_ref[part, i + H, rows] = value

    loop([(0, nx)], tail)
    for part in range(2):
        for i in range(H):
            lo_ref[part, i] = v_ref[part, H + i]
            hi_ref[part, i] = v_ref[part, nx + i]


def late_fields(b_ref, *refs):
    return ((b_ref, 0, False),) + tuple((ref, H, True) for ref in refs)


def inner_kernel(
    th_ref, e_ref, p_ref, n_ref, b_ref, ct_ref, v1_ref, v_ref,
    u_ref, w2_ref, w3_ref, v3_ref, v4_ref, out_ref,
):
    planes = p_ref.shape[1]
    th = shift_from(th_ref)

    def fill(i):
        u = cmul((p_ref[0, i], p_ref[1, i]), (v_ref[0, i], v_ref[1, i]))
        for part in range(2):
            u_ref[part, i] = u[part]

    loop([(H, planes - H)], fill)
    two_applications(
        inside, planes, th, p_ref, n_ref, u_ref, v_ref, (w2_ref, w3_ref), (v3_ref, v4_ref)
    )
    fields = late_fields(b_ref, v1_ref, v_ref, v3_ref, v4_ref)
    put(e_ref[0] + gram_rows(fields, ct_ref, LATE, [(H, planes - 3 * H)], 9), out_ref)


def second_kernel(th_ref, e_ref, xl_ref, xr_ref, p_ref, n_ref, b_ref, ct_ref, v1_ref, *refs):
    v2_ref, u_ref, w2_ref, w3_ref, v3_ref, v4_ref, out_ref = refs[6:]
    planes = p_ref.shape[1]
    th = shift_from(th_ref)
    for ref, base in ((xl_ref, 0), (xr_ref, planes - H)):
        for i in range(H):
            v = (ref[0, i], ref[1, i])
            u = cmul((p_ref[0, base + i], p_ref[1, base + i]), v)
            for part in range(2):
                v2_ref[part, base + i] = v[part]
                u_ref[part, base + i] = u[part]
    two_applications(
        outside, planes, th, p_ref, n_ref, u_ref, v2_ref, (w2_ref, w3_ref), (v3_ref, v4_ref)
    )
    fields = late_fields(b_ref, v1_ref, v2_ref, v3_ref, v4_ref)
    nx = planes - 2 * H
    put(e_ref[0] + gram_rows(fields, ct_ref, LATE, [(0, H), (nx - H, nx)], 9), out_ref)


def recurrences(th, gram):
    def inner(x, y):
        total = None
        for i, xi in enumerate(x):
            part = None
            for j, yj in enumerate(y):
                t = cmul(gram[i, j], yj)
                part = t if part is None else cadd(part, t)
            t = cmul(cconj(xi), part)
            total = t if total is None else cadd(total, t)
        return total

    def apply(x):
        scaled = [cmul(th, c) for c in x]
        return [scaled[0]] + [cadd(x[k], scaled[k + 1]) for k in range(len(x) - 1)] + [x[-1]]

    def lincomb(x, s, y):
        out = []
        for k in range(max(len(x), len(y))):
            a = x[k] if k < len(x) else None
            b = cmul(s, y[k]) if k < len(y) else None
            out.append(b if a is None else a if b is None else cadd(a, b))
        return out

    def neg(s):
        return (-s[0], -s[1])

    one = (jnp.ones((1, 1), F32), jnp.zeros((1, 1), F32))
    residual, direction, shadow, answer = [one], [one], [one], []
    rho = inner(shadow, residual)
    for step in range(2):
        image = apply(direction)
        alpha = cdiv(rho, inner(shadow, image))
        half = lincomb(residual, neg(alpha), image)
        second = apply(half)
        prod = inner(second, half)
        norm = inner(second, second)[0] + EPSILON
        omega = (prod[0] / norm, prod[1] / norm)
        answer = lincomb(lincomb(answer, alpha, direction), omega, half)
        residual = lincomb(half, neg(omega), second)
        if step == 0:
            rho_next = inner(shadow, residual)
            beta = cmul(cdiv(rho_next, rho), cdiv(alpha, omega))
            direction = lincomb(residual, beta, lincomb(direction, neg(omega), image))
            rho = rho_next
    return answer, residual


def final_kernel(
    th_ref, g_ref, b_ref, cf_ref, ct_ref,
    w0_ref, w1_ref, w2_ref, w3_ref, v1_ref, v2_ref, v3_ref, v4_ref,
    sol_any, res_any,
    sol_ref, res_ref, sems,
):
    nx, ny, nz = cf_ref.shape
    th = shift_from(th_ref)
    entries = gram_entries(total_of(g_ref), EARLY + LATE, {})
    answer, residual = recurrences(th, entries)

    def spread(c):
        return tuple(jnp.broadcast_to(x, (8, nz)) for x in c)

    answer, residual = [spread(c) for c in answer], [spread(c) for c in residual]

    def body(i, carry):
        for a in range(0, ny, 8):
            rows = pl.ds(a, 8)
            acc = None
            for c, ref in zip(answer, (w0_ref, w1_ref, w2_ref, w3_ref)):
                t = cmul(c, (ref[0, i + H, rows], ref[1, i + H, rows]))
                acc = t if acc is None else cadd(acc, t)
            inv = SCALE / cf_ref[i, rows]
            sol_ref[0, i, rows] = acc[0] * inv
            sol_ref[1, i, rows] = acc[1] * inv
            acc = None
            for c, ref in zip(residual[1:], (v1_ref, v2_ref, v3_ref, v4_ref)):
                t = cmul(c, (ref[0, i + H, rows], ref[1, i + H, rows]))
                acc = t if acc is None else cadd(acc, t)
            ct = ct_ref[i, rows]
            t = cmul(residual[0], (b_ref[0, i, rows], b_ref[1, i, rows]))
            res_ref[0, i, rows] = acc[0] * ct + t[0]
            res_ref[1, i, rows] = acc[1] * ct + t[1]
        return carry

    copies = []
    for k in range(CHUNKS):
        lo, hi = k * nx // CHUNKS, (k + 1) * nx // CHUNKS
        lax.fori_loop(lo, hi, body, 0, unroll=2)
        span = pl.ds(lo, hi - lo)
        for a, b in ((sol_ref, sol_any), (res_ref, res_any)):
            copies.append(
                pltpu.make_async_copy(a.at[:, span], b.at[:, span], sems.at[len(copies)])
            )
            copies[-1].start()
    for copy in copies:
        copy.wait()


def call(kernel, outs, scratch, *args, alias=None):
    return pl.pallas_call(
        kernel,
        out_shape=[jax.ShapeDtypeStruct(s, F32) for s in outs],
        in_specs=vmem(len(args)),
        out_specs=vmem(len(outs)),
        scratch_shapes=[pltpu.VMEM(s, F32) for s in scratch],
        input_output_aliases=alias or {},
        compiler_params=pltpu.CompilerParams(vmem_limit_bytes=LIMIT),
    )(*args)


def edge_call(kernel, outs, scratch, *args):
    return pl.pallas_call(
        kernel,
        out_shape=[jax.ShapeDtypeStruct(s, F32) for s in outs],
        in_specs=[pl.BlockSpec(memory_space=pl.ANY)] * len(args),
        out_specs=vmem(len(outs)),
        scratch_shapes=[pltpu.VMEM(s, F32) for s in scratch] + [pltpu.SemaphoreType.DMA((20,))],
        compiler_params=pltpu.CompilerParams(vmem_limit_bytes=LIMIT),
    )(*(pltpu.with_memory_space_constraint(x, pltpu.HBM) for x in args))


def both_ways(to_lower, to_upper, axis):
    n = lax.axis_size(axis)
    up = [(i, i + 1) for i in range(n - 1)]
    down = [(i + 1, i) for i in range(n - 1)]
    return lax.ppermute(to_upper, axis, up), lax.ppermute(to_lower, axis, down)


def local(b, cf, ct, mr, d):
    nx, ny, nz = cf.shape
    peers = lax.axis_size("gx") * lax.axis_size("gy")
    planes = nx + 2 * H
    own = (2, nx, ny, nz)
    ext = (2, planes, ny + 2 * H, nz)
    face = (2, H, ny + 2 * H, nz)
    rim = (nx + 3 * nx // 2, 8, nz)
    corner = (2, H + 3 * H // 2, 8, nz)
    inputs = (b, cf, ct, mr, d)

    lo, hi, top, bot = edge_call(
        edges_kernel, [(5, H, ny, nz)] * 2 + [rim, rim],
        [(2, 2, H, ny, nz), (2, 4, H, ny, nz), (2, 2, nx, 8, nz), (2, 4, nx, 8, nz)], *inputs
    )
    yl, yr = both_ways(top, bot, "gy")
    xl, xr = both_ways(lo, hi, "gx")
    *state, th, b, cf, ct = edge_call(
        own_kernel, [ext] * 4 + [(peers, 1, 128), b.shape, cf.shape, ct.shape],
        [mr.shape, d.shape, ext], *inputs,
    )
    th = lax.all_to_all(th, AXES, 0, 0)
    lo, hi = call(corners_kernel, [corner] * 2, [], th, yl, yr)
    cl, cr = both_ways(lo, hi, "gx")
    state = call(
        sides_kernel, [ext] * 8, [], th, xl, xr, yl, yr, *state,
        alias={5 + k: k for k in range(4)},
    )
    p, n, _, _, w0, w1, v1, v2, top, bot = call(
        first_kernel, [ext] * 8 + [(nx, 8, nz)] * 2, [], th, cl, cr, *state,
        alias={3 + k: k for k in range(8)},
    )
    yl, yr = both_ways(top, bot, "gy")
    early = call(early_kernel, [(1, 1, 128)], [], b, ct, v1, v2)[0]
    v2, lo, hi = call(rows_back_kernel, [ext, face, face], [], yl, yr, v2, alias={2: 0})
    xl, xr = both_ways(lo, hi, "gx")
    *state, early = call(
        inner_kernel, [ext] * 5 + [(1, 1, 128)], [], th, early, p, n, b, ct, v1, v2
    )
    v2, _, w2, w3, v3, v4, gram = call(
        second_kernel, [ext] * 6 + [(peers, 1, 128)], [],
        th, early, xl, xr, p, n, b, ct, v1, v2, *state,
        alias={9 + k: k for k in range(6)},
    )
    gram = lax.all_to_all(gram, AXES, 0, 0)
    args = (th, gram, b, cf, ct, w0, w1, w2, w3, v1, v2, v3, v4)
    return tuple(
        pl.pallas_call(
            final_kernel,
            out_shape=[jax.ShapeDtypeStruct(own, F32)] * 2,
            in_specs=vmem(len(args)),
            out_specs=[pl.BlockSpec(memory_space=pl.ANY)] * 2,
            scratch_shapes=[pltpu.VMEM(own, F32)] * 2 + [pltpu.SemaphoreType.DMA((2 * CHUNKS,))],
            compiler_params=pltpu.CompilerParams(vmem_limit_bytes=LIMIT),
        )(*args)
    )


def solution(mesh):
    field, coef = P(None, "gx", "gy", None), P("gx", "gy", None)
    return jax.shard_map(
        local,
        mesh=mesh,
        in_specs=(field, coef, coef, coef, coef),
        out_specs=(field, field),
        check_vma=False,
    )
```
